32 devices in a mesh: dp: 8 (over y, x, core), mp: 4 (over z).
Axes of the slice: x: 2, y: 2, z: 4, core: 2. Of those that a mesh axis runs over, the one named last changes fastest.
Arguments:
- word_features: bfloat16 [10240, 768], P('dp'), may hold values from -6 to 6
- sentence_numbering: int32 [256, 40], P('dp'), may hold values from 0 to 1, as said below
- region_features: bfloat16 [256, 145, 1024], P('dp'), may hold values from -6 to 6
- picture_global_feature: bfloat16 [256, 1024], P('dp'), may hold values from -6 to 6
- matched_picture: int32 [256, 2], P('dp'), may hold values from 0 to 255
- sharpness_array: float32 [1], replicated, may hold values from 0.02 to 0.04
- incoming_adjoint: bfloat16 [10240, 768], P('dp'), may hold values from -6 to 6
- intra_asking_map: bfloat16 [768, 768], P(None, 'mp'), may hold values from -0.21875 to 0.21875
- intra_lookup_map: bfloat16 [768, 768], P(None, 'mp'), may hold values from -0.21875 to 0.21875
- intra_content_map: bfloat16 [768, 768], P(None, 'mp'), may hold values from -0.21875 to 0.21875
- intra_attend_exit_map: bfloat16 [768, 768], P('mp'), may hold values from -0.4375 to 0.4375
- visual_asking_map: bfloat16 [768, 768], P(None, 'mp'), may hold values from -0.21875 to 0.21875
- visual_lookup_map: bfloat16 [1024, 768], P(None, 'mp'), may hold values from -0.1875 to 0.1875
- visual_content_map: bfloat16 [1024, 768], P(None, 'mp'), may hold values from -0.1875 to 0.1875
- visual_attend_exit_map: bfloat16 [768, 768], P('mp'), may hold values from -0.75 to 0.75
- mlp_widening_factor: bfloat16 [768, 3072], P(None, 'mp'), may hold values from -0.21875 to 0.21875
- mlp_narrowing_factor: bfloat16 [3072, 768], P('mp'), may hold values from -0.109375 to 0.109375
- initial_standardize_scale: float32 [768], replicated, may hold values from 0.5 to 1.5
- initial_standardize_offset: float32 [768], replicated, may hold values from -3 to 3
- middle_standardize_scale: float32 [768], replicated, may hold values from 0.5 to 1.5
- middle_standardize_offset: float32 [768], replicated, may hold values from -3 to 3
- final_standardize_scale: float32 [768], replicated, may hold values from 0.5 to 1.5
- final_standardize_offset: float32 [768], replicated, may hold values from -3 to 3
- sentence_mapping_factor: bfloat16 [768, 256], replicated, may hold values from -0.21875 to 0.21875
- picture_mapping_factor: bfloat16 [1024, 256], replicated, may hold values from -0.1875 to 0.1875
Outputs:
- per_sentence_contrast_cost: float32 [256, 2], P('dp')
- block_exit_features: bfloat16 [10240, 768], P('dp')
- adjoint_word_features: float32 [10240, 768], P('dp')
- adjoint_region_features: bfloat16 [256, 145, 1024], P('dp')
- adjoint_picture_global: float32 [256, 1024], P('dp')
- grad_temperature: float32 [1], replicated
- grad_self_query: float32 [768, 768], P(None, 'mp')
- grad_self_key: float32 [768, 768], P(None, 'mp')
- grad_self_value: float32 [768, 768], P(None, 'mp')
- grad_self_out: float32 [768, 768], P('mp')
- grad_cross_query: float32 [768, 768], P(None, 'mp')
- grad_cross_key: float32 [1024, 768], P(None, 'mp')
- grad_cross_value: float32 [1024, 768], P(None, 'mp')
- grad_cross_out: float32 [768, 768], P('mp')
- grad_inner_up: float32 [768, 3072], P(None, 'mp')
- grad_inner_down: float32 [3072, 768], P('mp')
- grad_first_gain: float32 [768], replicated
- grad_first_shift: float32 [768], replicated
- grad_second_gain: float32 [768], replicated
- grad_second_shift: float32 [768], replicated
- grad_third_gain: float32 [768], replicated
- grad_third_shift: float32 [768], replicated
- grad_text_weight: float32 [768, 256], replicated
- grad_image_weight: float32 [1024, 256], replicated
The draws below stay inside these ranges and needn't reach their ends.
Inputs may be any that keep to these rules, and one draw needn't show every extreme that they name: `sentence_numbering`: each row holds two captions: segments is 0 on the first one and 1 on the second one, each caption at least one token long.
All inputs are finite; a program needn't handle non-finite values.
Results may differ from the reference program's by a relative error of at most 0.025.
Values may be sent and summed in bfloat16 or wider, within the bound.
A program may use at most 192 MiB of HBM per device.

```python
import math
import jax
import jax.numpy as jnp
from jax import lax

D = 768
HEADS = 12
HEAD = 64
FF = 3072
DV = 1024
EMB = 256
PATCH = 145
LEN = 40
ROWS = 256
TOKENS = 10240


def draw_sentence_numbering(key, part):
    key = jax.random.fold_in(key, 11)
    boundary = jax.random.randint(key, (ROWS, 1), 1, LEN)
    position = jnp.arange(LEN, dtype=jnp.int32)[None, :]
    return (position >= boundary).astype(jnp.int32)


def plant(drawn, own_key, least, high):
    shape = drawn.shape
    place = [jax.random.randint(jax.random.fold_in(own_key, axis), (), 0, shape[axis]) for axis in range(len(shape))]
    drawn = drawn.at[tuple(place)].set(least)
    longest = shape.index(max(shape))
    place[longest] = (place[longest] + 1) % shape[longest]
    return drawn.at[tuple(place)].set(high)


def level_of(rng, dims, shards, low, largest):
    level = 1.0
    for dim, shards_of in shards:
        steps = jax.random.uniform(jax.random.fold_in(jax.random.fold_in(rng, 6), dim), (shards_of,), jnp.float32, low / len(shards), largest / len(shards))
        level = level * jnp.repeat(jnp.exp(steps), dims[dim] // shards_of).reshape((-1,) + (1,) * (len(dims) - 1 - dim))
    return level


def normal_values(key, shape, deviation, most, cuts=(), kind=jnp.bfloat16):
    level = level_of(key, shape, cuts, -0.22, 0.18) if cuts else 1.0
    values = jax.random.normal(key, shape, jnp.float32) * deviation * level
    return jnp.minimum(jnp.maximum(values, -most), most).astype(kind)


def setup_inputs(seed: int = 0) -> dict:
    keys = jax.random.split(jax.random.key(seed), 26)
    word_features = normal_values(keys[0], (TOKENS, D), 1.0, 6.0, ((0, 8),))
    sentence_numbering = draw_sentence_numbering(jax.random.fold_in(keys[25], 71), 0)
    region_features = normal_values(keys[2], (ROWS, PATCH, DV), 1.0, 6.0, ((0, 8),))
    picture_global_feature = normal_values(keys[3], (ROWS, DV), 1.0, 6.0, ((0, 8),))
    matched_picture = plant(jax.random.randint(keys[4], (ROWS, 2), 0, ROWS), jax.random.fold_in(keys[4], 1), 0, ROWS - 1).astype(jnp.int32)
    sharpness_array = jnp.clip(jnp.exp(jax.random.uniform(keys[5], (1,), jnp.float32, math.log(0.02), math.log(0.04))), 0.02, 0.04)
    incoming_adjoint = normal_values(keys[6], (TOKENS, D), 1.0, 6.0, ((0, 8),))
    intra_asking_map = normal_values(keys[7], (D, D), D ** -0.5, 0.21875, ((1, 4),))
    intra_lookup_map = normal_values(keys[8], (D, D), D ** -0.5, 0.21875, ((1, 4),))
    intra_content_map = normal_values(keys[9], (D, D), D ** -0.5, 0.21875, ((1, 4),))
    intra_attend_exit_map = normal_values(keys[10], (D, D), (D // 4) ** -0.5, 0.4375, ((0, 4),))
    visual_asking_map = normal_values(keys[11], (D, D), D ** -0.5, 0.21875, ((1, 4),))
    visual_lookup_map = normal_values(keys[12], (DV, D), DV ** -0.5, 0.1875, ((1, 4),))
    visual_content_map = normal_values(keys[13], (DV, D), DV ** -0.5, 0.1875, ((1, 4),))
    visual_attend_exit_map = normal_values(keys[14], (D, D), (D // 12) ** -0.5, 0.75, ((0, 4),))
    mlp_widening_factor = normal_values(keys[15], (D, FF), D ** -0.5, 0.21875, ((1, 4),))
    mlp_narrowing_factor = normal_values(keys[16], (FF, D), FF ** -0.5, 0.109375, ((0, 4),))
    initial_standardize_scale = jnp.clip(1.0 + 0.1 * jax.random.normal(keys[17], (D,), jnp.float32), 0.5, 1.5)
    initial_standardize_offset = normal_values(keys[18], (D,), 0.5, 3.0, (), jnp.float32)
    middle_standardize_scale = jnp.clip(1.0 + 0.1 * jax.random.normal(keys[19], (D,), jnp.float32), 0.5, 1.5)
    middle_standardize_offset = normal_values(keys[20], (D,), 0.5, 3.0, (), jnp.float32)
    final_standardize_scale = jnp.clip(1.0 + 0.1 * jax.random.normal(keys[21], (D,), jnp.float32), 0.5, 1.5)
    final_standardize_offset = normal_values(keys[22], (D,), 0.5, 3.0, (), jnp.float32)
    sentence_mapping_factor = normal_values(keys[23], (D, EMB), D ** -0.5, 0.21875)
    picture_mapping_factor = normal_values(keys[24], (DV, EMB), DV ** -0.5, 0.1875)
    return dict(word_features=word_features, sentence_numbering=sentence_numbering, region_features=region_features, picture_global_feature=picture_global_feature, matched_picture=matched_picture, sharpness_array=sharpness_array, incoming_adjoint=incoming_adjoint, intra_asking_map=intra_asking_map, intra_lookup_map=intra_lookup_map, intra_content_map=intra_content_map, intra_attend_exit_map=intra_attend_exit_map, visual_asking_map=visual_asking_map, visual_lookup_map=visual_lookup_map, visual_content_map=visual_content_map, visual_attend_exit_map=visual_attend_exit_map, mlp_widening_factor=mlp_widening_factor, mlp_narrowing_factor=mlp_narrowing_factor, initial_standardize_scale=initial_standardize_scale, initial_standardize_offset=initial_standardize_offset, middle_standardize_scale=middle_standardize_scale, middle_standardize_offset=middle_standardize_offset, final_standardize_scale=final_standardize_scale, final_standardize_offset=final_standardize_offset, sentence_mapping_factor=sentence_mapping_factor, picture_mapping_factor=picture_mapping_factor)


@jax.custom_vjp
def low(v):
    return lax.optimization_barrier(v.astype(jnp.bfloat16)).astype(jnp.float32)

@jax.custom_vjp
def low_back(v):
    return v

def low_keep(v):
    return (low(v), None)

def low_pass(kept, grad):
    return (grad,)

def back_keep(v):
    return (v, None)

def back_low(kept, grad):
    return (low(grad),)
low.defvjp(low_keep, low_pass)
low_back.defvjp(back_keep, back_low)
LN_EPS = 1e-06
NORM_EPS = 1e-06
BIG_NEG = -1000000000.0
HIGH = lax.Precision.HIGHEST

def round_both(tensor):
    return low(low_back(tensor))

def matmul_high(left, right):
    return jnp.dot(left, right, precision=HIGH)

def layer_norm(inputs, norm_gain, norm_shift):
    center = inputs - lax.optimization_barrier(jnp.mean(inputs, axis=-1, keepdims=True))
    spread = lax.optimization_barrier(jnp.mean(center * center, axis=-1, keepdims=True))
    return center * lax.rsqrt(spread + LN_EPS) * norm_gain + norm_shift

def unit_rows(inputs):
    return inputs * lax.rsqrt(lax.optimization_barrier(jnp.sum(inputs * inputs, axis=-1, keepdims=True)) + NORM_EPS)

def attend(queries, key_heads, value_heads, mask_bias):
    scores = jnp.einsum('gqhd,gkhd->ghqk', queries, key_heads, precision=HIGH)
    scores = low_back(scores) * 0.125 + mask_bias
    weights = low(jax.nn.softmax(scores, axis=-1))
    return jnp.einsum('ghqk,gkhd->gqhd', weights, value_heads, precision=HIGH)

def cross_modal_layer(learnable_bundle, word_features, sentence_numbering, region_features):
    intra_asking_map, intra_lookup_map, intra_content_map, intra_attend_exit_map, visual_asking_map, visual_lookup_map, visual_content_map, visual_attend_exit_map, mlp_widening_factor, mlp_narrowing_factor, initial_standardize_scale, initial_standardize_offset, middle_standardize_scale, middle_standardize_offset, final_standardize_scale, final_standardize_offset = learnable_bundle
    groups = sentence_numbering.shape[0]

    def split_heads(tensor, how_many):
        return tensor.reshape(groups, how_many, HEADS, HEAD)
    same_doc = sentence_numbering[:, :, None] == sentence_numbering[:, None, :]
    self_bias = jnp.where(same_doc, 0.0, BIG_NEG).astype(jnp.float32)[:, None, :, :]
    queries = split_heads(round_both(matmul_high(word_features, intra_asking_map)), LEN)
    key_heads = split_heads(round_both(matmul_high(word_features, intra_lookup_map)), LEN)
    value_heads = split_heads(round_both(matmul_high(word_features, intra_content_map)), LEN)
    context = round_both(attend(queries, key_heads, value_heads, self_bias)).reshape(groups * LEN, D)
    attn_out = low_back(matmul_high(context, intra_attend_exit_map))
    hidden_one = layer_norm(word_features + attn_out, initial_standardize_scale, initial_standardize_offset)
    cross_q = split_heads(round_both(matmul_high(low(hidden_one), visual_asking_map)), LEN)
    flat_patches = region_features.reshape(groups * PATCH, DV)
    cross_k = split_heads(round_both(matmul_high(flat_patches, visual_lookup_map)), PATCH)
    cross_v = split_heads(round_both(matmul_high(flat_patches, visual_content_map)), PATCH)
    cross_ctx = round_both(attend(cross_q, cross_k, cross_v, 0.0)).reshape(groups * LEN, D)
    cross_add = low_back(matmul_high(cross_ctx, visual_attend_exit_map))
    hidden_two = layer_norm(hidden_one + cross_add, middle_standardize_scale, middle_standardize_offset)
    inner_pre = low_back(matmul_high(low(hidden_two), mlp_widening_factor))
    activated = low(jax.nn.gelu(inner_pre, approximate=False))
    inner_add = low_back(matmul_high(activated, mlp_narrowing_factor))
    return layer_norm(hidden_two + inner_add, final_standardize_scale, final_standardize_offset)

def finished_answer(word_features, region_features, picture_global_feature, sharpness_array, sentence_mapping_factor, picture_mapping_factor, learnable_bundle, sentence_numbering, matched_picture, incoming_adjoint):
    group = math.gcd(ROWS, 64)
    group_count = ROWS // group
    tok_groups = word_features.reshape(group_count, group * LEN, D)
    seg_groups = sentence_numbering.reshape(group_count, group, LEN)
    patch_groups = region_features.reshape(group_count, group, PATCH, DV)

    def one_group(inputs):
        return cross_modal_layer(learnable_bundle, inputs[0], inputs[1], inputs[2])
    block_exit_features = lax.map(jax.checkpoint(one_group), (tok_groups, seg_groups, patch_groups)).reshape(TOKENS, D)
    position = jnp.arange(LEN, dtype=jnp.int32)
    split_at = (LEN - lax.optimization_barrier(jnp.sum(sentence_numbering, axis=1))).astype(jnp.int32)
    starts = jnp.stack([jnp.zeros_like(split_at), split_at], axis=1)
    leader_mask = (position[None, None, :] == starts[:, :, None]).astype(jnp.float32)
    out_rows = block_exit_features.reshape(ROWS, LEN, D)
    leading = lax.optimization_barrier(jnp.sum(leader_mask[:, :, :, None] * out_rows[:, None, :, :], axis=2)).reshape(ROWS * 2, D)
    text_raw = low_back(matmul_high(low(leading), sentence_mapping_factor))
    text_unit = low(unit_rows(text_raw))
    image_raw = low_back(matmul_high(picture_global_feature, picture_mapping_factor))
    image_unit = low(unit_rows(image_raw))
    plain_affinity = low_back(jnp.dot(text_unit, image_unit.T, precision=HIGH))
    affinity_table = plain_affinity / sharpness_array[0]
    log_total = jax.nn.logsumexp(affinity_table, axis=1)
    columns = jnp.arange(ROWS, dtype=jnp.int32)
    target_hit = (columns[None, :] == matched_picture.reshape(-1)[:, None]).astype(jnp.float32)
    per_sentence_contrast_cost = log_total - lax.optimization_barrier(jnp.sum(target_hit * affinity_table, axis=1))
    total_value = jnp.sum(block_exit_features * incoming_adjoint) + jnp.sum(per_sentence_contrast_cost)
    return (total_value, (block_exit_features, per_sentence_contrast_cost.reshape(ROWS, 2)))

def reference(word_features, sentence_numbering, region_features, picture_global_feature, matched_picture, sharpness_array, incoming_adjoint, intra_asking_map, intra_lookup_map, intra_content_map, intra_attend_exit_map, visual_asking_map, visual_lookup_map, visual_content_map, visual_attend_exit_map, mlp_widening_factor, mlp_narrowing_factor, initial_standardize_scale, initial_standardize_offset, middle_standardize_scale, middle_standardize_offset, final_standardize_scale, final_standardize_offset, sentence_mapping_factor, picture_mapping_factor):
    learnable_bundle = tuple((weight.astype(jnp.float32) for weight in (intra_asking_map, intra_lookup_map, intra_content_map, intra_attend_exit_map, visual_asking_map, visual_lookup_map, visual_content_map, visual_attend_exit_map, mlp_widening_factor, mlp_narrowing_factor, initial_standardize_scale, initial_standardize_offset, middle_standardize_scale, middle_standardize_offset, final_standardize_scale, final_standardize_offset)))
    forward_arguments = (word_features.astype(jnp.float32), region_features.astype(jnp.float32), picture_global_feature.astype(jnp.float32), sharpness_array.astype(jnp.float32), sentence_mapping_factor.astype(jnp.float32), picture_mapping_factor.astype(jnp.float32), learnable_bundle)
    cot_float = incoming_adjoint.astype(jnp.float32)

    def closed(tok_in, patch_in, embed_in, temp_in, text_in, image_in, param_in):
        return finished_answer(tok_in, patch_in, embed_in, temp_in, text_in, image_in, param_in, sentence_numbering, matched_picture, cot_float)
    total_value, pull_back, outputs = jax.vjp(closed, *forward_arguments, has_aux=True)
    block_exit_features, per_sentence_contrast_cost = outputs
    derivative_bundle = pull_back(jnp.ones((), dtype=total_value.dtype))
    adjoint_word_features, adjoint_region_features, adjoint_picture_global, adjoint_sharpness_number, adjoint_sentence_features, adjoint_picture_features, adjoint_learnables = derivative_bundle
    adjoint_intra_asking, adjoint_intra_lookup, adjoint_intra_content, adjoint_intra_exit, adjoint_visual_asking, adjoint_visual_lookup, adjoint_visual_content, adjoint_visual_exit, adjoint_widening, adjoint_narrowing, adjoint_initial_scale, adjoint_initial_offset, adjoint_middle_scale, adjoint_middle_offset, adjoint_final_scale, adjoint_final_offset = adjoint_learnables
    return (per_sentence_contrast_cost, block_exit_features.astype(jnp.bfloat16), adjoint_word_features, adjoint_region_features.astype(jnp.bfloat16), adjoint_picture_global, adjoint_sharpness_number, adjoint_intra_asking, adjoint_intra_lookup, adjoint_intra_content, adjoint_intra_exit, adjoint_visual_asking, adjoint_visual_lookup, adjoint_visual_content, adjoint_visual_exit, adjoint_widening, adjoint_narrowing, adjoint_initial_scale, adjoint_initial_offset, adjoint_middle_scale, adjoint_middle_offset, adjoint_final_scale, adjoint_final_offset, adjoint_sentence_features, adjoint_picture_features)
```

```python
from functools import partial

import jax
import jax.numpy as jnp
from jax import lax
from jax.experimental import pallas as pl
from jax.experimental.pallas import tpu as pltpu
from jax.sharding import PartitionSpec as P

HEAD = 64
GROUP = 4 * HEAD
LN_EPS = 1e-06
NORM_EPS = 1e-06
BIG_NEG = -1000000000.0
F32 = jnp.float32
BF16 = jnp.bfloat16
VMEM_LIMIT = 60 * 2**20


def dot_nn(left, right):
    return lax.dot_general(left, right, (((1,), (0,)), ((), ())), preferred_element_type=F32)


def dot_nt(left, right):
    return lax.dot_general(left, right, (((1,), (1,)), ((), ())), preferred_element_type=F32)


def dot_tn(left, right):
    return lax.dot_general(left, right, (((0,), (0,)), ((), ())), preferred_element_type=F32)


def normalize(inputs):
    center = inputs - jnp.mean(inputs, axis=-1, keepdims=True)
    rstd = lax.rsqrt(jnp.mean(center * center, axis=-1, keepdims=True) + LN_EPS)
    return center * rstd, rstd


def norm_pull(grad, xhat, rstd, gain):
    scaled = grad * gain
    first = jnp.mean(scaled, axis=-1, keepdims=True)
    second = jnp.mean(scaled * xhat, axis=-1, keepdims=True)
    grad_in = rstd * (scaled - first - xhat * second)
    return grad_in, jnp.sum(grad * xhat, axis=0, keepdims=True), jnp.sum(grad, axis=0, keepdims=True)


def unit_pull(raw, grad):
    scale = lax.rsqrt(jnp.sum(raw * raw, axis=-1, keepdims=True) + NORM_EPS)
    inner = jnp.sum(grad * raw, axis=-1, keepdims=True)
    return scale * grad - raw * (scale * scale * scale * inner)


def spread_heads(tensor):
    count = tensor.shape[0]
    left = lax.broadcasted_iota(jnp.int32, (count, 2 * HEAD), 1) < HEAD
    low, high = tensor[:, : 2 * HEAD], tensor[:, 2 * HEAD :]
    zero = jnp.zeros_like(low)
    blank = jnp.zeros((2 * count, 2 * HEAD), tensor.dtype)
    near = jnp.concatenate([jnp.where(left, low, zero), jnp.where(left, zero, low), blank], axis=0)
    far = jnp.concatenate([blank, jnp.where(left, high, zero), jnp.where(left, zero, high)], axis=0)
    return jnp.concatenate([near, far], axis=1).astype(BF16)


def collect_heads(stacked, count):
    left = lax.broadcasted_iota(jnp.int32, (count, 2 * HEAD), 1) < HEAD
    low = jnp.where(left, stacked[:count, : 2 * HEAD], stacked[count : 2 * count, : 2 * HEAD])
    high = jnp.where(
        left, stacked[2 * count : 3 * count, 2 * HEAD :], stacked[3 * count :, 2 * HEAD :]
    )
    return jnp.concatenate([low, high], axis=1)


def attend_probs(query_blocks, keys, keep):
    scores = dot_nt(keys, query_blocks)
    scores = jnp.where(keep, scores, BIG_NEG)
    top = jnp.max(scores, axis=0, keepdims=True)
    shifted = jnp.exp(scores - top)
    total = jnp.sum(shifted, axis=0, keepdims=True)
    return shifted * (1.0 / total)


def attend_forward(query, keys, values, keep):
    probs = attend_probs(spread_heads(query), keys, keep).astype(BF16)
    return collect_heads(dot_tn(probs, values), query.shape[0])


def attend_backward(query, keys, values, keep, grad_context):
    query_blocks = spread_heads(query)
    grad_blocks = spread_heads(grad_context)
    probs = attend_probs(query_blocks, keys, keep)
    grad_probs = dot_nt(values, grad_blocks)
    inner = jnp.sum(grad_probs * probs, axis=0, keepdims=True)
    grad_scores = (probs * (grad_probs - inner)).astype(BF16)
    grad_values = dot_nn(probs.astype(BF16), grad_blocks)
    grad_keys = dot_nn(grad_scores, query_blocks)
    grad_query = collect_heads(dot_tn(grad_scores, keys), query.shape[0]) * 0.125
    return grad_query, grad_keys, grad_values


def row_keep(bound, length):
    key = lax.broadcasted_iota(jnp.int32, (length, 4 * length), 0)
    query = lax.broadcasted_iota(jnp.int32, (length, 4 * length), 1) % length
    return (key >= bound) == (query >= bound)


def own_part(tensor, which, width):
    out = tensor[:, :width]
    for index in range(1, tensor.shape[1] // width):
        out = jnp.where(which == index, tensor[:, index * width : (index + 1) * width], out)
    return out


def self_forward_kernel(
    length, bound_ref, tok_ref, wqkv_ref, wout_ref, gain_ref, shift_ref, wcq_ref,
    qkv_ref, ctx_ref, xhat_ref, rstd_ref, cq_ref,
):
    width = tok_ref.shape[1]
    rows = tok_ref.shape[0] // length
    step = pl.program_id(0)
    tok = tok_ref[...]
    for part in range(3):
        proj = dot_nt(tok, wqkv_ref[part * width : (part + 1) * width, :])
        if part == 0:
            proj = proj * 0.125
        qkv_ref[:, part * width : (part + 1) * width] = proj.astype(BF16)

    def pair(index, carry):
        span = pl.ds(pl.multiple_of(index * 2 * length, 16), 2 * length)
        keeps = [row_keep(bound_ref[step * rows + 2 * index + j], length) for j in range(2)]
        for group in range(width // GROUP):
            q, k, v = (
                qkv_ref[span, part * width + group * GROUP : part * width + (group + 1) * GROUP].astype(F32)
                for part in range(3)
            )
            out = []
            for j in range(2):
                at = slice(j * length, (j + 1) * length)
                out.append(attend_forward(q[at], k[at].astype(BF16), v[at].astype(BF16), keeps[j]))
            ctx_ref[span, group * GROUP : (group + 1) * GROUP] = jnp.concatenate(out, axis=0).astype(BF16)
        return carry

    lax.fori_loop(0, rows // 2, pair, 0)
    attn = dot_nn(ctx_ref[...], wout_ref[...])
    xhat, rstd = normalize(tok.astype(F32) + attn)
    xhat_ref[...] = xhat
    rstd_ref[...] = rstd
    hidden = (xhat * gain_ref[...] + shift_ref[...]).astype(BF16)
    cq_ref[...] = (dot_nt(hidden, wcq_ref[...]) * 0.125).astype(BF16)


def cross_forward_kernel(
    patch_count, length, region_ref, wkv_ref, cq_ref, xhat1_ref, gain1_ref, shift1_ref, wout_ref,
    kv_ref, ctx_ref, xhat_ref, rstd_ref, flat_ref,
):
    images = region_ref.shape[1]
    vision = region_ref.shape[2]
    width = cq_ref.shape[1]
    padded = kv_ref.shape[1]
    whole = patch_count // 8 * 8
    flat = region_ref[...].reshape(patch_count * images, vision)

    def chunk(index, carry):
        at = pl.ds(pl.multiple_of(index * GROUP, GROUP), GROUP)
        proj = dot_nt(flat, wkv_ref[at, :])
        row = lax.broadcasted_iota(jnp.int32, (padded - whole, 128), 0)
        for half in range(GROUP // 128):
            flat_ref[half] = proj[:, half * 128 : (half + 1) * 128]
        for half in range(GROUP // 128):
            lanes = pl.ds(pl.multiple_of(index * GROUP + half * 128, 128), 128)
            for image in range(images):
                main = flat_ref[half, pl.ds(image, whole, stride=images), :]
                kv_ref[image, 0:whole, lanes] = main.astype(BF16)
                last = flat_ref[half, pl.ds(whole * images + image, 1), :]
                kv_ref[image, whole:padded, lanes] = jnp.where(row == 0, last, 0.0).astype(BF16)
        return carry

    lax.fori_loop(0, 2 * width // GROUP, chunk, 0)
    keep = lax.broadcasted_iota(jnp.int32, (padded, 4 * length), 0) < patch_count

    def pair(index, carry):
        span = pl.ds(pl.multiple_of(index * 2 * length, 16), 2 * length)
        for group in range(width // GROUP):
            lanes = slice(group * GROUP, (group + 1) * GROUP)
            q = cq_ref[span, lanes].astype(F32)
            out = []
            for j in range(2):
                image = 2 * index + j
                keys = kv_ref[image, :, lanes]
                values = kv_ref[image, :, width + group * GROUP : width + (group + 1) * GROUP]
                out.append(attend_forward(q[j * length : (j + 1) * length], keys, values, keep))
            ctx_ref[span, lanes] = jnp.concatenate(out, axis=0).astype(BF16)
        return carry

    lax.fori_loop(0, images // 2, pair, 0)
    hidden1 = xhat1_ref[...] * gain1_ref[...] + shift1_ref[...]
    xhat, rstd = normalize(hidden1 + dot_nn(ctx_ref[...], wout_ref[...]))
    xhat_ref[...] = xhat
    rstd_ref[...] = rstd


def gelu_parts(inputs):
    cdf = 0.5 * (1.0 + lax.erf(inputs * 0.7071067811865476))
    density = jnp.exp(inputs * inputs * -0.5) * 0.3989422804014327
    return inputs * cdf, cdf + inputs * density


def feed_forward_kernel(
    length, bound_ref, which_ref, temp_ref, xhat2_ref, rstd2_ref, gain2_ref, shift2_ref, gain3_ref, shift3_ref,
    wup_ref, wdown_ref, adj_ref, target_ref, images_ref, wtext_ref,
    out_ref, loss_ref, pack_ref, dr2_ref, dup_ref, ddown_ref, dgain2_ref, dshift2_ref, dgain3_ref, dshift3_ref,
    dtext_ref, dtemp_ref,
    act_ref, slope_ref, final_ref, grad_ref, lead_ref, up_acc, down_acc, text_acc,
):
    step = pl.program_id(0)
    steps = pl.num_programs(0)
    tokens, width = xhat2_ref.shape
    hidden_units = wup_ref.shape[0]
    rows = tokens // length
    chunk = min(768, hidden_units)

    @pl.when(step == 0)
    def _():
        for ref in (dgain2_ref, dshift2_ref, dgain3_ref, dshift3_ref, dtemp_ref, up_acc, down_acc, text_acc):
            ref[...] = jnp.zeros_like(ref)

    xhat2 = xhat2_ref[...]
    hidden2 = xhat2 * gain2_ref[...] + shift2_ref[...]
    low = hidden2.astype(BF16)
    final_ref[...] = hidden2

    def forward(index, carry):
        at = pl.ds(pl.multiple_of(index * chunk, chunk), chunk)
        act, slope = gelu_parts(dot_nt(low, wup_ref[at, :]))
        act = act.astype(BF16)
        act_ref[:, at] = act
        slope_ref[:, at] = slope
        final_ref[...] += dot_nn(act, wdown_ref[at, :])
        return carry

    lax.fori_loop(0, hidden_units // chunk, forward, 0)
    xhat3, rstd3 = normalize(final_ref[...])
    final = xhat3 * gain3_ref[...] + shift3_ref[...]
    out_ref[...] = final.astype(BF16)
    final_ref[...] = final
    grad_ref[...] = adj_ref[...].astype(F32)

    for row in range(rows):
        lead_ref[pl.ds(2 * row, 1), :] = final_ref[pl.ds(row * length, 1), :]
        second = row * length + bound_ref[step * rows + row]
        lead_ref[pl.ds(2 * row + 1, 1), :] = final_ref[pl.ds(second, 1), :]
    lead = lead_ref[...].astype(BF16)
    raw = dot_nn(lead, wtext_ref[...])
    text = raw * lax.rsqrt(jnp.sum(raw * raw, axis=-1, keepdims=True) + NORM_EPS)
    text_low = text.astype(BF16)
    temp = temp_ref[0]
    logits = dot_nt(text_low, images_ref[...]) / temp
    top = jnp.max(logits, axis=1, keepdims=True)
    lse = top + jnp.log(jnp.sum(jnp.exp(logits - top), axis=1, keepdims=True))
    target = target_ref[...]
    hit = lax.broadcasted_iota(jnp.int32, logits.shape, 1) == target
    loss_ref[...] = lse - jnp.sum(jnp.where(hit, logits, 0.0), axis=1, keepdims=True)
    dlogits = jnp.exp(logits - lse) - hit.astype(F32)
    dtemp_ref[...] += -jnp.sum(jnp.sum(dlogits * logits, axis=1, keepdims=True), axis=0, keepdims=True) / temp
    embed = raw.shape[1]
    lane = lax.broadcasted_iota(jnp.int32, (2 * rows, 128), 1)
    pack_ref[:, :embed] = text_low.astype(F32)
    pack_ref[:, embed:] = jnp.where(lane == 0, lse, jnp.where(lane == 1, target.astype(F32), 0.0))
    dtext = dot_nn((dlogits / temp).astype(BF16), images_ref[...])
    draw = unit_pull(raw, dtext).astype(BF16)
    text_acc[...] += dot_tn(lead, draw)
    lead_ref[...] = dot_nt(draw, wtext_ref[...])
    for row in range(rows):
        first = pl.ds(row * length, 1)
        grad_ref[first, :] += lead_ref[pl.ds(2 * row, 1), :]
        second = pl.ds(row * length + bound_ref[step * rows + row], 1)
        grad_ref[second, :] += lead_ref[pl.ds(2 * row + 1, 1), :]

    dr3, dgain3, dshift3 = norm_pull(grad_ref[...], xhat3, rstd3, gain3_ref[...])
    dgain3_ref[...] += dgain3
    dshift3_ref[...] += dshift3
    grad_ref[...] = dr3
    dfinal = dr3.astype(BF16)
    own = hidden_units // 4
    own_at = pl.ds(pl.multiple_of(which_ref[0] * own, own), own)
    down_acc[...] += dot_tn(act_ref[:, own_at], dfinal)

    def backward(index, carry):
        at = pl.ds(pl.multiple_of(index * chunk, chunk), chunk)
        dact = dot_nt(dfinal, wdown_ref[at, :])
        dinner = (dact * slope_ref[:, at]).astype(BF16)
        act_ref[:, at] = dinner
        grad_ref[...] += dot_nn(dinner, wup_ref[at, :])
        return carry

    lax.fori_loop(0, hidden_units // chunk, backward, 0)
    up_acc[...] += dot_tn(low, act_ref[:, own_at])
    dr2, dgain2, dshift2 = norm_pull(grad_ref[...], xhat2, rstd2_ref[...], gain2_ref[...])
    dgain2_ref[...] += dgain2
    dshift2_ref[...] += dshift2
    dr2_ref[...] = dr2

    @pl.when(step == steps - 1)
    def _():
        dup_ref[...] = up_acc[...].astype(BF16)
        ddown_ref[...] = down_acc[...].astype(BF16)
        dtext_ref[...] = text_acc[...].astype(BF16)


def cross_backward_kernel(
    patch_count, length, which_ref, region_ref, kv_ref, cq_ref, ctx_ref, xhat1_ref, rstd1_ref, gain1_ref, shift1_ref,
    dr2_ref, wkv_ref, wout_ref, wcq_ref,
    dregion_ref, dr1_ref, dkv_ref, dcq_ref, dout_ref, dgain_ref, dshift_ref,
    dctx_ref, dq_ref, flat_ref, stage_ref, kv_acc, cq_acc, out_acc, sem,
):
    step = pl.program_id(0)
    steps = pl.num_programs(0)
    images = region_ref.shape[1]
    vision = region_ref.shape[2]
    width = cq_ref.shape[1]
    padded = kv_ref.shape[1]
    own = width // 4
    which = which_ref[0]

    @pl.when(step == 0)
    def _():
        for ref in (dgain_ref, dshift_ref, kv_acc, cq_acc, out_acc):
            ref[...] = jnp.zeros_like(ref)

    dr2 = dr2_ref[...]
    dx = dr2.astype(BF16)
    dctx_ref[...] = dot_nt(dx, wout_ref[...]).astype(BF16)
    out_acc[...] += dot_tn(own_part(ctx_ref[...].astype(F32), which, own).astype(BF16), dx)
    keep = lax.broadcasted_iota(jnp.int32, (padded, 4 * length), 0) < patch_count
    stored = flat_ref.shape[1] // images

    def pair(index, carry):
        span = pl.ds(pl.multiple_of(index * 2 * length, 16), 2 * length)
        for group in range(width // GROUP):
            lanes = slice(group * GROUP, (group + 1) * GROUP)
            value_lanes = slice(width + group * GROUP, width + (group + 1) * GROUP)
            q = cq_ref[span, lanes].astype(F32)
            d = dctx_ref[span, lanes].astype(F32)
            out = []
            for j in range(2):
                image = 2 * index + j
                at = slice(j * length, (j + 1) * length)
                dq, dk, dv = attend_backward(
                    q[at], kv_ref[image, :, lanes], kv_ref[image, :, value_lanes], keep, d[at]
                )
                out.append(dq)
                spot = pl.ds(image, stored, stride=images)
                for half in range(2):
                    near = slice(half * 128, half * 128 + 128)
                    flat_ref[(2 * group + half), spot, :] = dk[:stored, near]
                    flat_ref[(width // 128 + 2 * group + half), spot, :] = dv[:stored, near]
            dq_ref[span, lanes] = jnp.concatenate(out, axis=0).astype(BF16)
        return carry

    lax.fori_loop(0, images // 2, pair, 0)

    pieces = 5
    patches = patch_count // pieces
    tall = patches * images
    base = step * images

    def send(index):
        slot = index % 2
        return pltpu.make_async_copy(
            stage_ref.at[slot],
            dregion_ref.at[pl.ds(index * patches, patches), pl.ds(pl.multiple_of(base, 16), images), :],
            sem.at[slot],
        )

    for index in range(pieces):
        rows = slice(index * tall, (index + 1) * tall)
        low = jnp.concatenate([flat_ref[c, rows, :].astype(BF16) for c in range(2 * width // 128)], axis=1)
        grad = dot_nn(low, wkv_ref[...])
        if index >= 2:
            send(index - 2).wait()
        stage_ref[index % 2] = grad.astype(BF16).reshape(patches, images, vision)
        send(index).start()
        region = region_ref[index * patches : (index + 1) * patches].reshape(tall, vision)
        for part in range(2):
            mine = own_part(low[:, part * width : (part + 1) * width].astype(F32), which, own).astype(BF16)
            kv_acc[part * own : (part + 1) * own, :] += dot_tn(mine, region)
    send(pieces - 2).wait()
    send(pieces - 1).wait()

    xhat1 = xhat1_ref[...]
    hidden1 = (xhat1 * gain1_ref[...] + shift1_ref[...]).astype(BF16)
    dq = dq_ref[...]
    cq_acc[...] += dot_tn(own_part(dq.astype(F32), which, own).astype(BF16), hidden1)
    dh1 = dr2 + dot_nn(dq, wcq_ref[...])
    dr1, dgain, dshift = norm_pull(dh1, xhat1, rstd1_ref[...], gain1_ref[...])
    dr1_ref[...] = dr1
    dgain_ref[...] += dgain
    dshift_ref[...] += dshift

    @pl.when(step == steps - 1)
    def _():
        dkv_ref[...] = kv_acc[...].astype(BF16)
        dcq_ref[...] = cq_acc[...].astype(BF16)
        dout_ref[...] = out_acc[...].astype(BF16)


def self_backward_kernel(
    length, bound_ref, which_ref, tok_ref, qkv_ref, ctx_ref, dr1_ref, wqkv_ref, wout_ref,
    dtok_ref, dqkv_ref, dout_ref, dctx_ref, grads_ref, qkv_acc, out_acc,
):
    step = pl.program_id(0)
    steps = pl.num_programs(0)
    tokens, width = tok_ref.shape
    rows = tokens // length
    own = width // 4
    which = which_ref[0]

    @pl.when(step == 0)
    def _():
        for ref in (qkv_acc, out_acc):
            ref[...] = jnp.zeros_like(ref)

    dr1 = dr1_ref[...]
    da = dr1.astype(BF16)
    dctx_ref[...] = dot_nt(da, wout_ref[...]).astype(BF16)
    out_acc[...] += dot_tn(own_part(ctx_ref[...].astype(F32), which, own).astype(BF16), da)

    def pair(index, carry):
        span = pl.ds(pl.multiple_of(index * 2 * length, 16), 2 * length)
        keeps = [row_keep(bound_ref[step * rows + 2 * index + j], length) for j in range(2)]
        for group in range(width // GROUP):
            q, k, v = (
                qkv_ref[span, part * width + group * GROUP : part * width + (group + 1) * GROUP].astype(F32)
                for part in range(3)
            )
            d = dctx_ref[span, group * GROUP : (group + 1) * GROUP].astype(F32)
            outs = []
            for j in range(2):
                at = slice(j * length, (j + 1) * length)
                outs.append(attend_backward(q[at], k[at].astype(BF16), v[at].astype(BF16), keeps[j], d[at]))
            for part in range(3):
                both = jnp.concatenate([outs[0][part], outs[1][part]], axis=0).astype(BF16)
                grads_ref[span, part * width + group * GROUP : part * width + (group + 1) * GROUP] = both
        return carry

    lax.fori_loop(0, rows // 2, pair, 0)
    tok = tok_ref[...]
    dtok_ref[...] = dr1 + dot_nn(grads_ref[...], wqkv_ref[...])
    for part in range(3):
        mine = own_part(grads_ref[:, part * width : (part + 1) * width].astype(F32), which, own).astype(BF16)
        qkv_acc[part * own : (part + 1) * own, :] += dot_tn(mine, tok)

    @pl.when(step == steps - 1)
    def _():
        dqkv_ref[...] = qkv_acc[...].astype(BF16)
        dout_ref[...] = out_acc[...].astype(BF16)


def image_backward_kernel(
    first_ref, temp_ref, picture_ref, weight_ref, pack_ref, dpicture_ref, dweight_ref
):
    raw = dot_nn(picture_ref[...], weight_ref[...])
    own = (raw * lax.rsqrt(jnp.sum(raw * raw, axis=-1, keepdims=True) + NORM_EPS)).astype(BF16)
    embed = raw.shape[1]
    temp = temp_ref[0]
    text = pack_ref[:, :embed].astype(BF16)
    lse = pack_ref[:, embed : embed + 1]
    target = pack_ref[:, embed + 1 : embed + 2].astype(jnp.int32)
    logits = dot_nt(text, own) / temp
    hit = lax.broadcasted_iota(jnp.int32, logits.shape, 1) + first_ref[0] == target
    dlogits = jnp.exp(logits - lse) - hit.astype(F32)
    dimage = dot_tn((dlogits / temp).astype(BF16), text)
    draw = unit_pull(raw, dimage).astype(BF16)
    dpicture_ref[...] = dot_nt(draw, weight_ref[...])
    dweight_ref[...] = dot_tn(picture_ref[...], draw).astype(BF16)


def full(shape):
    return pl.BlockSpec(shape, lambda i: (0,) * len(shape), pipeline_mode=pl.Buffered(1))


def fixed(shape):
    return pl.BlockSpec(shape, lambda i: (0,) * len(shape))


def rows_of(count, width):
    return pl.BlockSpec((count, width), lambda i: (i, 0))


def rows_once(count, width):
    return pl.BlockSpec((count, width), lambda i: (i, 0), pipeline_mode=pl.Buffered(1))


SMEM = pl.BlockSpec(memory_space=pltpu.SMEM)


def shape_of(shape, kind):
    return jax.ShapeDtypeStruct(shape, kind)


def call(kernel, steps, ins, outs, args, scratch=(), flops=0, moved=0):
    specs, shapes = zip(*outs, strict=True)
    return pl.pallas_call(
        kernel,
        grid=(steps,),
        in_specs=list(ins),
        out_specs=list(specs),
        out_shape=list(shapes),
        scratch_shapes=list(scratch),
        compiler_params=pltpu.CompilerParams(
            vmem_limit_bytes=VMEM_LIMIT, dimension_semantics=("arbitrary",)
        ),
        cost_estimate=pl.CostEstimate(flops=flops, bytes_accessed=moved, transcendentals=0),
    )(*args)


def gather_weight(shard, pieces):
    index = lax.axis_index("dp")
    count = shard.shape[0] // pieces
    piece = lax.dynamic_slice_in_dim(shard, index * count, count, 0)
    return lax.all_gather(piece, ("mp", "dp"), axis=0, tiled=True)


def body(
    dp_size,
    word_features,
    sentence_numbering,
    region_features,
    picture_global_feature,
    matched_picture,
    sharpness_array,
    incoming_adjoint,
    intra_asking_map,
    intra_lookup_map,
    intra_content_map,
    intra_attend_exit_map,
    visual_asking_map,
    visual_lookup_map,
    visual_content_map,
    visual_attend_exit_map,
    mlp_widening_factor,
    mlp_narrowing_factor,
    initial_standardize_scale,
    initial_standardize_offset,
    middle_standardize_scale,
    middle_standardize_offset,
    final_standardize_scale,
    final_standardize_offset,
    sentence_mapping_factor,
    picture_mapping_factor,
):
    rows, length = sentence_numbering.shape
    tokens, width = word_features.shape
    patch_count, vision = region_features.shape[1:]
    padded = -(-patch_count // 16) * 16
    images = 16
    embed = sentence_mapping_factor.shape[1]
    hidden_units = mlp_widening_factor.shape[1] * 4
    own = width // 4
    which = lax.axis_index("mp").astype(jnp.int32).reshape(1)
    bound = (length - jnp.sum(sentence_numbering, axis=1)).astype(jnp.int32)
    target = matched_picture.reshape(-1, 1)
    gain1, shift1, gain2, shift2, gain3, shift3 = (
        v.reshape(1, width)
        for v in (
            initial_standardize_scale, initial_standardize_offset, middle_standardize_scale,
            middle_standardize_offset, final_standardize_scale, final_standardize_offset,
        )
    )

    def gather_all(shards):
        sizes = [s.shape[0] for s in shards]
        return [gather_weight(s, dp_size) for s in shards]

    wq, wk, wv, wo = gather_all(
        [intra_asking_map.T, intra_lookup_map.T, intra_content_map.T, intra_attend_exit_map]
    )
    wqkv = jnp.concatenate([wq, wk, wv], axis=0)
    wcq, wco = gather_all([visual_asking_map.T, visual_attend_exit_map])
    wkv = jnp.concatenate(gather_all([visual_lookup_map.T, visual_content_map.T]), axis=0)
    wup, wdown = gather_all([mlp_widening_factor.T, mlp_narrowing_factor])

    image_raw = dot_nn(picture_global_feature, picture_mapping_factor)
    image_scale = lax.rsqrt(jnp.sum(image_raw * image_raw, axis=-1, keepdims=True) + NORM_EPS)
    image_all = lax.all_gather((image_raw * image_scale).astype(BF16), "dp", axis=0, tiled=True)

    token_rows = 8
    block = token_rows * length
    steps = rows // token_rows
    vec = full((1, width))
    square = full((width, width))

    qkv, ctx1, xhat1, rstd1, cq = call(
        partial(self_forward_kernel, length),
        steps,
        [SMEM, rows_of(block, width), full((3 * width, width)), square, vec, vec, square],
        [
            (rows_of(block, 3 * width), shape_of((tokens, 3 * width), BF16)),
            (rows_of(block, width), shape_of((tokens, width), BF16)),
            (rows_of(block, width), shape_of((tokens, width), F32)),
            (rows_of(block, 1), shape_of((tokens, 1), F32)),
            (rows_of(block, width), shape_of((tokens, width), BF16)),
        ],
        (bound, word_features, wqkv, wo, gain1, shift1, wcq),
        flops=10 * tokens * width * width,
        moved=20 * tokens * width,
    )

    region = jnp.transpose(region_features, (1, 0, 2))
    block2 = images * length
    region_spec = pl.BlockSpec((patch_count, images, vision), lambda i: (0, i, 0))
    kv_spec = pl.BlockSpec((images, padded, 2 * width), lambda i: (i, 0, 0))
    kv, ctx2, xhat2, rstd2 = call(
        partial(cross_forward_kernel, patch_count, length),
        rows // images,
        [
            region_spec, full((2 * width, vision)), rows_of(block2, width), rows_of(block2, width), vec, vec,
            square,
        ],
        [
            (kv_spec, shape_of((rows, padded, 2 * width), BF16)),
            (rows_of(block2, width), shape_of((tokens, width), BF16)),
            (rows_of(block2, width), shape_of((tokens, width), F32)),
            (rows_of(block2, 1), shape_of((tokens, 1), F32)),
        ],
        (region, wkv, cq, xhat1, gain1, shift1, wco),
        scratch=[pltpu.VMEM((GROUP // 128, patch_count * images, 128), F32)],
        flops=4 * rows * patch_count * width * vision,
        moved=2 * rows * padded * (vision + 2 * width),
    )

    captions = 2 * token_rows
    ff_own = hidden_units // 4
    (
        block_exit, loss, pack, dr2, dup, ddown, dgain2, dshift2, dgain3, dshift3, dtext, dtemp,
    ) = call(
        partial(feed_forward_kernel, length),
        steps,
        [
            SMEM, SMEM, SMEM, rows_of(block, width), rows_of(block, 1), vec, vec, vec, vec,
            full((hidden_units, width)), full((hidden_units, width)), rows_of(block, width), rows_of(captions, 1),
            full(image_all.shape), full((width, embed)),
        ],
        [
            (rows_of(block, width), shape_of((tokens, width), BF16)),
            (rows_of(captions, 1), shape_of((2 * rows, 1), F32)),
            (rows_of(captions, embed + 128), shape_of((2 * rows, embed + 128), F32)),
            (rows_of(block, width), shape_of((tokens, width), F32)),
            (fixed((width, ff_own)), shape_of((width, ff_own), BF16)),
            (fixed((ff_own, width)), shape_of((ff_own, width), BF16)),
            (fixed((1, width)), shape_of((1, width), F32)),
            (fixed((1, width)), shape_of((1, width), F32)),
            (fixed((1, width)), shape_of((1, width), F32)),
            (fixed((1, width)), shape_of((1, width), F32)),
            (fixed((width, embed)), shape_of((width, embed), BF16)),
            (fixed((1, 1)), shape_of((1, 1), F32)),
        ],
        (
            bound, which, sharpness_array, xhat2, rstd2, gain2, shift2, gain3, shift3, wup, wdown, incoming_adjoint, target, image_all,
            sentence_mapping_factor,
        ),
        scratch=[
            pltpu.VMEM((block, hidden_units), BF16),
            pltpu.VMEM((block, hidden_units), F32),
            pltpu.VMEM((block, width), F32),
            pltpu.VMEM((block, width), F32),
            pltpu.VMEM((captions, width), F32),
            pltpu.VMEM((width, ff_own), F32),
            pltpu.VMEM((ff_own, width), F32),
            pltpu.VMEM((width, embed), F32),
        ],
        flops=10 * tokens * width * hidden_units,
        moved=20 * tokens * width,
    )

    pack_all = lax.all_gather(pack, "dp", axis=0, tiled=True)
    dp_sum = lambda grad: lax.psum(grad, "dp")
    dup, ddown, dtext = dp_sum((dup, ddown, dtext))

    first = (lax.axis_index("dp") * rows).astype(jnp.int32).reshape(1)
    dpicture, dimage = call(
        image_backward_kernel,
        1,
        [SMEM, SMEM, full(picture_global_feature.shape), full(picture_mapping_factor.shape), full(pack_all.shape)],
        [
            (fixed((rows, vision)), shape_of((rows, vision), F32)),
            (fixed((vision, embed)), shape_of((vision, embed), BF16)),
        ],
        (first, sharpness_array, picture_global_feature, picture_mapping_factor, pack_all),
    )

    dregion, dr1, dkv, dcq, dco, dgain1, dshift1 = call(
        partial(cross_backward_kernel, patch_count, length),
        rows // images,
        [
            SMEM,
            pl.BlockSpec((patch_count, images, vision), lambda i: (0, i, 0), pipeline_mode=pl.Buffered(1)),
            pl.BlockSpec((images, padded, 2 * width), lambda i: (i, 0, 0), pipeline_mode=pl.Buffered(1)),
            rows_of(block2, width), rows_of(block2, width), rows_once(block2, width), rows_of(block2, 1), vec, vec,
            rows_once(block2, width), full((2 * width, vision)), square, square,
        ],
        [
            (pl.BlockSpec(memory_space=pl.ANY), shape_of((patch_count, rows, vision), BF16)),
            (rows_of(block2, width), shape_of((tokens, width), F32)),
            (fixed((2 * own, vision)), shape_of((2 * own, vision), BF16)),
            (fixed((own, width)), shape_of((own, width), BF16)),
            (fixed((own, width)), shape_of((own, width), BF16)),
            (fixed((1, width)), shape_of((1, width), F32)),
            (fixed((1, width)), shape_of((1, width), F32)),
        ],
        (which, region, kv, cq, ctx2, xhat1, rstd1, gain1, shift1, dr2, wkv, wco, wcq),
        scratch=[
            pltpu.VMEM((block2, width), BF16),
            pltpu.VMEM((block2, width), BF16),
            pltpu.VMEM((2 * width // 128, -(-patch_count // 8) * 8 * images, 128), F32),
            pltpu.VMEM((2, patch_count // 5, images, vision), BF16),
            pltpu.VMEM((2 * own, vision), F32),
            pltpu.VMEM((own, width), F32),
            pltpu.VMEM((own, width), F32),
            pltpu.SemaphoreType.DMA((2,)),
        ],
        flops=6 * rows * patch_count * width * vision,
        moved=2 * rows * padded * 2 * (vision + width),
    )
    dkv, dcq, dco, dimage = dp_sum((dkv, dcq, dco, dimage))

    dtok, dqkv, dso = call(
        partial(self_backward_kernel, length),
        steps,
        [
            SMEM, SMEM, rows_of(block, width), rows_of(block, 3 * width), rows_of(block, width), rows_of(block, width),
            full((3 * width, width)), square,
        ],
        [
            (rows_of(block, width), shape_of((tokens, width), F32)),
            (fixed((3 * own, width)), shape_of((3 * own, width), BF16)),
            (fixed((own, width)), shape_of((own, width), BF16)),
        ],
        (bound, which, word_features, qkv, ctx1, dr1, wqkv, wo),
        scratch=[
            pltpu.VMEM((block, width), BF16),
            pltpu.VMEM((block, 3 * width), BF16),
            pltpu.VMEM((3 * own, width), F32),
            pltpu.VMEM((own, width), F32),
        ],
        flops=10 * tokens * width * width,
        moved=20 * tokens * width,
    )
    dqkv, dso = dp_sum((dqkv, dso))
    small = jnp.concatenate(
        [dgain1, dshift1, dgain2, dshift2, dgain3, dshift3, jnp.broadcast_to(dtemp, (1, width))], axis=0
    )
    small = lax.psum(small, "dp")

    return (
        loss.reshape(rows, 2),
        block_exit,
        dtok,
        jnp.transpose(dregion, (1, 0, 2)),
        dpicture,
        small[6, :1],
        dqkv[:own].astype(F32).T,
        dqkv[own : 2 * own].astype(F32).T,
        dqkv[2 * own :].astype(F32).T,
        dso.astype(F32),
        dcq.astype(F32).T,
        dkv[:own].astype(F32).T,
        dkv[own:].astype(F32).T,
        dco.astype(F32),
        dup.astype(F32),
        ddown.astype(F32),
        small[0],
        small[1],
        small[2],
        small[3],
        small[4],
        small[5],
        dtext.astype(F32),
        dimage.astype(F32),
    )


def solution(mesh):
    rows = P("dp", None)
    by_column = P(None, "mp")
    by_row = P("mp", None)
    in_specs = (
        rows, rows, P("dp", None, None), rows, rows, P(), rows,
        by_column, by_column, by_column, by_row, by_column, by_column, by_column, by_row, by_column, by_row,
        P(), P(), P(), P(), P(), P(), P(), P(),
    )
    out_specs = (
        rows, rows, rows, P("dp", None, None), rows, P(),
        by_column, by_column, by_column, by_row, by_column, by_column, by_column, by_row, by_column, by_row,
        P(), P(), P(), P(), P(), P(), P(), P(),
    )
    return jax.shard_map(
        partial(body, mesh.shape["dp"]), mesh=mesh, in_specs=in_specs, out_specs=out_specs, check_vma=False
    )
```

```python
from functools import partial

import jax
import jax.numpy as jnp
from jax import lax
from jax.experimental import pallas as pl
from jax.experimental.pallas import tpu as pltpu
from jax.sharding import PartitionSpec as P

HEAD = 64
GROUP = 4 * HEAD
LN_EPS = 1e-06
NORM_EPS = 1e-06
BIG_NEG = -1000000000.0
F32 = jnp.float32
BF16 = jnp.bfloat16
VMEM_LIMIT = 60 * 2**20


def dot_nn(left, right):
    return lax.dot_general(left, right, (((1,), (0,)), ((), ())), preferred_element_type=F32)


def dot_nt(left, right):
    return lax.dot_general(left, right, (((1,), (1,)), ((), ())), preferred_element_type=F32)


def dot_tn(left, right):
    return lax.dot_general(left, right, (((0,), (0,)), ((), ())), preferred_element_type=F32)


def normalize(inputs):
    center = inputs - jnp.mean(inputs, axis=-1, keepdims=True)
    rstd = lax.rsqrt(jnp.mean(center * center, axis=-1, keepdims=True) + LN_EPS)
    return center * rstd, rstd


def norm_pull(grad, xhat, rstd, gain):
    scaled = grad * gain
    first = jnp.mean(scaled, axis=-1, keepdims=True)
    second = jnp.mean(scaled * xhat, axis=-1, keepdims=True)
    grad_in = rstd * (scaled - first - xhat * second)
    return grad_in, jnp.sum(grad * xhat, axis=0, keepdims=True), jnp.sum(grad, axis=0, keepdims=True)


def unit_pull(raw, grad):
    scale = lax.rsqrt(jnp.sum(raw * raw, axis=-1, keepdims=True) + NORM_EPS)
    inner = jnp.sum(grad * raw, axis=-1, keepdims=True)
    return scale * grad - raw * (scale * scale * scale * inner)


MESH = pl.DeviceIdType.MESH
DMA = pltpu.SemaphoreType.DMA


class Gather:
    def __init__(self, shards, outs, refs):
        count = len(outs)
        self.ins, self.outs, self.shards, sems = refs[:count], outs, shards, refs[count:]
        self.local, self.up, self.down, self.across, self.below, self.above, self.near, self.out, self.back = sems
        self.dp, self.z = lax.axis_index("dp"), lax.axis_index("mp")
        dp, z = self.dp, self.z
        self.core, self.x, self.y = dp % 2, dp // 2 % 2, dp // 4
        self.depth = outs[0].shape[1]
        self.color = (self.x + self.y) % 2
        east, north = 2 - 4 * self.x, 4 - 8 * self.y
        self.peers = [(dp + east, z), (dp + north, z), (dp + east + north, z)]
        self.twin = (dp + 1 - 2 * self.core, z)

    @staticmethod
    def semaphores(count, depth):
        grid = (count, depth)
        return [DMA((count,)), DMA(grid), DMA(grid), DMA((3, *grid)), DMA(grid), DMA(grid), DMA((3, *grid)), DMA(grid), DMA(grid)]

    def enter(self, everyone=0):
        barrier = pltpu.get_barrier_semaphore()
        peers = [*self.peers, self.twin]
        if everyone:
            peers = [((self.dp + k) % everyone, self.z) for k in range(1, everyone)]
        for peer in peers:
            pl.semaphore_signal(barrier, inc=1, device_id=peer, device_id_type=MESH)
        for step in (-1, 1):

            @pl.when(self.inside(self.z + step))
            def _(step=step):
                pl.semaphore_signal(barrier, inc=1, device_id=(self.dp, self.z + step), device_id_type=MESH)

        ends = (self.z > 0).astype(jnp.int32) + (self.z < self.depth - 1).astype(jnp.int32)
        pl.semaphore_wait(barrier, len(peers) + ends)

    def inside(self, z):
        return (z >= 0) & (z < self.depth)

    def part(self, index, source, first, size, core=None):
        mats = self.ins[index].shape[0] // 2
        core = self.core if core is None else core
        return self.outs[index].at[pl.ds(core * mats, mats), source, pl.ds(pl.multiple_of(first, 16), size), :]

    def copy(self, src, dst, send, recv, to):
        return pltpu.make_async_remote_copy(
            src_ref=src, dst_ref=dst, send_sem=send, recv_sem=recv, device_id=to, device_id_type=MESH
        )

    def span(self, index):
        tall = self.ins[index].shape[1]
        return self.color * (tall // 2) + self.y * (tall // 6), tall // 3

    def hop(self, index, source, step):
        spot = self.part(index, source, *self.span(index))
        send, recv = (self.up, self.below) if step > 0 else (self.down, self.above)
        return self.copy(spot, spot, send.at[index, source], recv.at[index, source], (self.dp, self.z + step))

    def first_hop(self, index, step):
        first, size = self.span(index)
        mats = self.ins[index].shape[0] // 2
        src = self.ins[index].at[pl.ds(self.core * mats, mats), pl.ds(pl.multiple_of(first, 16), size), :]
        send, recv = (self.up, self.below) if step > 0 else (self.down, self.above)
        spot = self.part(index, self.z, first, size)
        return self.copy(src, spot, send.at[index, self.z], recv.at[index, self.z], (self.dp, self.z + step))

    def side(self, index, source, which, inward=False):
        tall = self.ins[index].shape[1]
        color, y = self.color, self.y
        if inward:
            color, y = (1 - color, y) if which == 0 else (1 - color, 1 - y) if which == 1 else (color, 1 - y)
        pace, size = ((tall // 4, tall // 4), (tall // 4, tall // 4), (tall // 3, tall // 6))[which]
        spot = self.part(index, source, color * (tall // 2) + y * pace, size)
        sems = self.across.at[which, index, source], self.near.at[which, index, source]
        return self.copy(spot, spot, *sems, self.peers[which])

    def pass_on(self, index, source, inward=False):
        core = 1 - self.core if inward else self.core
        spot = self.part(index, source, 0, self.ins[index].shape[1], core)
        return self.copy(spot, spot, self.out.at[index, source], self.back.at[index, source], self.twin)

    def keep(self, index):
        return pltpu.make_async_copy(self.ins[index], self.outs[index].at[:, self.z], self.local.at[index])

    def start(self, everyone=0):
        count = 0
        for stack in self.ins:
            for index in range(stack.shape[0]):
                stack[index] = self.shards[count][...]
                count += 1
        self.enter(everyone)
        for index in range(len(self.ins)):
            for step in (1, -1):

                @pl.when(self.inside(self.z + step))
                def _(index=index, step=step):
                    self.first_hop(index, step).start()

            self.keep(index).start()

    def each(self, distance, what):
        for index in range(len(self.ins)):
            for step in (1, -1):
                source = self.z - step * distance

                @pl.when(self.inside(source))
                def _(index=index, step=step, source=source):
                    what(index, step, source)

    def pull(self, distance):
        def what(index, step, source):
            self.hop(index, source, step).wait_recv()

            @pl.when(self.inside(self.z + step))
            def _():
                self.hop(index, source, step).start()

            for which in range(3):
                self.side(index, source, which).start()

        self.each(distance, what)

    def pair(self, distance):
        def what(index, step, source):
            for which in range(3):
                self.side(index, source, which, inward=True).wait_recv()
            self.pass_on(index, source).start()

        self.each(distance, what)

    def finish(self):
        def what(index, step, source):
            self.pass_on(index, source, inward=True).wait_recv()
            self.pass_on(index, source).wait_send()
            for which in range(3):
                self.side(index, source, which).wait_send()

            @pl.when(self.inside(self.z + step))
            def _():
                self.hop(index, source, step).wait_send()

        for distance in range(1, self.depth):
            self.each(distance, what)
        for index in range(len(self.ins)):
            for step in (1, -1):

                @pl.when(self.inside(self.z + step))
                def _(index=index, step=step):
                    self.first_hop(index, step).wait_send()

            self.keep(index).wait()


class Reduce:
    def __init__(self, src, done, half, part, quarter, twin_sems, plane_sems):
        self.src, self.done, self.half, self.part, self.quarter = src, done, half, part, quarter
        self.twin_sems, self.plane_sems = twin_sems, plane_sems
        dp, z = lax.axis_index("dp"), lax.axis_index("mp")
        self.core, self.chip = dp % 2, dp // 2
        x, y = self.chip % 2, self.chip // 2
        east, north = 2 - 4 * x, 4 - 8 * y
        self.shifts = (east, north, east + north)
        self.peers = [(dp + shift, z) for shift in self.shifts]
        self.twin = (dp + 1 - 2 * self.core, z)
        self.tall = src.shape[0]

    @staticmethod
    def scratch(shape):
        rows, columns = shape
        sizes = ((rows, columns), (rows // 2, columns), (rows // 2, columns), (3, rows // 8, columns))
        return [*(pltpu.VMEM(size, BF16) for size in sizes), DMA((4,)), DMA((4, 3))]

    def enter(self):
        barrier = pltpu.get_barrier_semaphore()
        for peer in [*self.peers, self.twin]:
            pl.semaphore_signal(barrier, inc=1, device_id=peer, device_id_type=MESH)
        pl.semaphore_wait(barrier, 4)

    def copy(self, src, dst, send, recv, to):
        return pltpu.make_async_remote_copy(
            src_ref=src, dst_ref=dst, send_sem=send, recv_sem=recv, device_id=to, device_id_type=MESH
        )

    def mine(self, core):
        return pl.ds(pl.multiple_of(core * (self.tall // 2), 16), self.tall // 2)

    def slot(self, chip, core=None):
        first = chip * (self.tall // 8)
        if core is not None:
            first = first + core * (self.tall // 2)
        return pl.ds(pl.multiple_of(first, 16), self.tall // 8)

    def to_twin(self):
        sems = self.twin_sems.at[0], self.twin_sems.at[1]
        return self.copy(self.src.at[self.mine(1 - self.core)], self.half, *sems, self.twin)

    def scatter(self, which):
        chip = self.chip + self.shifts[which] // 2
        sems = self.plane_sems.at[0, which], self.plane_sems.at[1, which]
        return self.copy(self.part.at[self.slot(chip)], self.quarter.at[which], *sems, self.peers[which])

    def spread(self, which, chip):
        spot = self.done.at[self.slot(chip, self.core)]
        sems = self.plane_sems.at[2, which], self.plane_sems.at[3, which]
        return self.copy(spot, spot, *sems, self.peers[which])

    def back(self, core):
        spot = self.done.at[self.mine(core)]
        return self.copy(spot, spot, self.twin_sems.at[2], self.twin_sems.at[3], self.twin)

    def stage(self, number):
        if number == 1:
            self.to_twin().start()
        elif number == 2:
            self.to_twin().wait_recv()
            total = self.src[self.mine(self.core), :].astype(F32) + self.half[...].astype(F32)
            self.part[...] = total.astype(BF16)
            for which in range(3):
                self.scatter(which).start()
        elif number == 3:
            total = self.part[self.slot(self.chip), :].astype(F32)
            for which in range(3):
                self.scatter(which).wait_recv()
                total = total + self.quarter[which].astype(F32)
            self.done[self.slot(self.chip, self.core), :] = total.astype(BF16)
            for which in range(3):
                self.spread(which, self.chip).start()
        elif number == 4:
            for which in range(3):
                self.spread(which, self.chip + self.shifts[which] // 2).wait_recv()
            self.back(self.core).start()
        else:
            self.back(1 - self.core).wait_recv()
            self.to_twin().wait_send()
            for which in range(3):
                self.scatter(which).wait_send()
                self.spread(which, self.chip).wait_send()
            self.back(self.core).wait_send()


def spread_heads(tensor):
    count = tensor.shape[0]
    left = lax.broadcasted_iota(jnp.int32, (count, 2 * HEAD), 1) < HEAD
    low, high = tensor[:, : 2 * HEAD], tensor[:, 2 * HEAD :]
    zero = jnp.zeros_like(low)
    blank = jnp.zeros((2 * count, 2 * HEAD), tensor.dtype)
    near = jnp.concatenate([jnp.where(left, low, zero), jnp.where(left, zero, low), blank], axis=0)
    far = jnp.concatenate([blank, jnp.where(left, high, zero), jnp.where(left, zero, high)], axis=0)
    return jnp.concatenate([near, far], axis=1).astype(BF16)


def collect_heads(stacked, count):
    left = lax.broadcasted_iota(jnp.int32, (count, 2 * HEAD), 1) < HEAD
    low = jnp.where(left, stacked[:count, : 2 * HEAD], stacked[count : 2 * count, : 2 * HEAD])
    high = jnp.where(
        left, stacked[2 * count : 3 * count, 2 * HEAD :], stacked[3 * count :, 2 * HEAD :]
    )
    return jnp.concatenate([low, high], axis=1)


def attend_probs(query_blocks, keys, keep):
    scores = dot_nt(keys, query_blocks)
    scores = jnp.where(keep, scores, BIG_NEG)
    top = jnp.max(scores, axis=0, keepdims=True)
    shifted = jnp.exp(scores - top)
    total = jnp.sum(shifted, axis=0, keepdims=True)
    return shifted * (1.0 / total)


def attend_forward(query, keys, values, keep):
    probs = attend_probs(spread_heads(query), keys, keep).astype(BF16)
    return collect_heads(dot_tn(probs, values), query.shape[0])


def split_heads(tensor):
    left = lax.broadcasted_iota(jnp.int32, tensor.shape, 1) < HEAD
    zero = jnp.zeros_like(tensor)
    return jnp.concatenate([jnp.where(left, tensor, zero), jnp.where(left, zero, tensor)], axis=0).astype(BF16)


def attend_short(query, keys, values, keep):
    count = query.shape[0]
    left = lax.broadcasted_iota(jnp.int32, (count, 2 * HEAD), 1) < HEAD
    out = []
    for half in range(2):
        at = slice(half * 2 * HEAD, (half + 1) * 2 * HEAD)
        probs = attend_probs(split_heads(query[:, at]), keys[:, at], keep[:, : 2 * count])
        stacked = dot_nn(jnp.transpose(probs.astype(BF16)), values[:, at])
        out.append(jnp.where(left, stacked[:count], stacked[count:]))
    return jnp.concatenate(out, axis=1)


def attend_backward(query, keys, values, keep, grad_context):
    query_blocks = spread_heads(query)
    grad_blocks = spread_heads(grad_context)
    probs = attend_probs(query_blocks, keys, keep)
    grad_probs = dot_nt(values, grad_blocks)
    inner = jnp.sum(grad_probs * probs, axis=0, keepdims=True)
    grad_scores = (probs * (grad_probs - inner)).astype(BF16)
    grad_values = dot_nn(probs.astype(BF16), grad_blocks)
    grad_keys = dot_nn(grad_scores, query_blocks)
    grad_query = collect_heads(dot_tn(grad_scores, keys), query.shape[0]) * 0.125
    return grad_query, grad_keys, grad_values


def row_keep(bound, length):
    key = lax.broadcasted_iota(jnp.int32, (length, 4 * length), 0)
    query = lax.broadcasted_iota(jnp.int32, (length, 4 * length), 1) % length
    return (key >= bound) == (query >= bound)


def window(which, width):
    return pl.ds(pl.multiple_of(which * 3 // 2 * (width // 2), width // 2), width)


def own_rows(acc, which, own):
    odd = which % 2 == 1
    return jnp.where(odd, acc[acc.shape[0] - own :], acc[:own])


def prep_kernel(gathers, count, *refs):
    region_ref, picture_ref, weight_ref = refs[:3]
    shards, refs = refs[3 : 3 + count], refs[3 + count :]
    moved_ref, embed_ref = refs[:2]
    whole, refs = refs[2 : 2 + gathers], refs[2 + gathers :]
    flat_ref = refs[0]
    patch_count, images, lanes = region_ref.shape
    padded = moved_ref.shape[1]
    full_tiles = patch_count // 8 * 8
    step = pl.program_id(0)
    steps = pl.num_programs(0)
    gather = Gather(shards, whole, refs[1:]) if gathers else None

    @pl.when(step == 0)
    def _():
        if gather:
            gather.start()
        raw = dot_nn(picture_ref[...], weight_ref[...])
        scale = lax.rsqrt(jnp.sum(raw * raw, axis=-1, keepdims=True) + NORM_EPS)
        embed_ref[...] = (raw * scale).astype(BF16)

    flat_ref[...] = region_ref[...].reshape(patch_count * images, lanes).astype(F32)
    row = lax.broadcasted_iota(jnp.int32, (padded - full_tiles, lanes), 0)
    for image in range(images):
        main = flat_ref[pl.ds(image, full_tiles, stride=images), :]
        moved_ref[image, 0:full_tiles, :] = main.astype(BF16)
        last = flat_ref[pl.ds(full_tiles * images + image, 1), :]
        moved_ref[image, full_tiles:padded, :] = jnp.where(row == 0, last, 0.0).astype(BF16)

    if gather:

        for late, distance in ((6, 1), (4, 2), (2, 3)):

            @pl.when(step == steps - late)
            def _(distance=distance):
                gather.pull(distance)

        @pl.when(step == steps - 3)
        def _():
            gather.pair(1)

        @pl.when(step == steps - 1)
        def _():
            gather.pair(2)
            gather.pair(3)
            gather.finish()


def self_forward_kernel(length, gathers, count, *refs):
    bound_ref, tok_ref, wqkv_ref, wout_ref, embed_ref = refs[:5]
    shards, refs = refs[5 : 5 + count], refs[5 + count :]
    qkv_ref, ctx_ref, xhat_ref, rstd_ref = refs[:4]
    whole, refs = refs[4 : 4 + gathers], refs[4 + gathers :]
    width = tok_ref.shape[1]
    rows = tok_ref.shape[0] // length
    step = pl.program_id(0)
    steps = pl.num_programs(0)
    if gathers:
        images_ref, embed_local, embed_send, embed_recv = refs[:4]
        gather = Gather(shards, whole, refs[4:])
        dp, z = lax.axis_index("dp"), lax.axis_index("mp")
        dp_size = images_ref.shape[0] // embed_ref.shape[0]
        held = embed_ref.shape[0]

        def embed_copy(k, owner, to):
            spot = images_ref.at[pl.ds(pl.multiple_of(owner * held, 16), held), :]
            return pltpu.make_async_remote_copy(
                src_ref=embed_ref, dst_ref=spot, send_sem=embed_send.at[k], recv_sem=embed_recv.at[k],
                device_id=(to, z), device_id_type=MESH,
            )

        def embed_own():
            spot = images_ref.at[pl.ds(pl.multiple_of(dp * held, 16), held), :]
            return pltpu.make_async_copy(embed_ref, spot, embed_local)

        @pl.when(step == 0)
        def _():
            gather.start(everyone=dp_size)
            embed_own().start()
            for k in range(1, dp_size):
                embed_copy(k, dp, (dp + k) % dp_size).start()

        for distance in range(1, 4):

            @pl.when(step == distance)
            def _(distance=distance):
                gather.pull(distance)
                if distance > 1:
                    gather.pair(distance - 1)

    tok = tok_ref[...]
    for part in range(3):
        proj = dot_nt(tok, wqkv_ref[part * width : (part + 1) * width, :])
        if part == 0:
            proj = proj * 0.125
        qkv_ref[:, part * width : (part + 1) * width] = proj.astype(BF16)

    def pair(index, carry):
        span = pl.ds(pl.multiple_of(index * 2 * length, 16), 2 * length)
        keeps = [row_keep(bound_ref[step * rows + 2 * index + j], length) for j in range(2)]
        for group in range(width // GROUP):
            q, k, v = (
                qkv_ref[span, part * width + group * GROUP : part * width + (group + 1) * GROUP].astype(F32)
                for part in range(3)
            )
            out = []
            for j in range(2):
                at = slice(j * length, (j + 1) * length)
                out.append(attend_short(q[at], k[at].astype(BF16), v[at].astype(BF16), keeps[j]))
            ctx_ref[span, group * GROUP : (group + 1) * GROUP] = jnp.concatenate(out, axis=0).astype(BF16)
        return carry

    lax.fori_loop(0, rows // 2, pair, 0, unroll=2)
    attn = dot_nn(ctx_ref[...], wout_ref[...])
    xhat, rstd = normalize(tok.astype(F32) + attn)
    xhat_ref[...] = xhat
    rstd_ref[...] = rstd

    if gathers:

        @pl.when(step == steps - 1)
        def _():
            gather.pair(3)
            for k in range(1, dp_size):
                embed_copy(k, (dp + dp_size - k) % dp_size, (dp + k) % dp_size).wait_recv()
                embed_copy(k, dp, (dp + k) % dp_size).wait_send()
            embed_own().wait()
            gather.finish()


def cross_forward_kernel(patch_count, length, gathers, count, *refs):
    region_ref, wkv_ref, xhat1_ref, norm_ref, wcq_ref, wout_ref = refs[:6]
    shards, refs = refs[6 : 6 + count], refs[6 + count :]
    kv_ref, cq_ref, ctx_ref, xhat_ref, rstd_ref = refs[:5]
    whole, refs = refs[5 : 5 + gathers], refs[5 + gathers :]
    images, padded, vision = region_ref.shape
    width = cq_ref.shape[1]
    step = pl.program_id(0)
    steps = pl.num_programs(0)
    gather = Gather(shards, whole, refs) if gathers else None
    if gathers:

        @pl.when(step == 0)
        def _():
            gather.start()

        for distance in range(1, 4):

            @pl.when(step == distance)
            def _(distance=distance):
                gather.pull(distance)
                if distance > 1:
                    gather.pair(distance - 1)

    hidden1 = xhat1_ref[...] * norm_ref[0:1] + norm_ref[1:2]
    cq_ref[...] = (dot_nt(hidden1.astype(BF16), wcq_ref[...]) * 0.125).astype(BF16)
    flat = region_ref[...].reshape(images * padded, vision)

    def chunk(index, carry):
        at = pl.ds(pl.multiple_of(index * 512, 512), 512)
        proj = dot_nt(flat, wkv_ref[at, :])
        kv_ref[:, :, at] = proj.astype(BF16).reshape(images, padded, 512)
        return carry

    lax.fori_loop(0, 2 * width // 512, chunk, 0, unroll=True)
    keep = lax.broadcasted_iota(jnp.int32, (padded, 4 * length), 0) < patch_count

    def pair(index, carry):
        span = pl.ds(pl.multiple_of(index * 2 * length, 16), 2 * length)
        for group in range(width // GROUP):
            lanes = slice(group * GROUP, (group + 1) * GROUP)
            q = cq_ref[span, lanes].astype(F32)
            out = []
            for j in range(2):
                image = 2 * index + j
                keys = kv_ref[image, :, lanes]
                values = kv_ref[image, :, width + group * GROUP : width + (group + 1) * GROUP]
                out.append(attend_forward(q[j * length : (j + 1) * length], keys, values, keep))
            ctx_ref[span, lanes] = jnp.concatenate(out, axis=0).astype(BF16)
        return carry

    lax.fori_loop(0, images // 2, pair, 0, unroll=4)
    xhat, rstd = normalize(hidden1 + dot_nn(ctx_ref[...], wout_ref[...]))
    xhat_ref[...] = xhat
    rstd_ref[...] = rstd

    if gathers:

        @pl.when(step == steps - 1)
        def _():
            gather.pair(3)
            gather.finish()


def gelu_parts(inputs):
    cdf = 0.5 * (1.0 + lax.erf(inputs * 0.7071067811865476))
    density = jnp.exp(inputs * inputs * -0.5) * 0.3989422804014327
    return inputs * cdf, cdf + inputs * density


def feed_forward_kernel(
    length, bound_ref, which_ref, temp_ref, xhat2_ref, rstd2_ref, norm_ref,
    wup_ref, wdown_ref, adj_ref, target_ref, images_ref, wtext_ref,
    out_ref, loss_ref, pack_ref, dr2_ref, dup_ref, ddown_ref, dgain2_ref, dshift2_ref, dgain3_ref, dshift3_ref,
    dtext_ref, dtemp_ref,
    act_ref, slope_ref, final_ref, grad_ref, lead_ref, up_acc, down_acc, text_acc,
):
    step = pl.program_id(0)
    steps = pl.num_programs(0)
    tokens, width = xhat2_ref.shape
    hidden_units = wup_ref.shape[0]
    rows = tokens // length
    chunk = min(768, hidden_units)

    @pl.when(step == 0)
    def _():
        for ref in (dgain2_ref, dshift2_ref, dgain3_ref, dshift3_ref, dtemp_ref, up_acc, down_acc, text_acc):
            ref[...] = jnp.zeros_like(ref)

    xhat2 = xhat2_ref[...]
    hidden2 = xhat2 * norm_ref[2:3] + norm_ref[3:4]
    low = hidden2.astype(BF16)
    final_ref[...] = hidden2

    def forward(index, carry):
        at = pl.ds(pl.multiple_of(index * chunk, chunk), chunk)
        act, slope = gelu_parts(dot_nt(low, wup_ref[at, :]))
        act = act.astype(BF16)
        act_ref[:, at] = act
        slope_ref[:, at] = slope
        final_ref[...] += dot_nn(act, wdown_ref[at, :])
        return carry

    lax.fori_loop(0, hidden_units // chunk, forward, 0, unroll=True)
    xhat3, rstd3 = normalize(final_ref[...])
    final = xhat3 * norm_ref[4:5] + norm_ref[5:6]
    out_ref[...] = final.astype(BF16)
    final_ref[...] = final
    grad_ref[...] = adj_ref[...].astype(F32)

    for row in range(rows):
        lead_ref[pl.ds(2 * row, 1), :] = final_ref[pl.ds(row * length, 1), :]
        second = row * length + bound_ref[step * rows + row]
        lead_ref[pl.ds(2 * row + 1, 1), :] = final_ref[pl.ds(second, 1), :]
    lead = lead_ref[...].astype(BF16)
    raw = dot_nn(lead, wtext_ref[...])
    text = raw * lax.rsqrt(jnp.sum(raw * raw, axis=-1, keepdims=True) + NORM_EPS)
    text_low = text.astype(BF16)
    temp = temp_ref[0]
    logits = dot_nt(text_low, images_ref[...]) / temp
    top = jnp.max(logits, axis=1, keepdims=True)
    lse = top + jnp.log(jnp.sum(jnp.exp(logits - top), axis=1, keepdims=True))
    target = target_ref[...]
    hit = lax.broadcasted_iota(jnp.int32, logits.shape, 1) == target
    loss_ref[...] = lse - jnp.sum(jnp.where(hit, logits, 0.0), axis=1, keepdims=True)
    dlogits = jnp.exp(logits - lse) - hit.astype(F32)
    dtemp_ref[...] += -jnp.sum(jnp.sum(dlogits * logits, axis=1, keepdims=True), axis=0, keepdims=True) / temp
    embed = raw.shape[1]
    lane = lax.broadcasted_iota(jnp.int32, (2 * rows, 128), 1)
    pack_ref[:, :embed] = text_low.astype(F32)
    pack_ref[:, embed:] = jnp.where(lane == 0, lse, jnp.where(lane == 1, target.astype(F32), 0.0))
    dtext = dot_nn((dlogits / temp).astype(BF16), images_ref[...])
    draw = unit_pull(raw, dtext).astype(BF16)
    text_acc[...] += dot_tn(lead, draw)
    lead_ref[...] = dot_nt(draw, wtext_ref[...])
    for row in range(rows):
        first = pl.ds(row * length, 1)
        grad_ref[first, :] += lead_ref[pl.ds(2 * row, 1), :]
        second = pl.ds(row * length + bound_ref[step * rows + row], 1)
        grad_ref[second, :] += lead_ref[pl.ds(2 * row + 1, 1), :]

    dr3, dgain3, dshift3 = norm_pull(grad_ref[...], xhat3, rstd3, norm_ref[4:5])
    dgain3_ref[...] += dgain3
    dshift3_ref[...] += dshift3
    grad_ref[...] = dr3
    dfinal = dr3.astype(BF16)
    own = hidden_units // 4
    own_at = pl.ds(pl.multiple_of(which_ref[0] * own, own), own)
    down_acc[...] += dot_tn(act_ref[:, own_at], dfinal)

    def backward(index, carry):
        at = pl.ds(pl.multiple_of(index * chunk, chunk), chunk)
        dact = dot_nt(dfinal, wdown_ref[at, :])
        dinner = (dact * slope_ref[:, at]).astype(BF16)
        act_ref[:, at] = dinner
        grad_ref[...] += dot_nn(dinner, wup_ref[at, :])
        return carry

    lax.fori_loop(0, hidden_units // chunk, backward, 0, unroll=True)
    up_acc[...] += dot_tn(low, act_ref[:, own_at])
    dr2, dgain2, dshift2 = norm_pull(grad_ref[...], xhat2, rstd2_ref[...], norm_ref[2:3])
    dgain2_ref[...] += dgain2
    dshift2_ref[...] += dshift2
    dr2_ref[...] = dr2

    @pl.when(step == steps - 1)
    def _():
        dup_ref[...] = up_acc[...].astype(BF16)
        ddown_ref[...] = down_acc[...].astype(BF16)
        dtext_ref[...] = text_acc[...].astype(BF16)


def cross_backward_kernel(
    patch_count, length, which_ref, region_ref, kv_ref, cq_ref, ctx_ref, xhat1_ref, rstd1_ref, norm_ref,
    dr2_ref, wkv_ref, wout_ref, wcq_ref,
    dregion_ref, dr1_ref, dkv_ref, dqo_ref, dgain_ref, dshift_ref,
    dctx_ref, dq_ref, grads_ref, flat_ref, stage_ref, kv_acc, cq_acc, out_acc, sem,
):
    step = pl.program_id(0)
    steps = pl.num_programs(0)
    images, padded, vision = region_ref.shape
    width = cq_ref.shape[1]
    own = width // 4
    which = which_ref[0]
    mine = window(which, GROUP)
    wide = stage_ref.shape[2]
    parts = wide // images
    stored = flat_ref.shape[1] // wide

    @pl.when(step == 0)
    def _():
        for ref in (dgain_ref, dshift_ref, kv_acc, cq_acc, out_acc):
            ref[...] = jnp.zeros_like(ref)

    dr2 = dr2_ref[...]
    dx = dr2.astype(BF16)
    dctx_ref[...] = dot_nt(dx, wout_ref[...]).astype(BF16)
    out_acc[...] += dot_tn(ctx_ref[:, mine], dx)
    keep = lax.broadcasted_iota(jnp.int32, (padded, 4 * length), 0) < patch_count

    def pair(index, carry):
        span = pl.ds(pl.multiple_of(index * 2 * length, 16), 2 * length)
        for group in range(width // GROUP):
            lanes = slice(group * GROUP, (group + 1) * GROUP)
            value_lanes = slice(width + group * GROUP, width + (group + 1) * GROUP)
            q = cq_ref[span, lanes].astype(F32)
            d = dctx_ref[span, lanes].astype(F32)
            out = []
            for j in range(2):
                image = 2 * index + j
                at = slice(j * length, (j + 1) * length)
                dq, dk, dv = attend_backward(
                    q[at], kv_ref[image, :, lanes], kv_ref[image, :, value_lanes], keep, d[at]
                )
                out.append(dq)
                grads_ref[image, :, lanes] = dk.astype(BF16)
                grads_ref[image, :, value_lanes] = dv.astype(BF16)
            dq_ref[span, lanes] = jnp.concatenate(out, axis=0).astype(BF16)
        return carry

    lax.fori_loop(0, images // 2, pair, 0, unroll=4)

    some = 4
    for index in range(images // some):
        grads = grads_ref[index * some : (index + 1) * some].reshape(some * padded, 2 * width)
        dregion = dot_nn(grads, wkv_ref[...])
        for image in range(some):
            spot = pl.ds(step % parts * images + index * some + image, stored, stride=wide)
            for lane in range(vision // 128):
                flat_ref[lane, spot, :] = dregion[
                    image * padded : image * padded + stored, lane * 128 : (lane + 1) * 128
                ]
    region = region_ref[...].reshape(images * padded, vision)
    for part in range(2):
        at = window(which, GROUP)
        grads = grads_ref[:, :, pl.ds(pl.multiple_of(which * 3 // 2 * 128 + part * width, 128), GROUP)]
        kv_acc[part] += dot_tn(grads.reshape(images * padded, GROUP), region)

    pieces = 5
    patches = patch_count // pieces
    tall = patches * wide

    def send(index):
        slot = index % 2
        base = pl.multiple_of(step // parts * wide, 16)
        return pltpu.make_async_copy(
            stage_ref.at[slot],
            dregion_ref.at[pl.ds(index * patches, patches), pl.ds(base, wide), :],
            sem.at[slot],
        )

    @pl.when(step % parts == parts - 1)
    def _():
        for index in range(pieces):
            rows = slice(index * tall, (index + 1) * tall)
            low = jnp.concatenate([flat_ref[c, rows, :].astype(BF16) for c in range(vision // 128)], axis=1)
            if index >= 2:
                send(index - 2).wait()
            stage_ref[index % 2] = low.reshape(patches, wide, vision)
            send(index).start()
        send(pieces - 2).wait()
        send(pieces - 1).wait()

    xhat1 = xhat1_ref[...]
    hidden1 = (xhat1 * norm_ref[0:1] + norm_ref[1:2]).astype(BF16)
    cq_acc[...] += dot_tn(dq_ref[:, mine], hidden1)
    dh1 = dr2 + dot_nn(dq_ref[...], wcq_ref[...])
    dr1, dgain, dshift = norm_pull(dh1, xhat1, rstd1_ref[...], norm_ref[0:1])
    dr1_ref[...] = dr1
    dgain_ref[...] += dgain
    dshift_ref[...] += dshift

    @pl.when(step == steps - 1)
    def _():
        for part in range(2):
            dkv_ref[part * own : (part + 1) * own, :] = own_rows(kv_acc[part], which, own).astype(BF16)
        dqo_ref[:own, :] = own_rows(cq_acc[...], which, own).astype(BF16)
        dqo_ref[own:, :] = own_rows(out_acc[...], which, own).astype(BF16)


def self_backward_kernel(length, sums, *refs):
    bound_ref, tok_ref, qkv_ref, ctx_ref, dr1_ref, wqkv_ref, wout_ref = refs[:7]
    refs = refs[7:]
    if sums:
        dkv_ref, dqo_ref, temp_ref, pack_ref, picture_ref, wimage_ref = refs[:6]
        vectors, refs = refs[6:13], refs[13:]
    dtok_ref, last_ref = refs[:2]
    refs = refs[2:]
    if sums:
        outs, dpicture_ref, refs = refs[:4], refs[4], refs[5:]
    dctx_ref, grads_ref, qkv_acc, out_acc, last = refs[:5]
    refs = refs[5:]
    step = pl.program_id(0)
    steps = pl.num_programs(0)
    tokens, width = tok_ref.shape
    rows = tokens // length
    own = width // 4
    which = lax.axis_index("mp")
    if sums:
        packs, dimage, small, pack_sent, pack_came = refs[:5]
        refs = refs[5:]
        spots = (dkv_ref, dqo_ref, small, dimage, last.at[: 2 * own], last.at[2 * own :])
        kv_sum, qo_sum, small_sum, image_sum, *finals = (
            Reduce(spot, *refs[6 * i : 6 * i + 6]) for i, spot in enumerate(spots)
        )
        dp, z = lax.axis_index("dp"), lax.axis_index("mp")
        dp_size = packs.shape[0]

        def pack_copy(k, owner):
            return pltpu.make_async_remote_copy(
                src_ref=pack_ref, dst_ref=packs.at[owner], send_sem=pack_sent.at[k], recv_sem=pack_came.at[k],
                device_id=((dp + k) % dp_size, z), device_id_type=MESH,
            )

        @pl.when(step == 0)
        def _():
            small[...] = jnp.zeros(small.shape, BF16)
            lines = [ref[...] for ref in vectors[:6]] + [jnp.broadcast_to(vectors[6][...], (1, width))]
            lines = [*lines, jnp.zeros((16 - len(lines), width), F32)]
            small[0:16, :] = jnp.concatenate(lines, axis=0).astype(BF16)
            barrier = pltpu.get_barrier_semaphore()
            for k in range(1, dp_size):
                pl.semaphore_signal(barrier, inc=1, device_id=((dp + k) % dp_size, z), device_id_type=MESH)
            pl.semaphore_wait(barrier, dp_size - 1)
            for k in range(1, dp_size):
                pack_copy(k, dp).start()
            packs[dp] = pack_ref[...]
            for reduce in (kv_sum, qo_sum, small_sum):
                reduce.stage(1)

        @pl.when(step == 1)
        def _():
            for reduce in (kv_sum, qo_sum, small_sum):
                reduce.stage(2)
            for k in range(1, dp_size):
                pack_copy(k, (dp + dp_size - k) % dp_size).wait_recv()
                pack_copy(k, dp).wait_send()
            everyone = packs[...].reshape(-1, packs.shape[2])
            first = dp * picture_ref.shape[0]
            dpicture, dweight = image_backward(first, temp_ref[0], picture_ref[...], wimage_ref[...], everyone)
            dpicture_ref[...] = dpicture
            dimage[...] = dweight.astype(BF16)
            image_sum.stage(1)

        for number in (3, 4):

            @pl.when(step == number - 1)
            def _(number=number):
                for reduce in (kv_sum, qo_sum, small_sum):
                    reduce.stage(number)
                image_sum.stage(number - 1)

    @pl.when(step == 0)
    def _():
        for ref in (qkv_acc, out_acc):
            ref[...] = jnp.zeros_like(ref)

    dr1 = dr1_ref[...]
    da = dr1.astype(BF16)
    dctx_ref[...] = dot_nt(da, wout_ref[...]).astype(BF16)
    out_acc[...] += dot_tn(ctx_ref[:, window(which, GROUP)], da)

    def pair(index, carry):
        span = pl.ds(pl.multiple_of(index * 2 * length, 16), 2 * length)
        keeps = [row_keep(bound_ref[step * rows + 2 * index + j], length) for j in range(2)]
        for group in range(width // GROUP):
            q, k, v = (
                qkv_ref[span, part * width + group * GROUP : part * width + (group + 1) * GROUP].astype(F32)
                for part in range(3)
            )
            d = dctx_ref[span, group * GROUP : (group + 1) * GROUP].astype(F32)
            outs = []
            for j in range(2):
                at = slice(j * length, (j + 1) * length)
                outs.append(attend_backward(q[at], k[at].astype(BF16), v[at].astype(BF16), keeps[j], d[at]))
            for part in range(3):
                both = jnp.concatenate([outs[0][part], outs[1][part]], axis=0).astype(BF16)
                grads_ref[span, part * width + group * GROUP : part * width + (group + 1) * GROUP] = both
        return carry

    lax.fori_loop(0, rows // 2, pair, 0, unroll=4)
    tok = tok_ref[...]
    for part in range(3):
        mine = grads_ref[:, pl.ds(pl.multiple_of(which * 3 // 2 * 128 + part * width, 128), GROUP)]
        qkv_acc[part] += dot_tn(mine, tok)

    @pl.when(step == steps - 1)
    def _():
        for part in range(3):
            last[part * own : (part + 1) * own, :] = own_rows(qkv_acc[part], which, own).astype(BF16)
        last[3 * own : 4 * own, :] = own_rows(out_acc[...], which, own).astype(BF16)
        if sums:
            for reduce in finals:
                reduce.stage(1)

    dtok_ref[...] = dr1 + dot_nn(grads_ref[...], wqkv_ref[...])

    @pl.when(step == steps - 1)
    def _():
        if sums:
            image_sum.stage(4)
            for number in range(2, 6):
                for reduce in finals:
                    reduce.stage(number)
            for reduce in (kv_sum, qo_sum, small_sum, image_sum):
                reduce.stage(5)
            for reduce, out in zip((kv_sum, qo_sum, small_sum, image_sum), outs, strict=True):
                out[...] = reduce.done[...]
            last_ref[: 2 * own, :] = finals[0].done[...]
            last_ref[2 * own :, :] = finals[1].done[...]
        else:
            last_ref[...] = last[...]


def image_backward(first, temp, picture, weight, pack):
    raw = dot_nn(picture, weight)
    own = (raw * lax.rsqrt(jnp.sum(raw * raw, axis=-1, keepdims=True) + NORM_EPS)).astype(BF16)
    embed = raw.shape[1]
    text = pack[:, :embed].astype(BF16)
    lse = pack[:, embed : embed + 1]
    target = pack[:, embed + 1 : embed + 2].astype(jnp.int32)
    logits = dot_nt(text, own) / temp
    hit = lax.broadcasted_iota(jnp.int32, logits.shape, 1) + first == target
    dlogits = jnp.exp(logits - lse) - hit.astype(F32)
    dimage = dot_tn((dlogits / temp).astype(BF16), text)
    draw = unit_pull(raw, dimage).astype(BF16)
    return dot_nt(draw, weight), dot_tn(picture, draw)


def image_backward_kernel(
    first_ref, temp_ref, picture_ref, weight_ref, pack_ref, dpicture_ref, dweight_ref
):
    dpicture, dweight = image_backward(
        first_ref[0], temp_ref[0], picture_ref[...], weight_ref[...], pack_ref[...]
    )
    dpicture_ref[...] = dpicture
    dweight_ref[...] = dweight.astype(BF16)


def widen_kernel(own, last_ref, dkv_ref, dqo_ref, dimage_ref, dup_ref, ddown_ref, dtext_ref, small_ref, *outs):
    for index in range(4):
        outs[index][...] = last_ref[index * own : (index + 1) * own, :].astype(F32)
    for index in range(2):
        outs[4 + index][...] = dqo_ref[index * own : (index + 1) * own, :].astype(F32)
        outs[6 + index][...] = dkv_ref[index * own : (index + 1) * own, :].astype(F32)
    for out, ref in zip(outs[8:12], (dup_ref, ddown_ref, dtext_ref, dimage_ref), strict=True):
        out[...] = ref[...].astype(F32)
    small = small_ref[0:16, :].astype(F32)
    for index in range(6):
        outs[12 + index][...] = small[index]
    outs[18][...] = small[6:7, 0:1]


def full(shape):
    return pl.BlockSpec(shape, lambda i: (0,) * len(shape), pipeline_mode=pl.Buffered(1))


def fixed(shape):
    return pl.BlockSpec(shape, lambda i: (0,) * len(shape))


def rows_of(count, width):
    return pl.BlockSpec((count, width), lambda i: (i, 0))


SMEM = pl.BlockSpec(memory_space=pltpu.SMEM)


def shape_of(shape, kind):
    return jax.ShapeDtypeStruct(shape, kind)


def call(kernel, steps, ins, outs, args, scratch=(), flops=0, moved=0, ident=None):
    specs, shapes = zip(*outs, strict=True)
    remote = {} if ident is None else {"collective_id": ident, "has_side_effects": True}
    return pl.pallas_call(
        kernel,
        grid=(steps,),
        in_specs=list(ins),
        out_specs=list(specs),
        out_shape=list(shapes),
        scratch_shapes=list(scratch),
        compiler_params=pltpu.CompilerParams(
            vmem_limit_bytes=VMEM_LIMIT, dimension_semantics=("arbitrary",), **remote
        ),
        cost_estimate=pl.CostEstimate(flops=flops, bytes_accessed=moved, transcendentals=0),
    )(*args)


DEPTH = 4


def gathered(groups):
    shapes = [(len(group), *group[0].shape) for group in groups]
    outs = [
        (pl.BlockSpec(memory_space=pl.ANY), shape_of((shape[0], DEPTH, *shape[1:]), BF16)) for shape in shapes
    ]
    scratch = [pltpu.VMEM(shape, BF16) for shape in shapes]
    specs = [full(shard.shape) for group in groups for shard in group]
    return specs, outs, [*scratch, *Gather.semaphores(len(groups), DEPTH)] if groups else []


def flatten(groups):
    return [shard for group in groups for shard in group]


TOKEN_ROWS = 8
IMAGE_ROWS = 16


def square(width, index):
    return pl.BlockSpec((width, width), lambda i: (index, 0), pipeline_mode=pl.Buffered(1))


def run_prep(region, picture, wimage, shards):
    patch_count, rows, vision = region.shape
    padded = -(-patch_count // 16) * 16
    embed = wimage.shape[1]
    specs, outs, sems = gathered(shards)
    return call(
        partial(prep_kernel, len(shards), len(flatten(shards))),
        vision // 128,
        [pl.BlockSpec((patch_count, rows, 128), lambda i: (0, 0, i)), full(picture.shape), full(wimage.shape), *specs],
        [
            (pl.BlockSpec((rows, padded, 128), lambda i: (0, 0, i)), shape_of((rows, padded, vision), BF16)),
            (fixed((rows, embed)), shape_of((rows, embed), BF16)),
            *outs,
        ],
        (region, picture, wimage, *flatten(shards)),
        scratch=[pltpu.VMEM((patch_count * rows, 128), F32), *sems],
        moved=4 * rows * padded * vision,
        ident=1 if shards else None,
    )


def run_self_forward(length, dp_size, bound, tok, squares, embed, shards):
    tokens, width = tok.shape
    block = TOKEN_ROWS * length
    specs, outs, sems = gathered(shards)
    if shards:
        shape = shape_of((dp_size * embed.shape[0], embed.shape[1]), BF16)
        outs = [*outs, (pl.BlockSpec(memory_space=pl.ANY), shape)]
        sems = [DMA, DMA((dp_size,)), DMA((dp_size,)), *sems]
    return call(
        partial(self_forward_kernel, length, len(shards), len(flatten(shards))),
        tokens // block,
        [SMEM, rows_of(block, width), full((3 * width, width)), square(width, 3), full(embed.shape), *specs],
        [
            (rows_of(block, 3 * width), shape_of((tokens, 3 * width), BF16)),
            (rows_of(block, width), shape_of((tokens, width), BF16)),
            (rows_of(block, width), shape_of((tokens, width), F32)),
            (rows_of(block, 1), shape_of((tokens, 1), F32)),
            *outs,
        ],
        (bound, tok, squares, squares, embed, *flatten(shards)),
        scratch=sems,
        flops=10 * tokens * width * width,
        moved=20 * tokens * width,
        ident=2 if shards else None,
    )


def run_cross_forward(length, patch_count, region, wkv, xhat1, norms, wcq, wout, shards):
    rows, padded, vision = region.shape
    tokens, width = xhat1.shape
    images = TOKEN_ROWS
    block = images * length
    specs, outs, sems = gathered(shards)
    return call(
        partial(cross_forward_kernel, patch_count, length, len(shards), len(flatten(shards))),
        rows // images,
        [
            pl.BlockSpec((images, padded, vision), lambda i: (i, 0, 0)), full((2 * width, vision)),
            rows_of(block, width), full(norms.shape), square(width, 0), square(width, 1), *specs,
        ],
        [
            (
                pl.BlockSpec((images, padded, 2 * width), lambda i: (i, 0, 0)),
                shape_of((rows, padded, 2 * width), BF16),
            ),
            (rows_of(block, width), shape_of((tokens, width), BF16)),
            (rows_of(block, width), shape_of((tokens, width), BF16)),
            (rows_of(block, width), shape_of((tokens, width), F32)),
            (rows_of(block, 1), shape_of((tokens, 1), F32)),
            *outs,
        ],
        (region, wkv, xhat1, norms, wcq, wout, *flatten(shards)),
        scratch=sems,
        flops=4 * rows * padded * width * vision,
        moved=2 * rows * padded * (vision + 2 * width),
        ident=3 if shards else None,
    )


def run_feed_forward(
    length, bound, which, temp, xhat2, rstd2, norms, ffn, adjoint, target, image_all, wtext
):
    tokens, width = xhat2.shape
    hidden_units = ffn.shape[0] // 2
    embed = wtext.shape[1]
    block = IMAGE_ROWS * length
    captions = 2 * IMAGE_ROWS
    ff_own = hidden_units // 4
    return call(
        partial(feed_forward_kernel, length),
        tokens // block,
        [
            SMEM, SMEM, SMEM, rows_of(block, width), rows_of(block, 1), full(norms.shape),
            full((hidden_units, width)),
            pl.BlockSpec((hidden_units, width), lambda i: (1, 0), pipeline_mode=pl.Buffered(1)),
            rows_of(block, width), rows_of(captions, 1),
            full(image_all.shape), full((width, embed)),
        ],
        [
            (rows_of(block, width), shape_of((tokens, width), BF16)),
            (rows_of(captions, 1), shape_of(target.shape, F32)),
            (rows_of(captions, embed + 128), shape_of((target.shape[0], embed + 128), F32)),
            (rows_of(block, width), shape_of((tokens, width), F32)),
            (fixed((width, ff_own)), shape_of((width, ff_own), BF16)),
            (fixed((ff_own, width)), shape_of((ff_own, width), BF16)),
            (fixed((1, width)), shape_of((1, width), F32)),
            (fixed((1, width)), shape_of((1, width), F32)),
            (fixed((1, width)), shape_of((1, width), F32)),
            (fixed((1, width)), shape_of((1, width), F32)),
            (fixed((width, embed)), shape_of((width, embed), BF16)),
            (fixed((1, 1)), shape_of((1, 1), F32)),
        ],
        (
            bound, which, temp, xhat2, rstd2, norms, ffn, ffn, adjoint, target, image_all,
            wtext,
        ),
        scratch=[
            pltpu.VMEM((block, hidden_units), BF16),
            pltpu.VMEM((block, hidden_units), F32),
            pltpu.VMEM((block, width), F32),
            pltpu.VMEM((block, width), F32),
            pltpu.VMEM((captions, width), F32),
            pltpu.VMEM((width, ff_own), F32),
            pltpu.VMEM((ff_own, width), F32),
            pltpu.VMEM((width, embed), F32),
        ],
        flops=10 * tokens * width * hidden_units,
        moved=20 * tokens * width,
    )


def run_cross_backward(length, patch_count, which, region, kv, cq, ctx2, xhat1, rstd1, norms, dr2, wkv, wcq, wout):
    rows, padded, vision = region.shape
    tokens, width = cq.shape
    images = TOKEN_ROWS
    block = images * length
    own = width // 4
    stored = -(-patch_count // 8) * 8
    return call(
        partial(cross_backward_kernel, patch_count, length),
        rows // images,
        [
            SMEM,
            pl.BlockSpec((images, padded, vision), lambda i: (i, 0, 0)),
            pl.BlockSpec((images, padded, 2 * width), lambda i: (i, 0, 0)),
            rows_of(block, width), rows_of(block, width), rows_of(block, width), rows_of(block, 1), full(norms.shape),
            rows_of(block, width), full((2 * width, vision)), square(width, 1), square(width, 0),
        ],
        [
            (pl.BlockSpec(memory_space=pl.ANY), shape_of((patch_count, rows, vision), BF16)),
            (rows_of(block, width), shape_of((tokens, width), F32)),
            (fixed((2 * own, vision)), shape_of((2 * own, vision), BF16)),
            (fixed((2 * own, width)), shape_of((2 * own, width), BF16)),
            (fixed((1, width)), shape_of((1, width), F32)),
            (fixed((1, width)), shape_of((1, width), F32)),
        ],
        (which, region, kv, cq, ctx2, xhat1, rstd1, norms, dr2, wkv, wout, wcq),
        scratch=[
            pltpu.VMEM((block, width), BF16),
            pltpu.VMEM((block, width), BF16),
            pltpu.VMEM((images, padded, 2 * width), BF16),
            pltpu.VMEM((vision // 128, stored * IMAGE_ROWS, 128), F32),
            pltpu.VMEM((2, patch_count // 5, IMAGE_ROWS, vision), BF16),
            pltpu.VMEM((2, GROUP, vision), F32),
            pltpu.VMEM((GROUP, width), F32),
            pltpu.VMEM((GROUP, width), F32),
            DMA((2,)),
        ],
        flops=6 * rows * padded * width * vision,
        moved=2 * rows * padded * 2 * (vision + width),
    )


def run_self_backward(length, dp_size, bound, tok, qkv, ctx1, dr1, selves, others):
    tokens, width = tok.shape
    block = TOKEN_ROWS * length
    last = shape_of((width, width), BF16)
    extra, outs, scratch = [], [], []
    if others:
        dkv, dqo, _, pack, picture, wimage, *vectors = others
        image = shape_of(wimage.shape, BF16)
        small = shape_of((128, width), BF16)
        half = (width // 2, width)
        shapes = [shape_of(dkv.shape, BF16), shape_of(dqo.shape, BF16), small, image]
        extra = [full(dkv.shape), full(dqo.shape), SMEM, *(full(other.shape) for other in others[3:])]
        outs = [*((fixed(shape.shape), shape) for shape in shapes), (fixed(picture.shape), shape_of(picture.shape, F32))]
        scratch = [
            pltpu.VMEM((dp_size, *pack.shape), F32), pltpu.VMEM(image.shape, BF16), pltpu.VMEM(small.shape, BF16),
            DMA((dp_size,)), DMA((dp_size,)),
            *(spot for shape in (*(shape.shape for shape in shapes), half, half) for spot in Reduce.scratch(shape)),
        ]
    return call(
        partial(self_backward_kernel, length, bool(others)),
        tokens // block,
        [
            SMEM, rows_of(block, width), rows_of(block, 3 * width), rows_of(block, width), rows_of(block, width),
            full((3 * width, width)), square(width, 3), *extra,
        ],
        [(rows_of(block, width), shape_of((tokens, width), F32)), (fixed(last.shape), last), *outs],
        (bound, tok, qkv, ctx1, dr1, selves, selves, *others),
        scratch=[
            pltpu.VMEM((block, width), BF16),
            pltpu.VMEM((block, 3 * width), BF16),
            pltpu.VMEM((3, GROUP, width), F32),
            pltpu.VMEM((GROUP, width), F32),
            pltpu.VMEM(last.shape, BF16),
            *scratch,
        ],
        flops=10 * tokens * width * width,
        moved=20 * tokens * width,
        ident=4 if others else None,
    )


def run_widen(last, dkv, dqo, dimage, dup, ddown, dtext, small):
    width = last.shape[1]
    own = width // 4
    shapes = [(own, width)] * 6 + [(own, dkv.shape[1])] * 2
    shapes += [dup.shape, ddown.shape, dtext.shape, dimage.shape] + [(width,)] * 6 + [(1, 1)]
    args = (last, dkv, dqo, dimage, dup, ddown, dtext, small)
    return call(
        partial(widen_kernel, own),
        1,
        [fixed(array.shape) for array in args],
        [(fixed(shape), shape_of(shape, F32)) for shape in shapes],
        args,
        moved=20 * width * width,
    )


def body(
    dp_size,
    word_features,
    sentence_numbering,
    region_features,
    picture_global_feature,
    matched_picture,
    sharpness_array,
    incoming_adjoint,
    intra_asking_map,
    intra_lookup_map,
    intra_content_map,
    intra_attend_exit_map,
    visual_asking_map,
    visual_lookup_map,
    visual_content_map,
    visual_attend_exit_map,
    mlp_widening_factor,
    mlp_narrowing_factor,
    initial_standardize_scale,
    initial_standardize_offset,
    middle_standardize_scale,
    middle_standardize_offset,
    final_standardize_scale,
    final_standardize_offset,
    sentence_mapping_factor,
    picture_mapping_factor,
):
    rows, length = sentence_numbering.shape
    tokens, width = word_features.shape
    patch_count, vision = region_features.shape[1:]
    embed = sentence_mapping_factor.shape[1]
    hidden_units = mlp_widening_factor.shape[1] * 4
    own = width // 4
    which = lax.axis_index("mp").astype(jnp.int32).reshape(1)
    bound = (length - jnp.sum(sentence_numbering, axis=1)).astype(jnp.int32)
    target = matched_picture.reshape(-1, 1)
    norms = jnp.stack([
        initial_standardize_scale, initial_standardize_offset, middle_standardize_scale,
        middle_standardize_offset, final_standardize_scale, final_standardize_offset,
    ])

    selves = (intra_asking_map.T, intra_lookup_map.T, intra_content_map.T, intra_attend_exit_map)
    crosses = (visual_asking_map.T, visual_attend_exit_map)
    wides = (visual_lookup_map.T, visual_content_map.T)
    ffns = (mlp_widening_factor.T, mlp_narrowing_factor)
    region = jnp.transpose(region_features, (1, 0, 2))
    local = dp_size == 8 and lax.axis_size("mp") == DEPTH

    def each(*shards):
        return list(shards) if local else []

    region, image_own, *found = run_prep(region, picture_global_feature, picture_mapping_factor, each(selves))
    selves = (found[0] if local else lax.all_gather(jnp.stack(selves), "mp", axis=1)).reshape(-1, width)
    qkv, ctx1, xhat1, rstd1, *found = run_self_forward(
        length, dp_size, bound, word_features, selves, image_own, each(crosses, wides)
    )
    if local:
        crosses, wides, image_all = found
    else:
        crosses, wides = (lax.all_gather(jnp.stack(group), "mp", axis=1) for group in (crosses, wides))
        image_all = lax.all_gather(image_own, "dp", axis=0, tiled=True)
    crosses = crosses.reshape(-1, width)
    wkv = wides.reshape(-1, vision)
    kv, cq, ctx2, xhat2, rstd2, *found = run_cross_forward(
        length, patch_count, region, wkv, xhat1, norms, crosses, crosses, each(ffns)
    )
    ffns = (found[0] if local else lax.all_gather(jnp.stack(ffns), "mp", axis=1)).reshape(-1, width)
    (
        block_exit, loss, pack, dr2, dup, ddown, dgain2, dshift2, dgain3, dshift3, dtext, dtemp,
    ) = run_feed_forward(
        length, bound, which, sharpness_array, xhat2, rstd2, norms, ffns, incoming_adjoint, target, image_all,
        sentence_mapping_factor,
    )

    dp_sum = lambda grad: lax.psum(grad, "dp")
    dup, ddown, dtext = dp_sum((dup, ddown, dtext))
    dregion, dr1, dkv, dqo, dgain1, dshift1 = run_cross_backward(
        length, patch_count, which, region, kv, cq, ctx2, xhat1, rstd1, norms, dr2, wkv, crosses, crosses
    )
    vectors = (dgain1, dshift1, dgain2, dshift2, dgain3, dshift3, dtemp)
    pictures = (picture_global_feature, picture_mapping_factor)
    dtok, last, *found = run_self_backward(
        length, dp_size, bound, word_features, qkv, ctx1, dr1, selves,
        each(dkv, dqo, sharpness_array, pack, *pictures, *vectors),
    )
    if local:
        dkv, dqo, small, dimage, dpicture = found
    else:
        pack_all = lax.all_gather(pack, "dp", axis=0, tiled=True)
        first = (lax.axis_index("dp") * rows).astype(jnp.int32).reshape(1)
        dpicture, dimage = call(
            image_backward_kernel,
            1,
            [SMEM, SMEM, *(full(array.shape) for array in (*pictures, pack_all))],
            [
                (fixed((rows, vision)), shape_of((rows, vision), F32)),
                (fixed((vision, embed)), shape_of((vision, embed), BF16)),
            ],
            (first, sharpness_array, *pictures, pack_all),
        )
        lines = [*vectors[:6], jnp.broadcast_to(dtemp, (1, width)), jnp.zeros((9, width), F32)]
        small = jnp.concatenate(lines).astype(BF16)
        dkv, dqo, dimage, last, small = dp_sum((dkv, dqo, dimage, last, small))
    dq, dk, dv, dso, dcq, dco, dck, dcv, dup, ddown, dtext, dimage, *vectors = run_widen(
        last, dkv, dqo, dimage, dup, ddown, dtext, small
    )
    return (
        loss.reshape(rows, 2),
        block_exit,
        dtok,
        jnp.transpose(dregion, (1, 0, 2)),
        dpicture,
        vectors[6].reshape(1),
        dq.T,
        dk.T,
        dv.T,
        dso,
        dcq.T,
        dck.T,
        dcv.T,
        dco,
        dup,
        ddown,
        *vectors[:6],
        dtext,
        dimage,
    )


def solution(mesh):
    rows = P("dp", None)
    by_column = P(None, "mp")
    by_row = P("mp", None)
    in_specs = (
        rows, rows, P("dp", None, None), rows, rows, P(), rows,
        by_column, by_column, by_column, by_row, by_column, by_column, by_column, by_row, by_column, by_row,
        P(), P(), P(), P(), P(), P(), P(), P(),
    )
    out_specs = (
        rows, rows, rows, P("dp", None, None), rows, P(),
        by_column, by_column, by_column, by_row, by_column, by_column, by_column, by_row, by_column, by_row,
        P(), P(), P(), P(), P(), P(), P(), P(),
    )
    return jax.shard_map(
        partial(body, mesh.shape["dp"]), mesh=mesh, in_specs=in_specs, out_specs=out_specs, check_vma=False
    )
```

```python
from functools import partial

import jax
import jax.numpy as jnp
from jax import lax
from jax.experimental import pallas as pl
from jax.experimental.pallas import tpu as pltpu
from jax.sharding import PartitionSpec as P

HEAD = 64
GROUP = 4 * HEAD
LN_EPS = 1e-06
NORM_EPS = 1e-06
BIG_NEG = -1000000000.0
F32 = jnp.float32
BF16 = jnp.bfloat16
VMEM_LIMIT = 60 * 2**20


def dot_nn(left, right):
    return lax.dot_general(left, right, (((1,), (0,)), ((), ())), preferred_element_type=F32)


def dot_nt(left, right):
    return lax.dot_general(left, right, (((1,), (1,)), ((), ())), preferred_element_type=F32)


def dot_tn(left, right):
    return lax.dot_general(left, right, (((0,), (0,)), ((), ())), preferred_element_type=F32)


def normalize(inputs):
    center = inputs - jnp.mean(inputs, axis=-1, keepdims=True)
    rstd = lax.rsqrt(jnp.mean(center * center, axis=-1, keepdims=True) + LN_EPS)
    return center * rstd, rstd


def norm_pull(grad, xhat, rstd, gain):
    scaled = grad * gain
    first = jnp.mean(scaled, axis=-1, keepdims=True)
    second = jnp.mean(scaled * xhat, axis=-1, keepdims=True)
    grad_in = rstd * (scaled - first - xhat * second)
    return grad_in, jnp.sum(grad * xhat, axis=0, keepdims=True), jnp.sum(grad, axis=0, keepdims=True)


def unit_pull(raw, grad):
    scale = lax.rsqrt(jnp.sum(raw * raw, axis=-1, keepdims=True) + NORM_EPS)
    inner = jnp.sum(grad * raw, axis=-1, keepdims=True)
    return scale * grad - raw * (scale * scale * scale * inner)


MESH = pl.DeviceIdType.MESH
DMA = pltpu.SemaphoreType.DMA


class Gather:
    def __init__(self, shards, outs, refs):
        count = len(outs)
        self.ins, self.outs, self.shards, sems = refs[:count], outs, shards, refs[count:]
        self.local, self.up, self.down, self.across, self.below, self.above, self.near, self.out, self.back = sems
        self.dp, self.z = lax.axis_index("dp"), lax.axis_index("mp")
        dp, z = self.dp, self.z
        self.core, self.x, self.y = dp % 2, dp // 2 % 2, dp // 4
        self.depth = outs[0].shape[1]
        self.color = (self.x + self.y) % 2
        east, north = 2 - 4 * self.x, 4 - 8 * self.y
        self.peers = [(dp + east, z), (dp + north, z), (dp + east + north, z)]
        self.twin = (dp + 1 - 2 * self.core, z)

    @staticmethod
    def semaphores(count, depth):
        grid = (count, depth)
        return [DMA((count,)), DMA(grid), DMA(grid), DMA((3, *grid)), DMA(grid), DMA(grid), DMA((3, *grid)), DMA(grid), DMA(grid)]

    def enter(self, everyone=0):
        barrier = pltpu.get_barrier_semaphore()
        peers = [*self.peers, self.twin]
        if everyone:
            peers = [((self.dp + k) % everyone, self.z) for k in range(1, everyone)]
        for peer in peers:
            pl.semaphore_signal(barrier, inc=1, device_id=peer, device_id_type=MESH)
        for step in (-1, 1):

            @pl.when(self.inside(self.z + step))
            def _(step=step):
                pl.semaphore_signal(barrier, inc=1, device_id=(self.dp, self.z + step), device_id_type=MESH)

        ends = (self.z > 0).astype(jnp.int32) + (self.z < self.depth - 1).astype(jnp.int32)
        pl.semaphore_wait(barrier, len(peers) + ends)

    def inside(self, z):
        return (z >= 0) & (z < self.depth)

    def part(self, index, source, first, size, core=None):
        mats = self.ins[index].shape[0] // 2
        core = self.core if core is None else core
        return self.outs[index].at[pl.ds(core * mats, mats), source, pl.ds(pl.multiple_of(first, 16), size), :]

    def copy(self, src, dst, send, recv, to):
        return pltpu.make_async_remote_copy(
            src_ref=src, dst_ref=dst, send_sem=send, recv_sem=recv, device_id=to, device_id_type=MESH
        )

    def span(self, index):
        tall = self.ins[index].shape[1]
        return self.color * (tall // 2) + self.y * (tall // 6), tall // 3

    def hop(self, index, source, step):
        spot = self.part(index, source, *self.span(index))
        send, recv = (self.up, self.below) if step > 0 else (self.down, self.above)
        return self.copy(spot, spot, send.at[index, source], recv.at[index, source], (self.dp, self.z + step))

    def first_hop(self, index, step):
        first, size = self.span(index)
        mats = self.ins[index].shape[0] // 2
        src = self.ins[index].at[pl.ds(self.core * mats, mats), pl.ds(pl.multiple_of(first, 16), size), :]
        send, recv = (self.up, self.below) if step > 0 else (self.down, self.above)
        spot = self.part(index, self.z, first, size)
        return self.copy(src, spot, send.at[index, self.z], recv.at[index, self.z], (self.dp, self.z + step))

    def side(self, index, source, which, inward=False):
        tall = self.ins[index].shape[1]
        color, y = self.color, self.y
        if inward:
            color, y = (1 - color, y) if which == 0 else (1 - color, 1 - y) if which == 1 else (color, 1 - y)
        pace, size = ((tall // 4, tall // 4), (tall // 4, tall // 4), (tall // 3, tall // 6))[which]
        spot = self.part(index, source, color * (tall // 2) + y * pace, size)
        sems = self.across.at[which, index, source], self.near.at[which, index, source]
        return self.copy(spot, spot, *sems, self.peers[which])

    def pass_on(self, index, source, inward=False):
        core = 1 - self.core if inward else self.core
        spot = self.part(index, source, 0, self.ins[index].shape[1], core)
        return self.copy(spot, spot, self.out.at[index, source], self.back.at[index, source], self.twin)

    def keep(self, index):
        return pltpu.make_async_copy(self.ins[index], self.outs[index].at[:, self.z], self.local.at[index])

    def start(self, everyone=0):
        count = 0
        for stack in self.ins:
            for index in range(stack.shape[0]):
                stack[index] = self.shards[count][...]
                count += 1
        self.enter(everyone)
        for index in range(len(self.ins)):
            for step in (1, -1):

                @pl.when(self.inside(self.z + step))
                def _(index=index, step=step):
                    self.first_hop(index, step).start()

            self.keep(index).start()

    def each(self, distance, what):
        for index in range(len(self.ins)):
            for step in (1, -1):
                source = self.z - step * distance

                @pl.when(self.inside(source))
                def _(index=index, step=step, source=source):
                    what(index, step, source)

    def pull(self, distance):
        def what(index, step, source):
            self.hop(index, source, step).wait_recv()

            @pl.when(self.inside(self.z + step))
            def _():
                self.hop(index, source, step).start()

            for which in range(3):
                self.side(index, source, which).start()

        self.each(distance, what)

    def pair(self, distance):
        def what(index, step, source):
            for which in range(3):
                self.side(index, source, which, inward=True).wait_recv()
            self.pass_on(index, source).start()

        self.each(distance, what)

    def finish(self):
        def what(index, step, source):
            self.pass_on(index, source, inward=True).wait_recv()
            self.pass_on(index, source).wait_send()
            for which in range(3):
                self.side(index, source, which).wait_send()

            @pl.when(self.inside(self.z + step))
            def _():
                self.hop(index, source, step).wait_send()

        for distance in range(1, self.depth):
            self.each(distance, what)
        for index in range(len(self.ins)):
            for step in (1, -1):

                @pl.when(self.inside(self.z + step))
                def _(index=index, step=step):
                    self.first_hop(index, step).wait_send()

            self.keep(index).wait()


class Reduce:
    def __init__(self, src, done, half, part, quarter, twin_sems, plane_sems):
        self.src, self.done, self.half, self.part, self.quarter = src, done, half, part, quarter
        self.twin_sems, self.plane_sems = twin_sems, plane_sems
        dp, z = lax.axis_index("dp"), lax.axis_index("mp")
        self.core, self.chip = dp % 2, dp // 2
        x, y = self.chip % 2, self.chip // 2
        east, north = 2 - 4 * x, 4 - 8 * y
        self.shifts = (east, north, east + north)
        self.peers = [(dp + shift, z) for shift in self.shifts]
        self.twin = (dp + 1 - 2 * self.core, z)
        self.tall = src.shape[0]

    @staticmethod
    def scratch(shape):
        rows, columns = shape
        sizes = ((rows, columns), (rows // 2, columns), (rows // 2, columns), (3, rows // 8, columns))
        return [*(pltpu.VMEM(size, BF16) for size in sizes), DMA((4,)), DMA((4, 3))]

    def enter(self):
        barrier = pltpu.get_barrier_semaphore()
        for peer in [*self.peers, self.twin]:
            pl.semaphore_signal(barrier, inc=1, device_id=peer, device_id_type=MESH)
        pl.semaphore_wait(barrier, 4)

    def copy(self, src, dst, send, recv, to):
        return pltpu.make_async_remote_copy(
            src_ref=src, dst_ref=dst, send_sem=send, recv_sem=recv, device_id=to, device_id_type=MESH
        )

    def mine(self, core):
        return pl.ds(pl.multiple_of(core * (self.tall // 2), 16), self.tall // 2)

    def slot(self, chip, core=None):
        first = chip * (self.tall // 8)
        if core is not None:
            first = first + core * (self.tall // 2)
        return pl.ds(pl.multiple_of(first, 16), self.tall // 8)

    def to_twin(self):
        sems = self.twin_sems.at[0], self.twin_sems.at[1]
        return self.copy(self.src.at[self.mine(1 - self.core)], self.half, *sems, self.twin)

    def scatter(self, which):
        chip = self.chip + self.shifts[which] // 2
        sems = self.plane_sems.at[0, which], self.plane_sems.at[1, which]
        return self.copy(self.part.at[self.slot(chip)], self.quarter.at[which], *sems, self.peers[which])

    def spread(self, which, chip):
        spot = self.done.at[self.slot(chip, self.core)]
        sems = self.plane_sems.at[2, which], self.plane_sems.at[3, which]
        return self.copy(spot, spot, *sems, self.peers[which])

    def back(self, core):
        spot = self.done.at[self.mine(core)]
        return self.copy(spot, spot, self.twin_sems.at[2], self.twin_sems.at[3], self.twin)

    def stage(self, number):
        if number == 1:
            self.to_twin().start()
        elif number == 2:
            self.to_twin().wait_recv()
            total = self.src[self.mine(self.core), :].astype(F32) + self.half[...].astype(F32)
            self.part[...] = total.astype(BF16)
            for which in range(3):
                self.scatter(which).start()
        elif number == 3:
            total = self.part[self.slot(self.chip), :].astype(F32)
            for which in range(3):
                self.scatter(which).wait_recv()
                total = total + self.quarter[which].astype(F32)
            self.done[self.slot(self.chip, self.core), :] = total.astype(BF16)
            for which in range(3):
                self.spread(which, self.chip).start()
        elif number == 4:
            for which in range(3):
                self.spread(which, self.chip + self.shifts[which] // 2).wait_recv()
            self.back(self.core).start()
        else:
            self.back(1 - self.core).wait_recv()
            self.to_twin().wait_send()
            for which in range(3):
                self.scatter(which).wait_send()
                self.spread(which, self.chip).wait_send()
            self.back(self.core).wait_send()


def spread_heads(tensor):
    count = tensor.shape[0]
    left = lax.broadcasted_iota(jnp.int32, (count, 2 * HEAD), 1) < HEAD
    low, high = tensor[:, : 2 * HEAD], tensor[:, 2 * HEAD :]
    zero = jnp.zeros_like(low)
    blank = jnp.zeros((2 * count, 2 * HEAD), tensor.dtype)
    near = jnp.concatenate([jnp.where(left, low, zero), jnp.where(left, zero, low), blank], axis=0)
    far = jnp.concatenate([blank, jnp.where(left, high, zero), jnp.where(left, zero, high)], axis=0)
    return jnp.concatenate([near, far], axis=1).astype(BF16)


def collect_heads(stacked, count):
    left = lax.broadcasted_iota(jnp.int32, (count, 2 * HEAD), 1) < HEAD
    low = jnp.where(left, stacked[:count, : 2 * HEAD], stacked[count : 2 * count, : 2 * HEAD])
    high = jnp.where(
        left, stacked[2 * count : 3 * count, 2 * HEAD :], stacked[3 * count :, 2 * HEAD :]
    )
    return jnp.concatenate([low, high], axis=1)


def attend_probs(query_blocks, keys, keep):
    scores = dot_nt(keys, query_blocks)
    scores = jnp.where(keep, scores, BIG_NEG)
    top = jnp.max(scores, axis=0, keepdims=True)
    shifted = jnp.exp(scores - top)
    total = jnp.sum(shifted, axis=0, keepdims=True)
    return shifted * (1.0 / total)


def attend_forward(query, keys, values, keep):
    probs = attend_probs(spread_heads(query), keys, keep).astype(BF16)
    return collect_heads(dot_tn(probs, values), query.shape[0]), probs


def split_heads(tensor):
    left = lax.broadcasted_iota(jnp.int32, tensor.shape, 1) < HEAD
    zero = jnp.zeros_like(tensor)
    return jnp.concatenate([jnp.where(left, tensor, zero), jnp.where(left, zero, tensor)], axis=0).astype(BF16)


def attend_short(query, keys, values, keep):
    count = query.shape[0]
    left = lax.broadcasted_iota(jnp.int32, (count, 2 * HEAD), 1) < HEAD
    out = []
    for half in range(2):
        at = slice(half * 2 * HEAD, (half + 1) * 2 * HEAD)
        probs = attend_probs(split_heads(query[:, at]), keys[:, at], keep[:, : 2 * count])
        stacked = dot_nn(jnp.transpose(probs.astype(BF16)), values[:, at])
        out.append(jnp.where(left, stacked[:count], stacked[count:]))
    return jnp.concatenate(out, axis=1)


def attend_backward(query, keys, values, keep, grad_context, kept=None):
    query_blocks = spread_heads(query)
    grad_blocks = spread_heads(grad_context)
    probs = attend_probs(query_blocks, keys, keep) if kept is None else kept.astype(F32)
    grad_probs = dot_nt(values, grad_blocks)
    inner = jnp.sum(grad_probs * probs, axis=0, keepdims=True)
    grad_scores = (probs * (grad_probs - inner)).astype(BF16)
    grad_values = dot_nn(probs.astype(BF16) if kept is None else kept, grad_blocks)
    grad_keys = dot_nn(grad_scores, query_blocks)
    grad_query = collect_heads(dot_tn(grad_scores, keys), query.shape[0]) * 0.125
    return grad_query, grad_keys, grad_values


def row_keep(bound, length):
    key = lax.broadcasted_iota(jnp.int32, (length, 4 * length), 0)
    query = lax.broadcasted_iota(jnp.int32, (length, 4 * length), 1) % length
    return (key >= bound) == (query >= bound)


def window(which, width):
    return pl.ds(pl.multiple_of(which * 3 // 2 * (width // 2), width // 2), width)


def own_rows(acc, which, own):
    odd = which % 2 == 1
    return jnp.where(odd, acc[acc.shape[0] - own :], acc[:own])


def prep_kernel(gathers, count, *refs):
    region_ref, picture_ref, weight_ref = refs[:3]
    shards, refs = refs[3 : 3 + count], refs[3 + count :]
    moved_ref, embed_ref = refs[:2]
    whole, refs = refs[2 : 2 + gathers], refs[2 + gathers :]
    flat_ref = refs[0]
    patch_count, images, lanes = region_ref.shape
    padded = moved_ref.shape[1]
    full_tiles = patch_count // 8 * 8
    step = pl.program_id(0)
    steps = pl.num_programs(0)
    gather = Gather(shards, whole, refs[1:]) if gathers else None

    @pl.when(step == 0)
    def _():
        if gather:
            gather.start()
        raw = dot_nn(picture_ref[...], weight_ref[...])
        scale = lax.rsqrt(jnp.sum(raw * raw, axis=-1, keepdims=True) + NORM_EPS)
        embed_ref[...] = (raw * scale).astype(BF16)

    flat_ref[...] = region_ref[...].reshape(patch_count * images, lanes).astype(F32)
    row = lax.broadcasted_iota(jnp.int32, (padded - full_tiles, lanes), 0)
    for image in range(images):
        main = flat_ref[pl.ds(image, full_tiles, stride=images), :]
        moved_ref[image, 0:full_tiles, :] = main.astype(BF16)
        last = flat_ref[pl.ds(full_tiles * images + image, 1), :]
        moved_ref[image, full_tiles:padded, :] = jnp.where(row == 0, last, 0.0).astype(BF16)

    if gather:

        for late, distance in ((6, 1), (4, 2), (2, 3)):

            @pl.when(step == steps - late)
            def _(distance=distance):
                gather.pull(distance)

        @pl.when(step == steps - 1)
        def _():
            gather.pair(1)
            gather.pair(2)
            gather.pair(3)
            gather.finish()


def self_forward_kernel(length, gathers, count, *refs):
    bound_ref, tok_ref, wqkv_ref, wout_ref, embed_ref = refs[:5]
    shards, refs = refs[5 : 5 + count], refs[5 + count :]
    qkv_ref, ctx_ref, xhat_ref, rstd_ref = refs[:4]
    whole, refs = refs[4 : 4 + gathers], refs[4 + gathers :]
    width = tok_ref.shape[1]
    rows = tok_ref.shape[0] // length
    step = pl.program_id(0)
    steps = pl.num_programs(0)
    if gathers:
        images_ref, embed_local, embed_send, embed_recv = refs[:4]
        gather = Gather(shards, whole, refs[4:])
        dp, z = lax.axis_index("dp"), lax.axis_index("mp")
        dp_size = images_ref.shape[0] // embed_ref.shape[0]
        held = embed_ref.shape[0]

        def embed_copy(k, owner, to):
            spot = images_ref.at[pl.ds(pl.multiple_of(owner * held, 16), held), :]
            return pltpu.make_async_remote_copy(
                src_ref=embed_ref, dst_ref=spot, send_sem=embed_send.at[k], recv_sem=embed_recv.at[k],
                device_id=(to, z), device_id_type=MESH,
            )

        def embed_own():
            spot = images_ref.at[pl.ds(pl.multiple_of(dp * held, 16), held), :]
            return pltpu.make_async_copy(embed_ref, spot, embed_local)

        @pl.when(step == 0)
        def _():
            gather.start(everyone=dp_size)
            embed_own().start()
            for k in range(1, dp_size):
                embed_copy(k, dp, (dp + k) % dp_size).start()

        for distance in range(1, 4):

            @pl.when(step == distance)
            def _(distance=distance):
                gather.pull(distance)

    tok = tok_ref[...]
    for part in range(3):
        proj = dot_nt(tok, wqkv_ref[part * width : (part + 1) * width, :])
        if part == 0:
            proj = proj * 0.125
        qkv_ref[:, part * width : (part + 1) * width] = proj.astype(BF16)

    def pair(index, carry):
        span = pl.ds(pl.multiple_of(index * 2 * length, 16), 2 * length)
        keeps = [row_keep(bound_ref[step * rows + 2 * index + j], length) for j in range(2)]
        for group in range(width // GROUP):
            q, k, v = (
                qkv_ref[span, part * width + group * GROUP : part * width + (group + 1) * GROUP].astype(F32)
                for part in range(3)
            )
            out = []
            for j in range(2):
                at = slice(j * length, (j + 1) * length)
                out.append(attend_short(q[at], k[at].astype(BF16), v[at].astype(BF16), keeps[j]))
            ctx_ref[span, group * GROUP : (group + 1) * GROUP] = jnp.concatenate(out, axis=0).astype(BF16)
        return carry

    lax.fori_loop(0, rows // 2, pair, 0, unroll=2)
    attn = dot_nn(ctx_ref[...], wout_ref[...])
    xhat, rstd = normalize(tok.astype(F32) + attn)
    xhat_ref[...] = xhat
    rstd_ref[...] = rstd

    if gathers:

        @pl.when(step == steps - 1)
        def _():
            for distance in range(1, 4):
                gather.pair(distance)
            for k in range(1, dp_size):
                embed_copy(k, (dp + dp_size - k) % dp_size, (dp + k) % dp_size).wait_recv()
                embed_copy(k, dp, (dp + k) % dp_size).wait_send()
            embed_own().wait()
            gather.finish()


def cross_forward_kernel(patch_count, length, gathers, count, *refs):
    region_ref, wkv_ref, xhat1_ref, norm_ref, wcq_ref, wout_ref = refs[:6]
    shards, refs = refs[6 : 6 + count], refs[6 + count :]
    kv_ref, cq_ref, ctx_ref, xhat_ref, rstd_ref, probs_ref = refs[:6]
    whole, refs = refs[6 : 6 + gathers], refs[6 + gathers :]
    images, padded, vision = region_ref.shape
    width = cq_ref.shape[1]
    step = pl.program_id(0)
    steps = pl.num_programs(0)
    gather = Gather(shards, whole, refs) if gathers else None
    if gathers:

        @pl.when(step == 0)
        def _():
            gather.start()

        for distance in range(1, 4):

            @pl.when(step == distance)
            def _(distance=distance):
                gather.pull(distance)

    hidden1 = xhat1_ref[...] * norm_ref[0:1] + norm_ref[1:2]
    cq_ref[...] = (dot_nt(hidden1.astype(BF16), wcq_ref[...]) * 0.125).astype(BF16)
    flat = region_ref[...].reshape(images * padded, vision)

    def chunk(index, carry):
        at = pl.ds(pl.multiple_of(index * 512, 512), 512)
        proj = dot_nt(flat, wkv_ref[at, :])
        kv_ref[:, :, at] = proj.astype(BF16).reshape(images, padded, 512)
        return carry

    lax.fori_loop(0, 2 * width // 512, chunk, 0, unroll=True)
    keep = lax.broadcasted_iota(jnp.int32, (padded, 4 * length), 0) < patch_count

    def pair(index, carry):
        span = pl.ds(pl.multiple_of(index * 2 * length, 16), 2 * length)
        for group in range(width // GROUP):
            lanes = slice(group * GROUP, (group + 1) * GROUP)
            q = cq_ref[span, lanes].astype(F32)
            out = []
            for j in range(2):
                image = 2 * index + j
                keys = kv_ref[image, :, lanes]
                values = kv_ref[image, :, width + group * GROUP : width + (group + 1) * GROUP]
                context, probs = attend_forward(q[j * length : (j + 1) * length], keys, values, keep)
                out.append(context)
                probs_ref[image, group] = probs
            ctx_ref[span, lanes] = jnp.concatenate(out, axis=0).astype(BF16)
        return carry

    lax.fori_loop(0, images // 2, pair, 0, unroll=4)
    xhat, rstd = normalize(hidden1 + dot_nn(ctx_ref[...], wout_ref[...]))
    xhat_ref[...] = xhat
    rstd_ref[...] = rstd

    if gathers:

        @pl.when(step == steps - 1)
        def _():
            for distance in range(1, 4):
                gather.pair(distance)
            gather.finish()


def gelu_parts(inputs):
    cdf = 0.5 * (1.0 + lax.erf(inputs * 0.7071067811865476))
    density = jnp.exp(inputs * inputs * -0.5) * 0.3989422804014327
    return inputs * cdf, cdf + inputs * density


def feed_forward_kernel(
    length, bound_ref, which_ref, temp_ref, xhat2_ref, rstd2_ref, norm_ref,
    wup_ref, wdown_ref, adj_ref, target_ref, images_ref, wtext_ref,
    out_ref, loss_ref, pack_ref, dr2_ref, dup_ref, ddown_ref, dgain2_ref, dshift2_ref, dgain3_ref, dshift3_ref,
    dtext_ref, dtemp_ref,
    act_ref, slope_ref, final_ref, grad_ref, lead_ref, up_acc, down_acc, text_acc,
):
    step = pl.program_id(0)
    steps = pl.num_programs(0)
    tokens, width = xhat2_ref.shape
    hidden_units = wup_ref.shape[0]
    rows = tokens // length
    chunk = min(768, hidden_units)

    @pl.when(step == 0)
    def _():
        for ref in (dgain2_ref, dshift2_ref, dgain3_ref, dshift3_ref, dtemp_ref, up_acc, down_acc, text_acc):
            ref[...] = jnp.zeros_like(ref)

    xhat2 = xhat2_ref[...]
    hidden2 = xhat2 * norm_ref[2:3] + norm_ref[3:4]
    low = hidden2.astype(BF16)
    final_ref[...] = hidden2

    def forward(index, carry):
        at = pl.ds(pl.multiple_of(index * chunk, chunk), chunk)
        act, slope = gelu_parts(dot_nt(low, wup_ref[at, :]))
        act = act.astype(BF16)
        act_ref[:, at] = act
        slope_ref[:, at] = slope
        final_ref[...] += dot_nn(act, wdown_ref[at, :])
        return carry

    lax.fori_loop(0, hidden_units // chunk, forward, 0, unroll=True)
    xhat3, rstd3 = normalize(final_ref[...])
    final = xhat3 * norm_ref[4:5] + norm_ref[5:6]
    out_ref[...] = final.astype(BF16)
    final_ref[...] = final
    grad_ref[...] = adj_ref[...].astype(F32)

    for row in range(rows):
        lead_ref[pl.ds(2 * row, 1), :] = final_ref[pl.ds(row * length, 1), :]
        second = row * length + bound_ref[step * rows + row]
        lead_ref[pl.ds(2 * row + 1, 1), :] = final_ref[pl.ds(second, 1), :]
    lead = lead_ref[...].astype(BF16)
    raw = dot_nn(lead, wtext_ref[...])
    text = raw * lax.rsqrt(jnp.sum(raw * raw, axis=-1, keepdims=True) + NORM_EPS)
    text_low = text.astype(BF16)
    temp = temp_ref[0]
    logits = dot_nt(text_low, images_ref[...]) / temp
    top = jnp.max(logits, axis=1, keepdims=True)
    lse = top + jnp.log(jnp.sum(jnp.exp(logits - top), axis=1, keepdims=True))
    target = target_ref[...]
    hit = lax.broadcasted_iota(jnp.int32, logits.shape, 1) == target
    loss_ref[...] = lse - jnp.sum(jnp.where(hit, logits, 0.0), axis=1, keepdims=True)
    dlogits = jnp.exp(logits - lse) - hit.astype(F32)
    dtemp_ref[...] += -jnp.sum(jnp.sum(dlogits * logits, axis=1, keepdims=True), axis=0, keepdims=True) / temp
    embed = raw.shape[1]
    lane = lax.broadcasted_iota(jnp.int32, (2 * rows, 128), 1)
    pack_ref[:, :embed] = text_low.astype(F32)
    pack_ref[:, embed:] = jnp.where(lane == 0, lse, jnp.where(lane == 1, target.astype(F32), 0.0))
    dtext = dot_nn((dlogits / temp).astype(BF16), images_ref[...])
    draw = unit_pull(raw, dtext).astype(BF16)
    text_acc[...] += dot_tn(lead, draw)
    lead_ref[...] = dot_nt(draw, wtext_ref[...])
    for row in range(rows):
        first = pl.ds(row * length, 1)
        grad_ref[first, :] += lead_ref[pl.ds(2 * row, 1), :]
        second = pl.ds(row * length + bound_ref[step * rows + row], 1)
        grad_ref[second, :] += lead_ref[pl.ds(2 * row + 1, 1), :]

    dr3, dgain3, dshift3 = norm_pull(grad_ref[...], xhat3, rstd3, norm_ref[4:5])
    dgain3_ref[...] += dgain3
    dshift3_ref[...] += dshift3
    grad_ref[...] = dr3
    dfinal = dr3.astype(BF16)
    own = hidden_units // 4
    own_at = pl.ds(pl.multiple_of(which_ref[0] * own, own), own)
    down_acc[...] += dot_tn(act_ref[:, own_at], dfinal)

    def backward(index, carry):
        at = pl.ds(pl.multiple_of(index * chunk, chunk), chunk)
        dact = dot_nt(dfinal, wdown_ref[at, :])
        dinner = (dact * slope_ref[:, at]).astype(BF16)
        act_ref[:, at] = dinner
        grad_ref[...] += dot_nn(dinner, wup_ref[at, :])
        return carry

    lax.fori_loop(0, hidden_units // chunk, backward, 0, unroll=True)
    up_acc[...] += dot_tn(low, act_ref[:, own_at])
    dr2, dgain2, dshift2 = norm_pull(grad_ref[...], xhat2, rstd2_ref[...], norm_ref[2:3])
    dgain2_ref[...] += dgain2
    dshift2_ref[...] += dshift2
    dr2_ref[...] = dr2

    @pl.when(step == steps - 1)
    def _():
        dup_ref[...] = up_acc[...].astype(BF16)
        ddown_ref[...] = down_acc[...].astype(BF16)
        dtext_ref[...] = text_acc[...].astype(BF16)


def cross_backward_kernel(
    patch_count, length, which_ref, region_ref, kv_ref, cq_ref, ctx_ref, xhat1_ref, rstd1_ref, norm_ref,
    dr2_ref, wkv_ref, wout_ref, wcq_ref, probs_ref,
    dregion_ref, dr1_ref, dkv_ref, dqo_ref, dgain_ref, dshift_ref,
    dctx_ref, dq_ref, grads_ref, flat_ref, stage_ref, kv_acc, cq_acc, out_acc, sem,
):
    step = pl.program_id(0)
    steps = pl.num_programs(0)
    images, padded, vision = region_ref.shape
    width = cq_ref.shape[1]
    own = width // 4
    which = which_ref[0]
    mine = window(which, GROUP)
    wide = stage_ref.shape[2]
    parts = wide // images
    stored = flat_ref.shape[1] // wide

    @pl.when(step == 0)
    def _():
        for ref in (dgain_ref, dshift_ref, kv_acc, cq_acc, out_acc):
            ref[...] = jnp.zeros_like(ref)

    dr2 = dr2_ref[...]
    dx = dr2.astype(BF16)
    dctx_ref[...] = dot_nt(dx, wout_ref[...]).astype(BF16)
    out_acc[...] += dot_tn(ctx_ref[:, mine], dx)

    def pair(index, carry):
        span = pl.ds(pl.multiple_of(index * 2 * length, 16), 2 * length)
        for group in range(width // GROUP):
            lanes = slice(group * GROUP, (group + 1) * GROUP)
            value_lanes = slice(width + group * GROUP, width + (group + 1) * GROUP)
            q = cq_ref[span, lanes].astype(F32)
            d = dctx_ref[span, lanes].astype(F32)
            out = []
            for j in range(2):
                image = 2 * index + j
                at = slice(j * length, (j + 1) * length)
                dq, dk, dv = attend_backward(
                    q[at], kv_ref[image, :, lanes], kv_ref[image, :, value_lanes], None, d[at], probs_ref[image, group]
                )
                out.append(dq)
                grads_ref[image, :, lanes] = dk.astype(BF16)
                grads_ref[image, :, value_lanes] = dv.astype(BF16)
            dq_ref[span, lanes] = jnp.concatenate(out, axis=0).astype(BF16)
        return carry

    lax.fori_loop(0, images // 2, pair, 0, unroll=4)

    some = 4
    for index in range(images // some):
        grads = grads_ref[index * some : (index + 1) * some].reshape(some * padded, 2 * width)
        dregion = dot_nn(grads, wkv_ref[...])
        for image in range(some):
            spot = pl.ds(step % parts * images + index * some + image, stored, stride=wide)
            for lane in range(vision // 128):
                flat_ref[lane, spot, :] = dregion[
                    image * padded : image * padded + stored, lane * 128 : (lane + 1) * 128
                ]
    region = region_ref[...].reshape(images * padded, vision)
    for part in range(2):
        at = window(which, GROUP)
        grads = grads_ref[:, :, pl.ds(pl.multiple_of(which * 3 // 2 * 128 + part * width, 128), GROUP)]
        kv_acc[part] += dot_tn(grads.reshape(images * padded, GROUP), region)

    pieces = 5
    patches = patch_count // pieces
    tall = patches * wide

    def send(index):
        slot = index % 2
        base = pl.multiple_of(step // parts * wide, 16)
        return pltpu.make_async_copy(
            stage_ref.at[slot],
            dregion_ref.at[pl.ds(index * patches, patches), pl.ds(base, wide), :],
            sem.at[slot],
        )

    @pl.when(step % parts == parts - 1)
    def _():
        for index in range(pieces):
            rows = slice(index * tall, (index + 1) * tall)
            low = jnp.concatenate([flat_ref[c, rows, :].astype(BF16) for c in range(vision // 128)], axis=1)
            if index >= 2:
                send(index - 2).wait()
            stage_ref[index % 2] = low.reshape(patches, wide, vision)
            send(index).start()
        send(pieces - 2).wait()
        send(pieces - 1).wait()

    xhat1 = xhat1_ref[...]
    hidden1 = (xhat1 * norm_ref[0:1] + norm_ref[1:2]).astype(BF16)
    cq_acc[...] += dot_tn(dq_ref[:, mine], hidden1)
    dh1 = dr2 + dot_nn(dq_ref[...], wcq_ref[...])
    dr1, dgain, dshift = norm_pull(dh1, xhat1, rstd1_ref[...], norm_ref[0:1])
    dr1_ref[...] = dr1
    dgain_ref[...] += dgain
    dshift_ref[...] += dshift

    @pl.when(step == steps - 1)
    def _():
        for part in range(2):
            dkv_ref[part * own : (part + 1) * own, :] = own_rows(kv_acc[part], which, own).astype(BF16)
        dqo_ref[:own, :] = own_rows(cq_acc[...], which, own).astype(BF16)
        dqo_ref[own:, :] = own_rows(out_acc[...], which, own).astype(BF16)


def self_backward_kernel(length, sums, *refs):
    bound_ref, tok_ref, qkv_ref, ctx_ref, dr1_ref, wqkv_ref, wout_ref = refs[:7]
    refs = refs[7:]
    if sums:
        dkv_ref, dqo_ref, temp_ref, pack_ref, picture_ref, wimage_ref = refs[:6]
        vectors, refs = refs[6:13], refs[13:]
    dtok_ref, last_ref = refs[:2]
    refs = refs[2:]
    if sums:
        outs, dpicture_ref, refs = refs[:4], refs[4], refs[5:]
    dctx_ref, grads_ref, qkv_acc, out_acc, last = refs[:5]
    refs = refs[5:]
    step = pl.program_id(0)
    steps = pl.num_programs(0)
    half = steps // 2
    tokens, width = tok_ref.shape
    rows = tokens // length
    own = width // 4
    which = lax.axis_index("mp")
    if sums:
        packs, dimage, small, pack_sent, pack_came = refs[:5]
        refs = refs[5:]
        spots = (dkv_ref, dqo_ref, small, dimage, last.at[: 2 * own], last.at[2 * own :])
        kv_sum, qo_sum, small_sum, image_sum, *finals = (
            Reduce(spot, *refs[6 * i : 6 * i + 6]) for i, spot in enumerate(spots)
        )
        dp, z = lax.axis_index("dp"), lax.axis_index("mp")
        dp_size = packs.shape[0]

        def pack_copy(k, owner):
            return pltpu.make_async_remote_copy(
                src_ref=pack_ref, dst_ref=packs.at[owner], send_sem=pack_sent.at[k], recv_sem=pack_came.at[k],
                device_id=((dp + k) % dp_size, z), device_id_type=MESH,
            )

        @pl.when(step == 0)
        def _():
            small[...] = jnp.zeros(small.shape, BF16)
            lines = [ref[...] for ref in vectors[:6]] + [jnp.broadcast_to(vectors[6][...], (1, width))]
            lines = [*lines, jnp.zeros((16 - len(lines), width), F32)]
            small[0:16, :] = jnp.concatenate(lines, axis=0).astype(BF16)
            barrier = pltpu.get_barrier_semaphore()
            for k in range(1, dp_size):
                pl.semaphore_signal(barrier, inc=1, device_id=((dp + k) % dp_size, z), device_id_type=MESH)
            pl.semaphore_wait(barrier, dp_size - 1)
            for k in range(1, dp_size):
                pack_copy(k, dp).start()
            packs[dp] = pack_ref[...]
            for reduce in (kv_sum, qo_sum, small_sum):
                reduce.stage(1)

        @pl.when(step == 1)
        def _():
            for reduce in (kv_sum, qo_sum, small_sum):
                reduce.stage(2)
            for k in range(1, dp_size):
                pack_copy(k, (dp + dp_size - k) % dp_size).wait_recv()
                pack_copy(k, dp).wait_send()
            everyone = packs[...].reshape(-1, packs.shape[2])
            first = dp * picture_ref.shape[0]
            dpicture, dweight = image_backward(first, temp_ref[0], picture_ref[...], wimage_ref[...], everyone)
            dpicture_ref[...] = dpicture
            dimage[...] = dweight.astype(BF16)
            image_sum.stage(1)

        for number in (3, 4):

            @pl.when(step == number - 1)
            def _(number=number):
                for reduce in (kv_sum, qo_sum, small_sum):
                    reduce.stage(number)
                image_sum.stage(number - 1)

    @pl.when(step == 0)
    def _():
        for ref in (qkv_acc, out_acc):
            ref[...] = jnp.zeros_like(ref)

    @pl.when(step < half)
    def _():
        all_rows = pl.ds(pl.multiple_of(step * tokens, 16), tokens)
        da = dr1_ref[...].astype(BF16)
        dctx_ref[...] = dot_nt(da, wout_ref[...]).astype(BF16)
        out_acc[...] += dot_tn(ctx_ref[:, window(which, GROUP)], da)

        def pair(index, carry):
            span = pl.ds(pl.multiple_of(index * 2 * length, 16), 2 * length)
            far = pl.ds(pl.multiple_of(step * tokens + index * 2 * length, 16), 2 * length)
            keeps = [row_keep(bound_ref[step * rows + 2 * index + j], length) for j in range(2)]
            for group in range(width // GROUP):
                q, k, v = (
                    qkv_ref[span, part * width + group * GROUP : part * width + (group + 1) * GROUP].astype(F32)
                    for part in range(3)
                )
                d = dctx_ref[span, group * GROUP : (group + 1) * GROUP].astype(F32)
                outs = []
                for j in range(2):
                    at = slice(j * length, (j + 1) * length)
                    outs.append(attend_backward(q[at], k[at].astype(BF16), v[at].astype(BF16), keeps[j], d[at]))
                for part in range(3):
                    both = jnp.concatenate([outs[0][part], outs[1][part]], axis=0).astype(BF16)
                    grads_ref[far, part * width + group * GROUP : part * width + (group + 1) * GROUP] = both
            return carry

        lax.fori_loop(0, rows // 2, pair, 0, unroll=4)
        tok = tok_ref[...]
        for part in range(3):
            mine = grads_ref[all_rows, pl.ds(pl.multiple_of(which * 3 // 2 * 128 + part * width, 128), GROUP)]
            qkv_acc[part] += dot_tn(mine, tok)

    @pl.when(step == half - 1)
    def _():
        for part in range(3):
            last[part * own : (part + 1) * own, :] = own_rows(qkv_acc[part], which, own).astype(BF16)
        last[3 * own : 4 * own, :] = own_rows(out_acc[...], which, own).astype(BF16)
        if sums:
            for reduce in finals:
                reduce.stage(1)

    @pl.when(step >= half)
    def _():
        done = pl.ds(pl.multiple_of((step - half) * tokens, 16), tokens)
        dtok_ref[...] = dr1_ref[...] + dot_nn(grads_ref[done, :], wqkv_ref[...])

    if sums:

        @pl.when(step == half)
        def _():
            image_sum.stage(4)
            for reduce in finals:
                reduce.stage(2)

    @pl.when(step == steps - 1)
    def _():
        if sums:
            for reduce in finals:
                reduce.stage(3)
            for reduce in (kv_sum, qo_sum, small_sum, image_sum):
                reduce.stage(5)
            for reduce, out in zip((kv_sum, qo_sum, small_sum, image_sum), outs, strict=True):
                out[...] = reduce.done[...]
            for number in (4, 5):
                for reduce in finals:
                    reduce.stage(number)
            last_ref[: 2 * own, :] = finals[0].done[...]
            last_ref[2 * own :, :] = finals[1].done[...]
        else:
            last_ref[...] = last[...]


def image_backward(first, temp, picture, weight, pack):
    raw = dot_nn(picture, weight)
    own = (raw * lax.rsqrt(jnp.sum(raw * raw, axis=-1, keepdims=True) + NORM_EPS)).astype(BF16)
    embed = raw.shape[1]
    text = pack[:, :embed].astype(BF16)
    lse = pack[:, embed : embed + 1]
    target = pack[:, embed + 1 : embed + 2].astype(jnp.int32)
    logits = dot_nt(text, own) / temp
    hit = lax.broadcasted_iota(jnp.int32, logits.shape, 1) + first == target
    dlogits = jnp.exp(logits - lse) - hit.astype(F32)
    dimage = dot_tn((dlogits / temp).astype(BF16), text)
    draw = unit_pull(raw, dimage).astype(BF16)
    return dot_nt(draw, weight), dot_tn(picture, draw)


def image_backward_kernel(
    first_ref, temp_ref, picture_ref, weight_ref, pack_ref, dpicture_ref, dweight_ref
):
    dpicture, dweight = image_backward(
        first_ref[0], temp_ref[0], picture_ref[...], weight_ref[...], pack_ref[...]
    )
    dpicture_ref[...] = dpicture
    dweight_ref[...] = dweight.astype(BF16)


def widen_kernel(own, last_ref, dkv_ref, dqo_ref, dimage_ref, dup_ref, ddown_ref, dtext_ref, small_ref, *outs):
    for index in range(4):
        outs[index][...] = last_ref[index * own : (index + 1) * own, :].astype(F32)
    for index in range(2):
        outs[4 + index][...] = dqo_ref[index * own : (index + 1) * own, :].astype(F32)
        outs[6 + index][...] = dkv_ref[index * own : (index + 1) * own, :].astype(F32)
    for out, ref in zip(outs[8:12], (dup_ref, ddown_ref, dtext_ref, dimage_ref), strict=True):
        out[...] = ref[...].astype(F32)
    small = small_ref[0:16, :].astype(F32)
    for index in range(6):
        outs[12 + index][...] = small[index]
    outs[18][...] = small[6:7, 0:1]


def full(shape):
    return pl.BlockSpec(shape, lambda i: (0,) * len(shape), pipeline_mode=pl.Buffered(1))


def fixed(shape):
    return pl.BlockSpec(shape, lambda i: (0,) * len(shape))


def rows_of(count, width):
    return pl.BlockSpec((count, width), lambda i: (i, 0))


SMEM = pl.BlockSpec(memory_space=pltpu.SMEM)


def shape_of(shape, kind):
    return jax.ShapeDtypeStruct(shape, kind)


def call(kernel, steps, ins, outs, args, scratch=(), flops=0, moved=0, ident=None):
    specs, shapes = zip(*outs, strict=True)
    remote = {} if ident is None else {"collective_id": ident, "has_side_effects": True}
    return pl.pallas_call(
        kernel,
        grid=(steps,),
        in_specs=list(ins),
        out_specs=list(specs),
        out_shape=list(shapes),
        scratch_shapes=list(scratch),
        compiler_params=pltpu.CompilerParams(
            vmem_limit_bytes=VMEM_LIMIT, dimension_semantics=("arbitrary",), **remote
        ),
        cost_estimate=pl.CostEstimate(flops=flops, bytes_accessed=moved, transcendentals=0),
    )(*args)


DEPTH = 4


def gathered(groups):
    shapes = [(len(group), *group[0].shape) for group in groups]
    outs = [
        (pl.BlockSpec(memory_space=pl.ANY), shape_of((shape[0], DEPTH, *shape[1:]), BF16)) for shape in shapes
    ]
    scratch = [pltpu.VMEM(shape, BF16) for shape in shapes]
    specs = [full(shard.shape) for group in groups for shard in group]
    return specs, outs, [*scratch, *Gather.semaphores(len(groups), DEPTH)] if groups else []


def flatten(groups):
    return [shard for group in groups for shard in group]


TOKEN_ROWS = 8
IMAGE_ROWS = 16


def square(width, index):
    return pl.BlockSpec((width, width), lambda i: (index, 0), pipeline_mode=pl.Buffered(1))


def run_prep(region, picture, wimage, shards):
    patch_count, rows, vision = region.shape
    padded = -(-patch_count // 16) * 16
    embed = wimage.shape[1]
    specs, outs, sems = gathered(shards)
    return call(
        partial(prep_kernel, len(shards), len(flatten(shards))),
        vision // 128,
        [pl.BlockSpec((patch_count, rows, 128), lambda i: (0, 0, i)), full(picture.shape), full(wimage.shape), *specs],
        [
            (pl.BlockSpec((rows, padded, 128), lambda i: (0, 0, i)), shape_of((rows, padded, vision), BF16)),
            (fixed((rows, embed)), shape_of((rows, embed), BF16)),
            *outs,
        ],
        (region, picture, wimage, *flatten(shards)),
        scratch=[pltpu.VMEM((patch_count * rows, 128), F32), *sems],
        moved=4 * rows * padded * vision,
        ident=1 if shards else None,
    )


def run_self_forward(length, dp_size, bound, tok, squares, embed, shards):
    tokens, width = tok.shape
    block = TOKEN_ROWS * length
    specs, outs, sems = gathered(shards)
    if shards:
        shape = shape_of((dp_size * embed.shape[0], embed.shape[1]), BF16)
        outs = [*outs, (pl.BlockSpec(memory_space=pl.ANY), shape)]
        sems = [DMA, DMA((dp_size,)), DMA((dp_size,)), *sems]
    return call(
        partial(self_forward_kernel, length, len(shards), len(flatten(shards))),
        tokens // block,
        [SMEM, rows_of(block, width), full((3 * width, width)), square(width, 3), full(embed.shape), *specs],
        [
            (rows_of(block, 3 * width), shape_of((tokens, 3 * width), BF16)),
            (rows_of(block, width), shape_of((tokens, width), BF16)),
            (rows_of(block, width), shape_of((tokens, width), F32)),
            (rows_of(block, 1), shape_of((tokens, 1), F32)),
            *outs,
        ],
        (bound, tok, squares, squares, embed, *flatten(shards)),
        scratch=sems,
        flops=10 * tokens * width * width,
        moved=20 * tokens * width,
        ident=2 if shards else None,
    )


def probs_spec(width, length, padded):
    return pl.BlockSpec((TOKEN_ROWS, width // GROUP, padded, 4 * length), lambda i: (i, 0, 0, 0))


def run_cross_forward(length, patch_count, region, wkv, xhat1, norms, wcq, wout, shards):
    rows, padded, vision = region.shape
    tokens, width = xhat1.shape
    images = TOKEN_ROWS
    block = images * length
    specs, outs, sems = gathered(shards)
    return call(
        partial(cross_forward_kernel, patch_count, length, len(shards), len(flatten(shards))),
        rows // images,
        [
            pl.BlockSpec((images, padded, vision), lambda i: (i, 0, 0)), full((2 * width, vision)),
            rows_of(block, width), full(norms.shape), square(width, 0), square(width, 1), *specs,
        ],
        [
            (
                pl.BlockSpec((images, padded, 2 * width), lambda i: (i, 0, 0)),
                shape_of((rows, padded, 2 * width), BF16),
            ),
            (rows_of(block, width), shape_of((tokens, width), BF16)),
            (rows_of(block, width), shape_of((tokens, width), BF16)),
            (rows_of(block, width), shape_of((tokens, width), F32)),
            (rows_of(block, 1), shape_of((tokens, 1), F32)),
            (probs_spec(width, length, padded), shape_of((rows, width // GROUP, padded, 4 * length), BF16)),
            *outs,
        ],
        (region, wkv, xhat1, norms, wcq, wout, *flatten(shards)),
        scratch=sems,
        flops=4 * rows * padded * width * vision,
        moved=2 * rows * padded * (vision + 2 * width),
        ident=3 if shards else None,
    )


def run_feed_forward(
    length, bound, which, temp, xhat2, rstd2, norms, ffn, adjoint, target, image_all, wtext
):
    tokens, width = xhat2.shape
    hidden_units = ffn.shape[0] // 2
    embed = wtext.shape[1]
    block = IMAGE_ROWS * length
    captions = 2 * IMAGE_ROWS
    ff_own = hidden_units // 4
    return call(
        partial(feed_forward_kernel, length),
        tokens // block,
        [
            SMEM, SMEM, SMEM, rows_of(block, width), rows_of(block, 1), full(norms.shape),
            full((hidden_units, width)),
            pl.BlockSpec((hidden_units, width), lambda i: (1, 0), pipeline_mode=pl.Buffered(1)),
            rows_of(block, width), rows_of(captions, 1),
            full(image_all.shape), full((width, embed)),
        ],
        [
            (rows_of(block, width), shape_of((tokens, width), BF16)),
            (rows_of(captions, 1), shape_of(target.shape, F32)),
            (rows_of(captions, embed + 128), shape_of((target.shape[0], embed + 128), F32)),
            (rows_of(block, width), shape_of((tokens, width), F32)),
            (fixed((width, ff_own)), shape_of((width, ff_own), BF16)),
            (fixed((ff_own, width)), shape_of((ff_own, width), BF16)),
            (fixed((1, width)), shape_of((1, width), F32)),
            (fixed((1, width)), shape_of((1, width), F32)),
            (fixed((1, width)), shape_of((1, width), F32)),
            (fixed((1, width)), shape_of((1, width), F32)),
            (fixed((width, embed)), shape_of((width, embed), BF16)),
            (fixed((1, 1)), shape_of((1, 1), F32)),
        ],
        (
            bound, which, temp, xhat2, rstd2, norms, ffn, ffn, adjoint, target, image_all,
            wtext,
        ),
        scratch=[
            pltpu.VMEM((block, hidden_units), BF16),
            pltpu.VMEM((block, hidden_units), F32),
            pltpu.VMEM((block, width), F32),
            pltpu.VMEM((block, width), F32),
            pltpu.VMEM((captions, width), F32),
            pltpu.VMEM((width, ff_own), F32),
            pltpu.VMEM((ff_own, width), F32),
            pltpu.VMEM((width, embed), F32),
        ],
        flops=10 * tokens * width * hidden_units,
        moved=20 * tokens * width,
    )


def run_cross_backward(length, patch_count, which, region, kv, cq, ctx2, xhat1, rstd1, norms, dr2, wkv, wcq, wout, probs):
    rows, padded, vision = region.shape
    tokens, width = cq.shape
    images = TOKEN_ROWS
    block = images * length
    own = width // 4
    stored = -(-patch_count // 8) * 8
    return call(
        partial(cross_backward_kernel, patch_count, length),
        rows // images,
        [
            SMEM,
            pl.BlockSpec((images, padded, vision), lambda i: (i, 0, 0)),
            pl.BlockSpec((images, padded, 2 * width), lambda i: (i, 0, 0)),
            rows_of(block, width), rows_of(block, width), rows_of(block, width), rows_of(block, 1), full(norms.shape),
            rows_of(block, width), full((2 * width, vision)), square(width, 1), square(width, 0),
            probs_spec(width, length, padded),
        ],
        [
            (pl.BlockSpec(memory_space=pl.ANY), shape_of((patch_count, rows, vision), BF16)),
            (rows_of(block, width), shape_of((tokens, width), F32)),
            (fixed((2 * own, vision)), shape_of((2 * own, vision), BF16)),
            (fixed((2 * own, width)), shape_of((2 * own, width), BF16)),
            (fixed((1, width)), shape_of((1, width), F32)),
            (fixed((1, width)), shape_of((1, width), F32)),
        ],
        (which, region, kv, cq, ctx2, xhat1, rstd1, norms, dr2, wkv, wout, wcq, probs),
        scratch=[
            pltpu.VMEM((block, width), BF16),
            pltpu.VMEM((block, width), BF16),
            pltpu.VMEM((images, padded, 2 * width), BF16),
            pltpu.VMEM((vision // 128, stored * IMAGE_ROWS, 128), F32),
            pltpu.VMEM((2, patch_count // 5, IMAGE_ROWS, vision), BF16),
            pltpu.VMEM((2, GROUP, vision), F32),
            pltpu.VMEM((GROUP, width), F32),
            pltpu.VMEM((GROUP, width), F32),
            DMA((2,)),
        ],
        flops=6 * rows * padded * width * vision,
        moved=2 * rows * padded * 2 * (vision + width),
    )


def run_self_backward(length, dp_size, bound, tok, qkv, ctx1, dr1, selves, others):
    tokens, width = tok.shape
    block = TOKEN_ROWS * length
    steps = tokens // block
    last = shape_of((width, width), BF16)

    def early(lanes):
        return pl.BlockSpec((block, lanes), lambda i: (jnp.minimum(i, steps - 1), 0))

    extra, outs, scratch = [], [], []
    if others:
        dkv, dqo, _, pack, picture, wimage, *vectors = others
        image = shape_of(wimage.shape, BF16)
        small = shape_of((128, width), BF16)
        half = (width // 2, width)
        shapes = [shape_of(dkv.shape, BF16), shape_of(dqo.shape, BF16), small, image]
        extra = [full(dkv.shape), full(dqo.shape), SMEM, *(full(other.shape) for other in others[3:])]
        outs = [*((fixed(shape.shape), shape) for shape in shapes), (fixed(picture.shape), shape_of(picture.shape, F32))]
        scratch = [
            pltpu.VMEM((dp_size, *pack.shape), F32), pltpu.VMEM(image.shape, BF16), pltpu.VMEM(small.shape, BF16),
            DMA((dp_size,)), DMA((dp_size,)),
            *(spot for shape in (*(shape.shape for shape in shapes), half, half) for spot in Reduce.scratch(shape)),
        ]
    return call(
        partial(self_backward_kernel, length, bool(others)),
        2 * steps,
        [
            SMEM, early(width), early(3 * width), early(width),
            pl.BlockSpec((block, width), lambda i: (lax.rem(i, steps), 0)),
            full((3 * width, width)), square(width, 3), *extra,
        ],
        [
            (
                pl.BlockSpec((block, width), lambda i: (jnp.maximum(i - steps, 0), 0)),
                shape_of((tokens, width), F32),
            ),
            (fixed(last.shape), last),
            *outs,
        ],
        (bound, tok, qkv, ctx1, dr1, selves, selves, *others),
        scratch=[
            pltpu.VMEM((block, width), BF16),
            pltpu.VMEM((tokens, 3 * width), BF16),
            pltpu.VMEM((3, GROUP, width), F32),
            pltpu.VMEM((GROUP, width), F32),
            pltpu.VMEM(last.shape, BF16),
            *scratch,
        ],
        flops=10 * tokens * width * width,
        moved=20 * tokens * width,
        ident=4 if others else None,
    )


def run_widen(last, dkv, dqo, dimage, dup, ddown, dtext, small):
    width = last.shape[1]
    own = width // 4
    shapes = [(own, width)] * 6 + [(own, dkv.shape[1])] * 2
    shapes += [dup.shape, ddown.shape, dtext.shape, dimage.shape] + [(width,)] * 6 + [(1, 1)]
    args = (last, dkv, dqo, dimage, dup, ddown, dtext, small)
    return call(
        partial(widen_kernel, own),
        1,
        [fixed(array.shape) for array in args],
        [(fixed(shape), shape_of(shape, F32)) for shape in shapes],
        args,
        moved=20 * width * width,
    )


def body(
    dp_size,
    word_features,
    sentence_numbering,
    region_features,
    picture_global_feature,
    matched_picture,
    sharpness_array,
    incoming_adjoint,
    intra_asking_map,
    intra_lookup_map,
    intra_content_map,
    intra_attend_exit_map,
    visual_asking_map,
    visual_lookup_map,
    visual_content_map,
    visual_attend_exit_map,
    mlp_widening_factor,
    mlp_narrowing_factor,
    initial_standardize_scale,
    initial_standardize_offset,
    middle_standardize_scale,
    middle_standardize_offset,
    final_standardize_scale,
    final_standardize_offset,
    sentence_mapping_factor,
    picture_mapping_factor,
):
    rows, length = sentence_numbering.shape
    tokens, width = word_features.shape
    patch_count, vision = region_features.shape[1:]
    embed = sentence_mapping_factor.shape[1]
    hidden_units = mlp_widening_factor.shape[1] * 4
    own = width // 4
    which = lax.axis_index("mp").astype(jnp.int32).reshape(1)
    bound = (length - jnp.sum(sentence_numbering, axis=1)).astype(jnp.int32)
    target = matched_picture.reshape(-1, 1)
    norms = jnp.stack([
        initial_standardize_scale, initial_standardize_offset, middle_standardize_scale,
        middle_standardize_offset, final_standardize_scale, final_standardize_offset,
    ])

    selves = (intra_asking_map.T, intra_lookup_map.T, intra_content_map.T, intra_attend_exit_map)
    crosses = (visual_asking_map.T, visual_attend_exit_map)
    wides = (visual_lookup_map.T, visual_content_map.T)
    ffns = (mlp_widening_factor.T, mlp_narrowing_factor)
    region = jnp.transpose(region_features, (1, 0, 2))
    local = dp_size == 8 and lax.axis_size("mp") == DEPTH

    def each(*shards):
        return list(shards) if local else []

    region, image_own, *found = run_prep(region, picture_global_feature, picture_mapping_factor, each(selves))
    selves = (found[0] if local else lax.all_gather(jnp.stack(selves), "mp", axis=1)).reshape(-1, width)
    qkv, ctx1, xhat1, rstd1, *found = run_self_forward(
        length, dp_size, bound, word_features, selves, image_own, each(crosses, wides)
    )
    if local:
        crosses, wides, image_all = found
    else:
        crosses, wides = (lax.all_gather(jnp.stack(group), "mp", axis=1) for group in (crosses, wides))
        image_all = lax.all_gather(image_own, "dp", axis=0, tiled=True)
    crosses = crosses.reshape(-1, width)
    wkv = wides.reshape(-1, vision)
    kv, cq, ctx2, xhat2, rstd2, probs, *found = run_cross_forward(
        length, patch_count, region, wkv, xhat1, norms, crosses, crosses, each(ffns)
    )
    ffns = (found[0] if local else lax.all_gather(jnp.stack(ffns), "mp", axis=1)).reshape(-1, width)
    (
        block_exit, loss, pack, dr2, dup, ddown, dgain2, dshift2, dgain3, dshift3, dtext, dtemp,
    ) = run_feed_forward(
        length, bound, which, sharpness_array, xhat2, rstd2, norms, ffns, incoming_adjoint, target, image_all,
        sentence_mapping_factor,
    )

    dp_sum = lambda grad: lax.psum(grad, "dp")
    dup, ddown, dtext = dp_sum((dup, ddown, dtext))
    dregion, dr1, dkv, dqo, dgain1, dshift1 = run_cross_backward(
        length, patch_count, which, region, kv, cq, ctx2, xhat1, rstd1, norms, dr2, wkv, crosses, crosses, probs
    )
    vectors = (dgain1, dshift1, dgain2, dshift2, dgain3, dshift3, dtemp)
    pictures = (picture_global_feature, picture_mapping_factor)
    dtok, last, *found = run_self_backward(
        length, dp_size, bound, word_features, qkv, ctx1, dr1, selves,
        each(dkv, dqo, sharpness_array, pack, *pictures, *vectors),
    )
    if local:
        dkv, dqo, small, dimage, dpicture = found
    else:
        pack_all = lax.all_gather(pack, "dp", axis=0, tiled=True)
        first = (lax.axis_index("dp") * rows).astype(jnp.int32).reshape(1)
        dpicture, dimage = call(
            image_backward_kernel,
            1,
            [SMEM, SMEM, *(full(array.shape) for array in (*pictures, pack_all))],
            [
                (fixed((rows, vision)), shape_of((rows, vision), F32)),
                (fixed((vision, embed)), shape_of((vision, embed), BF16)),
            ],
            (first, sharpness_array, *pictures, pack_all),
        )
        lines = [*vectors[:6], jnp.broadcast_to(dtemp, (1, width)), jnp.zeros((9, width), F32)]
        small = jnp.concatenate(lines).astype(BF16)
        dkv, dqo, dimage, last, small = dp_sum((dkv, dqo, dimage, last, small))
    dq, dk, dv, dso, dcq, dco, dck, dcv, dup, ddown, dtext, dimage, *vectors = run_widen(
        last, dkv, dqo, dimage, dup, ddown, dtext, small
    )
    return (
        loss.reshape(rows, 2),
        block_exit,
        dtok,
        jnp.transpose(dregion, (1, 0, 2)),
        dpicture,
        vectors[6].reshape(1),
        dq.T,
        dk.T,
        dv.T,
        dso,
        dcq.T,
        dck.T,
        dcv.T,
        dco,
        dup,
        ddown,
        *vectors[:6],
        dtext,
        dimage,
    )


def solution(mesh):
    rows = P("dp", None)
    by_column = P(None, "mp")
    by_row = P("mp", None)
    in_specs = (
        rows, rows, P("dp", None, None), rows, rows, P(), rows,
        by_column, by_column, by_column, by_row, by_column, by_column, by_column, by_row, by_column, by_row,
        P(), P(), P(), P(), P(), P(), P(), P(),
    )
    out_specs = (
        rows, rows, rows, P("dp", None, None), rows, P(),
        by_column, by_column, by_column, by_row, by_column, by_column, by_column, by_row, by_column, by_row,
        P(), P(), P(), P(), P(), P(), P(), P(),
    )
    return jax.shard_map(
        partial(body, mesh.shape["dp"]), mesh=mesh, in_specs=in_specs, out_specs=out_specs, check_vma=False
    )
```

```python
from functools import partial

import jax
import jax.numpy as jnp
from jax import lax
from jax.experimental import pallas as pl
from jax.experimental.pallas import tpu as pltpu
from jax.sharding import PartitionSpec as P

HEAD = 64
GROUP = 4 * HEAD
LN_EPS = 1e-06
NORM_EPS = 1e-06
BIG_NEG = -1000000000.0
F32 = jnp.float32
BF16 = jnp.bfloat16
VMEM_LIMIT = 60 * 2**20


def dot_nn(left, right):
    return lax.dot_general(left, right, (((1,), (0,)), ((), ())), preferred_element_type=F32)


def dot_nt(left, right):
    return lax.dot_general(left, right, (((1,), (1,)), ((), ())), preferred_element_type=F32)


def dot_tn(left, right):
    return lax.dot_general(left, right, (((0,), (0,)), ((), ())), preferred_element_type=F32)


def normalize(inputs):
    center = inputs - jnp.mean(inputs, axis=-1, keepdims=True)
    rstd = lax.rsqrt(jnp.mean(center * center, axis=-1, keepdims=True) + LN_EPS)
    return center * rstd, rstd


def norm_pull(grad, xhat, rstd, gain):
    scaled = grad * gain
    first = jnp.mean(scaled, axis=-1, keepdims=True)
    second = jnp.mean(scaled * xhat, axis=-1, keepdims=True)
    grad_in = rstd * (scaled - first - xhat * second)
    return grad_in, jnp.sum(grad * xhat, axis=0, keepdims=True), jnp.sum(grad, axis=0, keepdims=True)


def unit_pull(raw, grad):
    scale = lax.rsqrt(jnp.sum(raw * raw, axis=-1, keepdims=True) + NORM_EPS)
    inner = jnp.sum(grad * raw, axis=-1, keepdims=True)
    return scale * grad - raw * (scale * scale * scale * inner)


MESH = pl.DeviceIdType.MESH
DMA = pltpu.SemaphoreType.DMA


class Gather:
    def __init__(self, shards, outs, refs, split=1):
        count = len(outs)
        self.units = [(array, piece) for array in range(count) for piece in range(split)]
        self.split = split
        self.ins, self.outs, self.shards, sems = refs[:count], outs, shards, refs[count:]
        self.local, self.up, self.down, self.across, self.below, self.above, self.near, self.out, self.back = sems
        self.dp, self.z = lax.axis_index("dp"), lax.axis_index("mp")
        dp, z = self.dp, self.z
        self.core, self.x, self.y = dp % 2, dp // 2 % 2, dp // 4
        self.depth = outs[0].shape[1]
        self.color = (self.x + self.y) % 2
        east, north = 2 - 4 * self.x, 4 - 8 * self.y
        self.peers = [(dp + east, z), (dp + north, z), (dp + east + north, z)]
        self.twin = (dp + 1 - 2 * self.core, z)

    @staticmethod
    def semaphores(count, depth):
        grid = (count, depth)
        return [DMA((count,)), DMA(grid), DMA(grid), DMA((3, *grid)), DMA(grid), DMA(grid), DMA((3, *grid)), DMA(grid), DMA(grid)]

    def enter(self, everyone=0):
        barrier = pltpu.get_barrier_semaphore()
        peers = [*self.peers, self.twin]
        if everyone:
            peers = [((self.dp + k) % everyone, self.z) for k in range(1, everyone)]
        for peer in peers:
            pl.semaphore_signal(barrier, inc=1, device_id=peer, device_id_type=MESH)
        for step in (-1, 1):

            @pl.when(self.inside(self.z + step))
            def _(step=step):
                pl.semaphore_signal(barrier, inc=1, device_id=(self.dp, self.z + step), device_id_type=MESH)

        ends = (self.z > 0).astype(jnp.int32) + (self.z < self.depth - 1).astype(jnp.int32)
        pl.semaphore_wait(barrier, len(peers) + ends)

    def inside(self, z):
        return (z >= 0) & (z < self.depth)

    def tall(self, index):
        return self.ins[self.units[index][0]].shape[1] // self.split

    def part(self, index, source, first, size, core=None):
        array, piece = self.units[index]
        mats = self.ins[array].shape[0] // 2
        core = self.core if core is None else core
        first = pl.multiple_of(piece * self.tall(index) + first, 16)
        return self.outs[array].at[pl.ds(core * mats, mats), source, pl.ds(first, size), :]

    def copy(self, src, dst, send, recv, to):
        return pltpu.make_async_remote_copy(
            src_ref=src, dst_ref=dst, send_sem=send, recv_sem=recv, device_id=to, device_id_type=MESH
        )

    def span(self, index):
        tall = self.tall(index)
        return self.color * (tall // 2) + self.y * (tall // 6), tall // 3

    def hop(self, index, source, step):
        spot = self.part(index, source, *self.span(index))
        send, recv = (self.up, self.below) if step > 0 else (self.down, self.above)
        return self.copy(spot, spot, send.at[index, source], recv.at[index, source], (self.dp, self.z + step))

    def first_hop(self, index, step):
        first, size = self.span(index)
        array, piece = self.units[index]
        mats = self.ins[array].shape[0] // 2
        begin = pl.multiple_of(piece * self.tall(index) + first, 16)
        src = self.ins[array].at[pl.ds(self.core * mats, mats), pl.ds(begin, size), :]
        send, recv = (self.up, self.below) if step > 0 else (self.down, self.above)
        spot = self.part(index, self.z, first, size)
        return self.copy(src, spot, send.at[index, self.z], recv.at[index, self.z], (self.dp, self.z + step))

    def side(self, index, source, which, inward=False):
        tall = self.tall(index)
        color, y = self.color, self.y
        if inward:
            color, y = (1 - color, y) if which == 0 else (1 - color, 1 - y) if which == 1 else (color, 1 - y)
        pace, size = ((tall // 4, tall // 4), (tall // 4, tall // 4), (tall // 3, tall // 6))[which]
        spot = self.part(index, source, color * (tall // 2) + y * pace, size)
        sems = self.across.at[which, index, source], self.near.at[which, index, source]
        return self.copy(spot, spot, *sems, self.peers[which])

    def pass_on(self, index, source, inward=False):
        core = 1 - self.core if inward else self.core
        spot = self.part(index, source, 0, self.tall(index), core)
        return self.copy(spot, spot, self.out.at[index, source], self.back.at[index, source], self.twin)

    def keep(self, index):
        array, piece = self.units[index]
        rows = pl.ds(piece * self.tall(index), self.tall(index))
        spot = self.outs[array].at[:, self.z, rows, :]
        return pltpu.make_async_copy(self.ins[array].at[:, rows, :], spot, self.local.at[index])

    def start(self, everyone=0):
        count = 0
        for stack in self.ins:
            for index in range(stack.shape[0]):
                stack[index] = self.shards[count][...]
                count += 1
        self.enter(everyone)
        for index in range(len(self.units)):
            for step in (1, -1):

                @pl.when(self.inside(self.z + step))
                def _(index=index, step=step):
                    self.first_hop(index, step).start()

            self.keep(index).start()

    def each(self, distance, what, only=None):
        for index in range(len(self.units)) if only is None else (only,):
            for step in (1, -1):
                source = self.z - step * distance

                @pl.when(self.inside(source))
                def _(index=index, step=step, source=source):
                    what(index, step, source)

    def pull(self, distance, only=None):
        def what(index, step, source):
            self.hop(index, source, step).wait_recv()

            @pl.when(self.inside(self.z + step))
            def _():
                self.hop(index, source, step).start()

            for which in range(3):
                self.side(index, source, which).start()

        self.each(distance, what, only)

    def pair(self, distance):
        def what(index, step, source):
            for which in range(3):
                self.side(index, source, which, inward=True).wait_recv()
            self.pass_on(index, source).start()

        self.each(distance, what)

    def finish(self):
        def what(index, step, source):
            self.pass_on(index, source, inward=True).wait_recv()
            self.pass_on(index, source).wait_send()
            for which in range(3):
                self.side(index, source, which).wait_send()

            @pl.when(self.inside(self.z + step))
            def _():
                self.hop(index, source, step).wait_send()

        for distance in range(1, self.depth):
            self.each(distance, what)
        for index in range(len(self.units)):
            for step in (1, -1):

                @pl.when(self.inside(self.z + step))
                def _(index=index, step=step):
                    self.first_hop(index, step).wait_send()

            self.keep(index).wait()


class Reduce:
    def __init__(self, src, done, half, part, quarter, twin_sems, plane_sems):
        self.src, self.done, self.half, self.part, self.quarter = src, done, half, part, quarter
        self.twin_sems, self.plane_sems = twin_sems, plane_sems
        dp, z = lax.axis_index("dp"), lax.axis_index("mp")
        self.core, self.chip = dp % 2, dp // 2
        x, y = self.chip % 2, self.chip // 2
        east, north = 2 - 4 * x, 4 - 8 * y
        self.shifts = (east, north, east + north)
        self.peers = [(dp + shift, z) for shift in self.shifts]
        self.twin = (dp + 1 - 2 * self.core, z)
        self.tall = src.shape[0]

    @staticmethod
    def scratch(shape):
        rows, columns = shape
        sizes = ((rows, columns), (rows // 2, columns), (rows // 2, columns), (3, rows // 8, columns))
        return [*(pltpu.VMEM(size, BF16) for size in sizes), DMA((4,)), DMA((4, 3))]

    def enter(self):
        barrier = pltpu.get_barrier_semaphore()
        for peer in [*self.peers, self.twin]:
            pl.semaphore_signal(barrier, inc=1, device_id=peer, device_id_type=MESH)
        pl.semaphore_wait(barrier, 4)

    def copy(self, src, dst, send, recv, to):
        return pltpu.make_async_remote_copy(
            src_ref=src, dst_ref=dst, send_sem=send, recv_sem=recv, device_id=to, device_id_type=MESH
        )

    def mine(self, core):
        return pl.ds(pl.multiple_of(core * (self.tall // 2), 16), self.tall // 2)

    def slot(self, chip, core=None):
        first = chip * (self.tall // 8)
        if core is not None:
            first = first + core * (self.tall // 2)
        return pl.ds(pl.multiple_of(first, 16), self.tall // 8)

    def to_twin(self):
        sems = self.twin_sems.at[0], self.twin_sems.at[1]
        return self.copy(self.src.at[self.mine(1 - self.core)], self.half, *sems, self.twin)

    def scatter(self, which):
        chip = self.chip + self.shifts[which] // 2
        sems = self.plane_sems.at[0, which], self.plane_sems.at[1, which]
        return self.copy(self.part.at[self.slot(chip)], self.quarter.at[which], *sems, self.peers[which])

    def spread(self, which, chip):
        spot = self.done.at[self.slot(chip, self.core)]
        sems = self.plane_sems.at[2, which], self.plane_sems.at[3, which]
        return self.copy(spot, spot, *sems, self.peers[which])

    def back(self, core):
        spot = self.done.at[self.mine(core)]
        return self.copy(spot, spot, self.twin_sems.at[2], self.twin_sems.at[3], self.twin)

    def stage(self, number):
        if number == 1:
            self.to_twin().start()
        elif number == 2:
            self.to_twin().wait_recv()
            total = self.src[self.mine(self.core), :].astype(F32) + self.half[...].astype(F32)
            self.part[...] = total.astype(BF16)
            for which in range(3):
                self.scatter(which).start()
        elif number == 3:
            total = self.part[self.slot(self.chip), :].astype(F32)
            for which in range(3):
                self.scatter(which).wait_recv()
                total = total + self.quarter[which].astype(F32)
            self.done[self.slot(self.chip, self.core), :] = total.astype(BF16)
            for which in range(3):
                self.spread(which, self.chip).start()
        elif number == 4:
            for which in range(3):
                self.spread(which, self.chip + self.shifts[which] // 2).wait_recv()
            self.back(self.core).start()
        else:
            self.back(1 - self.core).wait_recv()
            self.to_twin().wait_send()
            for which in range(3):
                self.scatter(which).wait_send()
                self.spread(which, self.chip).wait_send()
            self.back(self.core).wait_send()


ARRIVALS = ((1, 0), (1, 1), (2, 0), (2, 1), (3, 0), (3, 1))


def spread_heads(tensor):
    count = tensor.shape[0]
    left = lax.broadcasted_iota(jnp.int32, (count, 2 * HEAD), 1) < HEAD
    low, high = tensor[:, : 2 * HEAD], tensor[:, 2 * HEAD :]
    zero = jnp.zeros_like(low)
    blank = jnp.zeros((2 * count, 2 * HEAD), tensor.dtype)
    near = jnp.concatenate([jnp.where(left, low, zero), jnp.where(left, zero, low), blank], axis=0)
    far = jnp.concatenate([blank, jnp.where(left, high, zero), jnp.where(left, zero, high)], axis=0)
    return jnp.concatenate([near, far], axis=1).astype(BF16)


def collect_heads(stacked, count):
    left = lax.broadcasted_iota(jnp.int32, (count, 2 * HEAD), 1) < HEAD
    low = jnp.where(left, stacked[:count, : 2 * HEAD], stacked[count : 2 * count, : 2 * HEAD])
    high = jnp.where(
        left, stacked[2 * count : 3 * count, 2 * HEAD :], stacked[3 * count :, 2 * HEAD :]
    )
    return jnp.concatenate([low, high], axis=1)


def attend_probs(query_blocks, keys, keep):
    scores = dot_nt(keys, query_blocks)
    scores = jnp.where(keep, scores, BIG_NEG)
    top = jnp.max(scores, axis=0, keepdims=True)
    shifted = jnp.exp(scores - top)
    total = jnp.sum(shifted, axis=0, keepdims=True)
    return shifted * (1.0 / total)


def attend_forward(query, keys, values, keep):
    probs = attend_probs(spread_heads(query), keys, keep).astype(BF16)
    return collect_heads(dot_tn(probs, values), query.shape[0]), probs


def split_heads(tensor):
    left = lax.broadcasted_iota(jnp.int32, tensor.shape, 1) < HEAD
    zero = jnp.zeros_like(tensor)
    return jnp.concatenate([jnp.where(left, tensor, zero), jnp.where(left, zero, tensor)], axis=0).astype(BF16)


def attend_short(query, keys, values, keep):
    count = query.shape[0]
    left = lax.broadcasted_iota(jnp.int32, (count, 2 * HEAD), 1) < HEAD
    out = []
    for half in range(2):
        at = slice(half * 2 * HEAD, (half + 1) * 2 * HEAD)
        probs = attend_probs(split_heads(query[:, at]), keys[:, at], keep[:, : 2 * count])
        stacked = dot_nn(jnp.transpose(probs.astype(BF16)), values[:, at])
        out.append(jnp.where(left, stacked[:count], stacked[count:]))
    return jnp.concatenate(out, axis=1)


def attend_backward(query, keys, values, keep, grad_context, kept=None):
    query_blocks = spread_heads(query)
    grad_blocks = spread_heads(grad_context)
    probs = attend_probs(query_blocks, keys, keep) if kept is None else kept.astype(F32)
    grad_probs = dot_nt(values, grad_blocks)
    inner = jnp.sum(grad_probs * probs, axis=0, keepdims=True)
    grad_scores = (probs * (grad_probs - inner)).astype(BF16)
    grad_values = dot_nn(probs.astype(BF16) if kept is None else kept, grad_blocks)
    grad_keys = dot_nn(grad_scores, query_blocks)
    grad_query = collect_heads(dot_tn(grad_scores, keys), query.shape[0]) * 0.125
    return grad_query, grad_keys, grad_values


def row_keep(bound, length):
    key = lax.broadcasted_iota(jnp.int32, (length, 4 * length), 0)
    query = lax.broadcasted_iota(jnp.int32, (length, 4 * length), 1) % length
    return (key >= bound) == (query >= bound)


def window(which, width):
    return pl.ds(pl.multiple_of(which * 3 // 2 * (width // 2), width // 2), width)


def own_rows(acc, which, own):
    odd = which % 2 == 1
    return jnp.where(odd, acc[acc.shape[0] - own :], acc[:own])


def prep_kernel(gathers, count, *refs):
    region_ref, picture_ref, weight_ref = refs[:3]
    shards, refs = refs[3 : 3 + count], refs[3 + count :]
    moved_ref, embed_ref = refs[:2]
    whole, refs = refs[2 : 2 + gathers], refs[2 + gathers :]
    flat_ref = refs[0]
    patch_count, images, lanes = region_ref.shape
    padded = moved_ref.shape[1]
    full_tiles = patch_count // 8 * 8
    step = pl.program_id(0)
    steps = pl.num_programs(0)
    gather = Gather(shards, whole, refs[1:]) if gathers else None

    @pl.when(step == 0)
    def _():
        if gather:
            gather.start()
        raw = dot_nn(picture_ref[...], weight_ref[...])
        scale = lax.rsqrt(jnp.sum(raw * raw, axis=-1, keepdims=True) + NORM_EPS)
        embed_ref[...] = (raw * scale).astype(BF16)

    flat_ref[...] = region_ref[...].reshape(patch_count * images, lanes).astype(F32)
    row = lax.broadcasted_iota(jnp.int32, (padded - full_tiles, lanes), 0)
    for image in range(images):
        main = flat_ref[pl.ds(image, full_tiles, stride=images), :]
        moved_ref[image, 0:full_tiles, :] = main.astype(BF16)
        last = flat_ref[pl.ds(full_tiles * images + image, 1), :]
        moved_ref[image, full_tiles:padded, :] = jnp.where(row == 0, last, 0.0).astype(BF16)

    if gather:

        for place, arrival in enumerate(ARRIVALS):

            @pl.when(step == place + 1)
            def _(arrival=arrival):
                gather.pull(*arrival)

        @pl.when(step == steps - 1)
        def _():
            gather.pair(1)
            gather.pair(2)
            gather.pair(3)
            gather.finish()


def self_forward_kernel(length, gathers, count, *refs):
    bound_ref, tok_ref, wqk_ref, wv_ref, wout_ref, embed_ref = refs[:6]
    shards, refs = refs[6 : 6 + count], refs[6 + count :]
    qkv_ref, ctx_ref, xhat_ref, rstd_ref = refs[:4]
    whole, refs = refs[4 : 4 + gathers], refs[4 + gathers :]
    width = tok_ref.shape[1]
    rows = tok_ref.shape[0] // length
    step = pl.program_id(0)
    steps = pl.num_programs(0)
    if gathers:
        images_ref, embed_local, embed_send, embed_recv = refs[:4]
        gather = Gather(shards, whole, refs[4:])
        dp, z = lax.axis_index("dp"), lax.axis_index("mp")
        dp_size = images_ref.shape[0] // embed_ref.shape[0]
        held = embed_ref.shape[0]

        def embed_copy(k, owner, to):
            spot = images_ref.at[pl.ds(pl.multiple_of(owner * held, 16), held), :]
            return pltpu.make_async_remote_copy(
                src_ref=embed_ref, dst_ref=spot, send_sem=embed_send.at[k], recv_sem=embed_recv.at[k],
                device_id=(to, z), device_id_type=MESH,
            )

        def embed_own():
            spot = images_ref.at[pl.ds(pl.multiple_of(dp * held, 16), held), :]
            return pltpu.make_async_copy(embed_ref, spot, embed_local)

        @pl.when(step == 0)
        def _():
            gather.start(everyone=dp_size)
            embed_own().start()
            for k in range(1, dp_size):
                embed_copy(k, dp, (dp + k) % dp_size).start()

        for distance in range(1, 4):

            @pl.when(step == distance)
            def _(distance=distance):
                gather.pull(distance, 1 if distance == 3 else None)

    tok = tok_ref[...]
    for part in range(3):
        weight = wv_ref[...] if part == 2 else wqk_ref[part * width : (part + 1) * width, :]
        proj = dot_nt(tok, weight)
        if part == 0:
            proj = proj * 0.125
        qkv_ref[:, part * width : (part + 1) * width] = proj.astype(BF16)

    if gathers:

        @pl.when(step == 2)
        def _():
            gather.pull(3, 0)

    def pair(index, carry):
        span = pl.ds(pl.multiple_of(index * 2 * length, 16), 2 * length)
        keeps = [row_keep(bound_ref[step * rows + 2 * index + j], length) for j in range(2)]
        for group in range(width // GROUP):
            q, k, v = (
                qkv_ref[span, part * width + group * GROUP : part * width + (group + 1) * GROUP].astype(F32)
                for part in range(3)
            )
            out = []
            for j in range(2):
                at = slice(j * length, (j + 1) * length)
                out.append(attend_short(q[at], k[at].astype(BF16), v[at].astype(BF16), keeps[j]))
            ctx_ref[span, group * GROUP : (group + 1) * GROUP] = jnp.concatenate(out, axis=0).astype(BF16)
        return carry

    lax.fori_loop(0, rows // 2, pair, 0, unroll=2)
    attn = dot_nn(ctx_ref[...], wout_ref[...])
    xhat, rstd = normalize(tok.astype(F32) + attn)
    xhat_ref[...] = xhat
    rstd_ref[...] = rstd

    if gathers:

        @pl.when(step == steps - 1)
        def _():
            for distance in range(1, 4):
                gather.pair(distance)
            for k in range(1, dp_size):
                embed_copy(k, (dp + dp_size - k) % dp_size, (dp + k) % dp_size).wait_recv()
                embed_copy(k, dp, (dp + k) % dp_size).wait_send()
            embed_own().wait()
            gather.finish()


def cross_forward_kernel(patch_count, length, gathers, count, *refs):
    region_ref, wkv_ref, xhat1_ref, norm_ref, wcq_ref, wout_ref = refs[:6]
    shards, refs = refs[6 : 6 + count], refs[6 + count :]
    kv_ref, cq_ref, ctx_ref, xhat_ref, rstd_ref, probs_ref = refs[:6]
    whole, refs = refs[6 : 6 + gathers], refs[6 + gathers :]
    images, padded, vision = region_ref.shape
    width = cq_ref.shape[1]
    step = pl.program_id(0)
    steps = pl.num_programs(0)
    gather = Gather(shards, whole, refs, split=2) if gathers else None
    if gathers:

        @pl.when(step == 0)
        def _():
            gather.start()

        for place, arrival in enumerate(ARRIVALS[1::2]):

            @pl.when(step == place + 1)
            def _(arrival=arrival):
                gather.pull(*arrival)

    hidden1 = xhat1_ref[...] * norm_ref[0:1] + norm_ref[1:2]
    cq_ref[...] = (dot_nt(hidden1.astype(BF16), wcq_ref[...]) * 0.125).astype(BF16)
    flat = region_ref[...].reshape(images * padded, vision)

    def chunk(index, carry):
        at = pl.ds(pl.multiple_of(index * 512, 512), 512)
        proj = dot_nt(flat, wkv_ref[at, :])
        kv_ref[:, :, at] = proj.astype(BF16).reshape(images, padded, 512)
        return carry

    lax.fori_loop(0, 2 * width // 512, chunk, 0, unroll=True)
    if gathers:
        for place, arrival in enumerate(ARRIVALS[::2]):

            @pl.when(step == place)
            def _(arrival=arrival):
                gather.pull(*arrival)

    keep = lax.broadcasted_iota(jnp.int32, (padded, 4 * length), 0) < patch_count

    def pair(index, carry):
        span = pl.ds(pl.multiple_of(index * 2 * length, 16), 2 * length)
        for group in range(width // GROUP):
            lanes = slice(group * GROUP, (group + 1) * GROUP)
            q = cq_ref[span, lanes].astype(F32)
            out = []
            for j in range(2):
                image = 2 * index + j
                keys = kv_ref[image, :, lanes]
                values = kv_ref[image, :, width + group * GROUP : width + (group + 1) * GROUP]
                context, probs = attend_forward(q[j * length : (j + 1) * length], keys, values, keep)
                out.append(context)
                probs_ref[image, group] = probs
            ctx_ref[span, lanes] = jnp.concatenate(out, axis=0).astype(BF16)
        return carry

    lax.fori_loop(0, images // 2, pair, 0, unroll=4)
    xhat, rstd = normalize(hidden1 + dot_nn(ctx_ref[...], wout_ref[...]))
    xhat_ref[...] = xhat
    rstd_ref[...] = rstd

    if gathers:

        @pl.when(step == steps - 1)
        def _():
            for distance in range(1, 4):
                gather.pair(distance)
            gather.finish()


def gelu_parts(inputs):
    cdf = 0.5 * (1.0 + lax.erf(inputs * 0.7071067811865476))
    density = jnp.exp(inputs * inputs * -0.5) * 0.3989422804014327
    return inputs * cdf, cdf + inputs * density


def feed_forward_kernel(
    length, bound_ref, which_ref, temp_ref, xhat2_ref, rstd2_ref, norm_ref,
    wup_ref, wdown_ref, adj_ref, target_ref, images_ref, wtext_ref,
    out_ref, loss_ref, pack_ref, dr2_ref, dup_ref, ddown_ref, dgain2_ref, dshift2_ref, dgain3_ref, dshift3_ref,
    dtext_ref, dtemp_ref,
    act_ref, slope_ref, final_ref, grad_ref, lead_ref, up_acc, down_acc, text_acc,
):
    step = pl.program_id(0)
    steps = pl.num_programs(0)
    tokens, width = xhat2_ref.shape
    hidden_units = wup_ref.shape[0]
    rows = tokens // length
    chunk = min(768, hidden_units)

    @pl.when(step == 0)
    def _():
        for ref in (dgain2_ref, dshift2_ref, dgain3_ref, dshift3_ref, dtemp_ref, up_acc, down_acc, text_acc):
            ref[...] = jnp.zeros_like(ref)

    xhat2 = xhat2_ref[...]
    hidden2 = xhat2 * norm_ref[2:3] + norm_ref[3:4]
    low = hidden2.astype(BF16)
    final_ref[...] = hidden2

    def forward(index, carry):
        at = pl.ds(pl.multiple_of(index * chunk, chunk), chunk)
        act, slope = gelu_parts(dot_nt(low, wup_ref[at, :]))
        act = act.astype(BF16)
        act_ref[:, at] = act
        slope_ref[:, at] = slope
        final_ref[...] += dot_nn(act, wdown_ref[at, :])
        return carry

    lax.fori_loop(0, hidden_units // chunk, forward, 0, unroll=True)
    xhat3, rstd3 = normalize(final_ref[...])
    final = xhat3 * norm_ref[4:5] + norm_ref[5:6]
    out_ref[...] = final.astype(BF16)
    final_ref[...] = final
    grad_ref[...] = adj_ref[...].astype(F32)

    for row in range(rows):
        lead_ref[pl.ds(2 * row, 1), :] = final_ref[pl.ds(row * length, 1), :]
        second = row * length + bound_ref[step * rows + row]
        lead_ref[pl.ds(2 * row + 1, 1), :] = final_ref[pl.ds(second, 1), :]
    lead = lead_ref[...].astype(BF16)
    raw = dot_nn(lead, wtext_ref[...])
    text = raw * lax.rsqrt(jnp.sum(raw * raw, axis=-1, keepdims=True) + NORM_EPS)
    text_low = text.astype(BF16)
    temp = temp_ref[0]
    logits = dot_nt(text_low, images_ref[...]) / temp
    top = jnp.max(logits, axis=1, keepdims=True)
    lse = top + jnp.log(jnp.sum(jnp.exp(logits - top), axis=1, keepdims=True))
    target = target_ref[...]
    hit = lax.broadcasted_iota(jnp.int32, logits.shape, 1) == target
    loss_ref[...] = lse - jnp.sum(jnp.where(hit, logits, 0.0), axis=1, keepdims=True)
    dlogits = jnp.exp(logits - lse) - hit.astype(F32)
    dtemp_ref[...] += -jnp.sum(jnp.sum(dlogits * logits, axis=1, keepdims=True), axis=0, keepdims=True) / temp
    embed = raw.shape[1]
    lane = lax.broadcasted_iota(jnp.int32, (2 * rows, 128), 1)
    pack_ref[:, :embed] = text_low.astype(F32)
    pack_ref[:, embed:] = jnp.where(lane == 0, lse, jnp.where(lane == 1, target.astype(F32), 0.0))
    dtext = dot_nn((dlogits / temp).astype(BF16), images_ref[...])
    draw = unit_pull(raw, dtext).astype(BF16)
    text_acc[...] += dot_tn(lead, draw)
    lead_ref[...] = dot_nt(draw, wtext_ref[...])
    for row in range(rows):
        first = pl.ds(row * length, 1)
        grad_ref[first, :] += lead_ref[pl.ds(2 * row, 1), :]
        second = pl.ds(row * length + bound_ref[step * rows + row], 1)
        grad_ref[second, :] += lead_ref[pl.ds(2 * row + 1, 1), :]

    dr3, dgain3, dshift3 = norm_pull(grad_ref[...], xhat3, rstd3, norm_ref[4:5])
    dgain3_ref[...] += dgain3
    dshift3_ref[...] += dshift3
    grad_ref[...] = dr3
    dfinal = dr3.astype(BF16)
    own = hidden_units // 4
    own_at = pl.ds(pl.multiple_of(which_ref[0] * own, own), own)
    down_acc[...] += dot_tn(act_ref[:, own_at], dfinal)

    def backward(index, carry):
        at = pl.ds(pl.multiple_of(index * chunk, chunk), chunk)
        dact = dot_nt(dfinal, wdown_ref[at, :])
        dinner = (dact * slope_ref[:, at]).astype(BF16)
        act_ref[:, at] = dinner
        grad_ref[...] += dot_nn(dinner, wup_ref[at, :])
        return carry

    lax.fori_loop(0, hidden_units // chunk, backward, 0, unroll=True)
    up_acc[...] += dot_tn(low, act_ref[:, own_at])
    dr2, dgain2, dshift2 = norm_pull(grad_ref[...], xhat2, rstd2_ref[...], norm_ref[2:3])
    dgain2_ref[...] += dgain2
    dshift2_ref[...] += dshift2
    dr2_ref[...] = dr2

    @pl.when(step == steps - 1)
    def _():
        dup_ref[...] = up_acc[...].astype(BF16)
        ddown_ref[...] = down_acc[...].astype(BF16)
        dtext_ref[...] = text_acc[...].astype(BF16)


def cross_backward_kernel(
    patch_count, length, which_ref, region_ref, kv_ref, cq_ref, ctx_ref, xhat1_ref, rstd1_ref, norm_ref,
    dr2_ref, wkv_ref, wout_ref, wcq_ref, probs_ref,
    dregion_ref, dr1_ref, dkv_ref, dqo_ref, dgain_ref, dshift_ref,
    dctx_ref, dq_ref, grads_ref, flat_ref, stage_ref, kv_acc, cq_acc, out_acc, sem,
):
    step = pl.program_id(0)
    steps = pl.num_programs(0)
    images, padded, vision = region_ref.shape
    width = cq_ref.shape[1]
    own = width // 4
    which = which_ref[0]
    mine = window(which, GROUP)
    wide = stage_ref.shape[2]
    parts = wide // images
    stored = flat_ref.shape[1] // wide

    @pl.when(step == 0)
    def _():
        for ref in (dgain_ref, dshift_ref, kv_acc, cq_acc, out_acc):
            ref[...] = jnp.zeros_like(ref)

    dr2 = dr2_ref[...]
    dx = dr2.astype(BF16)
    dctx_ref[...] = dot_nt(dx, wout_ref[...]).astype(BF16)
    out_acc[...] += dot_tn(ctx_ref[:, mine], dx)

    def pair(index, carry):
        span = pl.ds(pl.multiple_of(index * 2 * length, 16), 2 * length)
        for group in range(width // GROUP):
            lanes = slice(group * GROUP, (group + 1) * GROUP)
            value_lanes = slice(width + group * GROUP, width + (group + 1) * GROUP)
            q = cq_ref[span, lanes].astype(F32)
            d = dctx_ref[span, lanes].astype(F32)
            out = []
            for j in range(2):
                image = 2 * index + j
                at = slice(j * length, (j + 1) * length)
                dq, dk, dv = attend_backward(
                    q[at], kv_ref[image, :, lanes], kv_ref[image, :, value_lanes], None, d[at], probs_ref[image, group]
                )
                out.append(dq)
                grads_ref[image, :, lanes] = dk.astype(BF16)
                grads_ref[image, :, value_lanes] = dv.astype(BF16)
            dq_ref[span, lanes] = jnp.concatenate(out, axis=0).astype(BF16)
        return carry

    lax.fori_loop(0, images // 2, pair, 0, unroll=4)

    some = 4
    for index in range(images // some):
        grads = grads_ref[index * some : (index + 1) * some].reshape(some * padded, 2 * width)
        dregion = dot_nn(grads, wkv_ref[...])
        for image in range(some):
            spot = pl.ds(step % parts * images + index * some + image, stored, stride=wide)
            for lane in range(vision // 128):
                flat_ref[lane, spot, :] = dregion[
                    image * padded : image * padded + stored, lane * 128 : (lane + 1) * 128
                ]
    region = region_ref[...].reshape(images * padded, vision)
    for part in range(2):
        at = window(which, GROUP)
        grads = grads_ref[:, :, pl.ds(pl.multiple_of(which * 3 // 2 * 128 + part * width, 128), GROUP)]
        kv_acc[part] += dot_tn(grads.reshape(images * padded, GROUP), region)

    pieces = 5
    patches = patch_count // pieces
    tall = patches * wide

    def send(index):
        slot = index % 2
        base = pl.multiple_of(step // parts * wide, 16)
        return pltpu.make_async_copy(
            stage_ref.at[slot],
            dregion_ref.at[pl.ds(index * patches, patches), pl.ds(base, wide), :],
            sem.at[slot],
        )

    @pl.when(step % parts == parts - 1)
    def _():
        for index in range(pieces):
            rows = slice(index * tall, (index + 1) * tall)
            low = jnp.concatenate([flat_ref[c, rows, :].astype(BF16) for c in range(vision // 128)], axis=1)
            if index >= 2:
                send(index - 2).wait()
            stage_ref[index % 2] = low.reshape(patches, wide, vision)
            send(index).start()
        send(pieces - 2).wait()
        send(pieces - 1).wait()

    xhat1 = xhat1_ref[...]
    hidden1 = (xhat1 * norm_ref[0:1] + norm_ref[1:2]).astype(BF16)
    cq_acc[...] += dot_tn(dq_ref[:, mine], hidden1)
    dh1 = dr2 + dot_nn(dq_ref[...], wcq_ref[...])
    dr1, dgain, dshift = norm_pull(dh1, xhat1, rstd1_ref[...], norm_ref[0:1])
    dr1_ref[...] = dr1
    dgain_ref[...] += dgain
    dshift_ref[...] += dshift

    @pl.when(step == steps - 1)
    def _():
        for part in range(2):
            dkv_ref[part * own : (part + 1) * own, :] = own_rows(kv_acc[part], which, own).astype(BF16)
        dqo_ref[:own, :] = own_rows(cq_acc[...], which, own).astype(BF16)
        dqo_ref[own:, :] = own_rows(out_acc[...], which, own).astype(BF16)


def self_backward_kernel(length, sums, *refs):
    bound_ref, tok_ref, qkv_ref, ctx_ref, dr1_ref, wqk_ref, wv_ref, wout_ref = refs[:8]
    refs = refs[8:]
    if sums:
        dkv_ref, dqo_ref, temp_ref, pack_ref, picture_ref, wimage_ref = refs[:6]
        vectors, refs = refs[6:13], refs[13:]
    dtok_ref, last_ref = refs[:2]
    refs = refs[2:]
    if sums:
        outs, dpicture_ref, refs = refs[:4], refs[4], refs[5:]
    dctx_ref, grads_ref, qkv_acc, out_acc, last = refs[:5]
    refs = refs[5:]
    step = pl.program_id(0)
    steps = pl.num_programs(0)
    half = steps // 2
    tokens, width = tok_ref.shape
    rows = tokens // length
    own = width // 4
    which = lax.axis_index("mp")
    if sums:
        packs, dimage, small, pack_sent, pack_came = refs[:5]
        refs = refs[5:]
        spots = (dkv_ref, dqo_ref, small, dimage, last.at[: 2 * own], last.at[2 * own :])
        kv_sum, qo_sum, small_sum, image_sum, *finals = (
            Reduce(spot, *refs[6 * i : 6 * i + 6]) for i, spot in enumerate(spots)
        )
        dp, z = lax.axis_index("dp"), lax.axis_index("mp")
        dp_size = packs.shape[0]

        def pack_copy(k, owner):
            return pltpu.make_async_remote_copy(
                src_ref=pack_ref, dst_ref=packs.at[owner], send_sem=pack_sent.at[k], recv_sem=pack_came.at[k],
                device_id=((dp + k) % dp_size, z), device_id_type=MESH,
            )

        @pl.when(step == 0)
        def _():
            small[...] = jnp.zeros(small.shape, BF16)
            lines = [ref[...] for ref in vectors[:6]] + [jnp.broadcast_to(vectors[6][...], (1, width))]
            lines = [*lines, jnp.zeros((16 - len(lines), width), F32)]
            small[0:16, :] = jnp.concatenate(lines, axis=0).astype(BF16)
            barrier = pltpu.get_barrier_semaphore()
            for k in range(1, dp_size):
                pl.semaphore_signal(barrier, inc=1, device_id=((dp + k) % dp_size, z), device_id_type=MESH)
            pl.semaphore_wait(barrier, dp_size - 1)
            for k in range(1, dp_size):
                pack_copy(k, dp).start()
            packs[dp] = pack_ref[...]
            for reduce in (kv_sum, qo_sum, small_sum):
                reduce.stage(1)

        @pl.when(step == 1)
        def _():
            for reduce in (kv_sum, qo_sum, small_sum):
                reduce.stage(2)
            for k in range(1, dp_size):
                pack_copy(k, (dp + dp_size - k) % dp_size).wait_recv()
                pack_copy(k, dp).wait_send()
            everyone = packs[...].reshape(-1, packs.shape[2])
            first = dp * picture_ref.shape[0]
            dpicture, dweight = image_backward(first, temp_ref[0], picture_ref[...], wimage_ref[...], everyone)
            dpicture_ref[...] = dpicture
            dimage[...] = dweight.astype(BF16)
            image_sum.stage(1)

        for number in (3, 4):

            @pl.when(step == number - 1)
            def _(number=number):
                for reduce in (kv_sum, qo_sum, small_sum):
                    reduce.stage(number)
                image_sum.stage(number - 1)

    @pl.when(step == 0)
    def _():
        for ref in (qkv_acc, out_acc):
            ref[...] = jnp.zeros_like(ref)

    @pl.when(step < half)
    def _():
        all_rows = pl.ds(pl.multiple_of(step * tokens, 16), tokens)
        da = dr1_ref[...].astype(BF16)
        dctx_ref[...] = dot_nt(da, wout_ref[...]).astype(BF16)
        out_acc[...] += dot_tn(ctx_ref[:, window(which, GROUP)], da)

        def pair(index, carry):
            span = pl.ds(pl.multiple_of(index * 2 * length, 16), 2 * length)
            far = pl.ds(pl.multiple_of(step * tokens + index * 2 * length, 16), 2 * length)
            keeps = [row_keep(bound_ref[step * rows + 2 * index + j], length) for j in range(2)]
            for group in range(width // GROUP):
                q, k, v = (
                    qkv_ref[span, part * width + group * GROUP : part * width + (group + 1) * GROUP].astype(F32)
                    for part in range(3)
                )
                d = dctx_ref[span, group * GROUP : (group + 1) * GROUP].astype(F32)
                outs = []
                for j in range(2):
                    at = slice(j * length, (j + 1) * length)
                    outs.append(attend_backward(q[at], k[at].astype(BF16), v[at].astype(BF16), keeps[j], d[at]))
                for part in range(3):
                    both = jnp.concatenate([outs[0][part], outs[1][part]], axis=0).astype(BF16)
                    grads_ref[far, part * width + group * GROUP : part * width + (group + 1) * GROUP] = both
            return carry

        lax.fori_loop(0, rows // 2, pair, 0, unroll=4)
        tok = tok_ref[...]
        for part in range(3):
            mine = grads_ref[all_rows, pl.ds(pl.multiple_of(which * 3 // 2 * 128 + part * width, 128), GROUP)]
            qkv_acc[part] += dot_tn(mine, tok)

    @pl.when(step == half - 1)
    def _():
        for part in range(3):
            last[part * own : (part + 1) * own, :] = own_rows(qkv_acc[part], which, own).astype(BF16)
        last[3 * own : 4 * own, :] = own_rows(out_acc[...], which, own).astype(BF16)
        if sums:
            for reduce in finals:
                reduce.stage(1)

    @pl.when(step >= half)
    def _():
        done = pl.ds(pl.multiple_of((step - half) * tokens, 16), tokens)
        part = dr1_ref[...] + dot_nn(grads_ref[done, : 2 * width], wqk_ref[...])
        dtok_ref[...] = part + dot_nn(grads_ref[done, 2 * width :], wv_ref[...])

    if sums:

        @pl.when(step == half)
        def _():
            image_sum.stage(4)
            for reduce in finals:
                reduce.stage(2)

    @pl.when(step == steps - 1)
    def _():
        if sums:
            for reduce in finals:
                reduce.stage(3)
            for reduce in (kv_sum, qo_sum, small_sum, image_sum):
                reduce.stage(5)
            for reduce, out in zip((kv_sum, qo_sum, small_sum, image_sum), outs, strict=True):
                out[...] = reduce.done[...]
            for number in (4, 5):
                for reduce in finals:
                    reduce.stage(number)
            last_ref[: 2 * own, :] = finals[0].done[...]
            last_ref[2 * own :, :] = finals[1].done[...]
        else:
            last_ref[...] = last[...]


def image_backward(first, temp, picture, weight, pack):
    raw = dot_nn(picture, weight)
    own = (raw * lax.rsqrt(jnp.sum(raw * raw, axis=-1, keepdims=True) + NORM_EPS)).astype(BF16)
    embed = raw.shape[1]
    text = pack[:, :embed].astype(BF16)
    lse = pack[:, embed : embed + 1]
    target = pack[:, embed + 1 : embed + 2].astype(jnp.int32)
    logits = dot_nt(text, own) / temp
    hit = lax.broadcasted_iota(jnp.int32, logits.shape, 1) + first == target
    dlogits = jnp.exp(logits - lse) - hit.astype(F32)
    dimage = dot_tn((dlogits / temp).astype(BF16), text)
    draw = unit_pull(raw, dimage).astype(BF16)
    return dot_nt(draw, weight), dot_tn(picture, draw)


def image_backward_kernel(
    first_ref, temp_ref, picture_ref, weight_ref, pack_ref, dpicture_ref, dweight_ref
):
    dpicture, dweight = image_backward(
        first_ref[0], temp_ref[0], picture_ref[...], weight_ref[...], pack_ref[...]
    )
    dpicture_ref[...] = dpicture
    dweight_ref[...] = dweight.astype(BF16)


def widen_kernel(own, last_ref, dkv_ref, dqo_ref, dimage_ref, dup_ref, ddown_ref, dtext_ref, small_ref, *outs):
    for index in range(4):
        outs[index][...] = last_ref[index * own : (index + 1) * own, :].astype(F32)
    for index in range(2):
        outs[4 + index][...] = dqo_ref[index * own : (index + 1) * own, :].astype(F32)
        outs[6 + index][...] = dkv_ref[index * own : (index + 1) * own, :].astype(F32)
    for out, ref in zip(outs[8:12], (dup_ref, ddown_ref, dtext_ref, dimage_ref), strict=True):
        out[...] = ref[...].astype(F32)
    small = small_ref[0:16, :].astype(F32)
    for index in range(6):
        outs[12 + index][...] = small[index]
    outs[18][...] = small[6:7, 0:1]


def full(shape):
    return pl.BlockSpec(shape, lambda i: (0,) * len(shape), pipeline_mode=pl.Buffered(1))


def fixed(shape):
    return pl.BlockSpec(shape, lambda i: (0,) * len(shape))


def rows_of(count, width):
    return pl.BlockSpec((count, width), lambda i: (i, 0))


SMEM = pl.BlockSpec(memory_space=pltpu.SMEM)


def shape_of(shape, kind):
    return jax.ShapeDtypeStruct(shape, kind)


def call(kernel, steps, ins, outs, args, scratch=(), flops=0, moved=0, ident=None):
    specs, shapes = zip(*outs, strict=True)
    remote = {} if ident is None else {"collective_id": ident, "has_side_effects": True}
    return pl.pallas_call(
        kernel,
        grid=(steps,),
        in_specs=list(ins),
        out_specs=list(specs),
        out_shape=list(shapes),
        scratch_shapes=list(scratch),
        compiler_params=pltpu.CompilerParams(
            vmem_limit_bytes=VMEM_LIMIT, dimension_semantics=("arbitrary",), **remote
        ),
        cost_estimate=pl.CostEstimate(flops=flops, bytes_accessed=moved, transcendentals=0),
    )(*args)


DEPTH = 4


def gathered(groups, split=1):
    shapes = [(len(group), *group[0].shape) for group in groups]
    outs = [
        (pl.BlockSpec(memory_space=pl.ANY), shape_of((shape[0], DEPTH, *shape[1:]), BF16)) for shape in shapes
    ]
    scratch = [pltpu.VMEM(shape, BF16) for shape in shapes]
    specs = [full(shard.shape) for group in groups for shard in group]
    return specs, outs, [*scratch, *Gather.semaphores(len(groups) * split, DEPTH)] if groups else []


def flatten(groups):
    return [shard for group in groups for shard in group]


TOKEN_ROWS = 8
IMAGE_ROWS = 16


def square(width, index):
    return pl.BlockSpec((width, width), lambda i: (index, 0), pipeline_mode=pl.Buffered(1))


def run_prep(region, picture, wimage, shards):
    patch_count, rows, vision = region.shape
    padded = -(-patch_count // 16) * 16
    embed = wimage.shape[1]
    specs, outs, sems = gathered(shards)
    return call(
        partial(prep_kernel, len(shards), len(flatten(shards))),
        vision // 128,
        [pl.BlockSpec((patch_count, rows, 128), lambda i: (0, 0, i)), full(picture.shape), full(wimage.shape), *specs],
        [
            (pl.BlockSpec((rows, padded, 128), lambda i: (0, 0, i)), shape_of((rows, padded, vision), BF16)),
            (fixed((rows, embed)), shape_of((rows, embed), BF16)),
            *outs,
        ],
        (region, picture, wimage, *flatten(shards)),
        scratch=[pltpu.VMEM((patch_count * rows, 128), F32), *sems],
        moved=4 * rows * padded * vision,
        ident=1 if shards else None,
    )


def run_self_forward(length, dp_size, bound, tok, weights, embed, shards):
    tokens, width = tok.shape
    block = TOKEN_ROWS * length
    specs, outs, sems = gathered(shards)
    if shards:
        shape = shape_of((dp_size * embed.shape[0], embed.shape[1]), BF16)
        outs = [*outs, (pl.BlockSpec(memory_space=pl.ANY), shape)]
        sems = [DMA, DMA((dp_size,)), DMA((dp_size,)), *sems]
    return call(
        partial(self_forward_kernel, length, len(shards), len(flatten(shards))),
        tokens // block,
        [SMEM, rows_of(block, width), full((2 * width, width)), square(width, 0), square(width, 1), full(embed.shape), *specs],
        [
            (rows_of(block, 3 * width), shape_of((tokens, 3 * width), BF16)),
            (rows_of(block, width), shape_of((tokens, width), BF16)),
            (rows_of(block, width), shape_of((tokens, width), F32)),
            (rows_of(block, 1), shape_of((tokens, 1), F32)),
            *outs,
        ],
        (bound, tok, weights[0], weights[1], weights[1], embed, *flatten(shards)),
        scratch=sems,
        flops=10 * tokens * width * width,
        moved=20 * tokens * width,
        ident=2 if shards else None,
    )


def probs_spec(width, length, padded):
    return pl.BlockSpec((TOKEN_ROWS, width // GROUP, padded, 4 * length), lambda i: (i, 0, 0, 0))


def run_cross_forward(length, patch_count, region, wkv, xhat1, norms, wcq, wout, shards):
    rows, padded, vision = region.shape
    tokens, width = xhat1.shape
    images = TOKEN_ROWS
    block = images * length
    specs, outs, sems = gathered(shards, split=2)
    return call(
        partial(cross_forward_kernel, patch_count, length, len(shards), len(flatten(shards))),
        rows // images,
        [
            pl.BlockSpec((images, padded, vision), lambda i: (i, 0, 0)), full((2 * width, vision)),
            rows_of(block, width), full(norms.shape), square(width, 0), square(width, 1), *specs,
        ],
        [
            (
                pl.BlockSpec((images, padded, 2 * width), lambda i: (i, 0, 0)),
                shape_of((rows, padded, 2 * width), BF16),
            ),
            (rows_of(block, width), shape_of((tokens, width), BF16)),
            (rows_of(block, width), shape_of((tokens, width), BF16)),
            (rows_of(block, width), shape_of((tokens, width), F32)),
            (rows_of(block, 1), shape_of((tokens, 1), F32)),
            (probs_spec(width, length, padded), shape_of((rows, width // GROUP, padded, 4 * length), BF16)),
            *outs,
        ],
        (region, wkv, xhat1, norms, wcq, wout, *flatten(shards)),
        scratch=sems,
        flops=4 * rows * padded * width * vision,
        moved=2 * rows * padded * (vision + 2 * width),
        ident=3 if shards else None,
    )


def run_feed_forward(
    length, bound, which, temp, xhat2, rstd2, norms, ffn, adjoint, target, image_all, wtext
):
    tokens, width = xhat2.shape
    hidden_units = ffn.shape[0] // 2
    embed = wtext.shape[1]
    block = IMAGE_ROWS * length
    captions = 2 * IMAGE_ROWS
    ff_own = hidden_units // 4
    return call(
        partial(feed_forward_kernel, length),
        tokens // block,
        [
            SMEM, SMEM, SMEM, rows_of(block, width), rows_of(block, 1), full(norms.shape),
            full((hidden_units, width)),
            pl.BlockSpec((hidden_units, width), lambda i: (1, 0), pipeline_mode=pl.Buffered(1)),
            rows_of(block, width), rows_of(captions, 1),
            full(image_all.shape), full((width, embed)),
        ],
        [
            (rows_of(block, width), shape_of((tokens, width), BF16)),
            (rows_of(captions, 1), shape_of(target.shape, F32)),
            (rows_of(captions, embed + 128), shape_of((target.shape[0], embed + 128), F32)),
            (rows_of(block, width), shape_of((tokens, width), F32)),
            (fixed((width, ff_own)), shape_of((width, ff_own), BF16)),
            (fixed((ff_own, width)), shape_of((ff_own, width), BF16)),
            (fixed((1, width)), shape_of((1, width), F32)),
            (fixed((1, width)), shape_of((1, width), F32)),
            (fixed((1, width)), shape_of((1, width), F32)),
            (fixed((1, width)), shape_of((1, width), F32)),
            (fixed((width, embed)), shape_of((width, embed), BF16)),
            (fixed((1, 1)), shape_of((1, 1), F32)),
        ],
        (
            bound, which, temp, xhat2, rstd2, norms, ffn, ffn, adjoint, target, image_all,
            wtext,
        ),
        scratch=[
            pltpu.VMEM((block, hidden_units), BF16),
            pltpu.VMEM((block, hidden_units), F32),
            pltpu.VMEM((block, width), F32),
            pltpu.VMEM((block, width), F32),
            pltpu.VMEM((captions, width), F32),
            pltpu.VMEM((width, ff_own), F32),
            pltpu.VMEM((ff_own, width), F32),
            pltpu.VMEM((width, embed), F32),
        ],
        flops=10 * tokens * width * hidden_units,
        moved=20 * tokens * width,
    )


def run_cross_backward(length, patch_count, which, region, kv, cq, ctx2, xhat1, rstd1, norms, dr2, wkv, wcq, wout, probs):
    rows, padded, vision = region.shape
    tokens, width = cq.shape
    images = TOKEN_ROWS
    block = images * length
    own = width // 4
    stored = -(-patch_count // 8) * 8
    return call(
        partial(cross_backward_kernel, patch_count, length),
        rows // images,
        [
            SMEM,
            pl.BlockSpec((images, padded, vision), lambda i: (i, 0, 0)),
            pl.BlockSpec((images, padded, 2 * width), lambda i: (i, 0, 0)),
            rows_of(block, width), rows_of(block, width), rows_of(block, width), rows_of(block, 1), full(norms.shape),
            rows_of(block, width), full((2 * width, vision)), square(width, 1), square(width, 0),
            probs_spec(width, length, padded),
        ],
        [
            (pl.BlockSpec(memory_space=pl.ANY), shape_of((patch_count, rows, vision), BF16)),
            (rows_of(block, width), shape_of((tokens, width), F32)),
            (fixed((2 * own, vision)), shape_of((2 * own, vision), BF16)),
            (fixed((2 * own, width)), shape_of((2 * own, width), BF16)),
            (fixed((1, width)), shape_of((1, width), F32)),
            (fixed((1, width)), shape_of((1, width), F32)),
        ],
        (which, region, kv, cq, ctx2, xhat1, rstd1, norms, dr2, wkv, wout, wcq, probs),
        scratch=[
            pltpu.VMEM((block, width), BF16),
            pltpu.VMEM((block, width), BF16),
            pltpu.VMEM((images, padded, 2 * width), BF16),
            pltpu.VMEM((vision // 128, stored * IMAGE_ROWS, 128), F32),
            pltpu.VMEM((2, patch_count // 5, IMAGE_ROWS, vision), BF16),
            pltpu.VMEM((2, GROUP, vision), F32),
            pltpu.VMEM((GROUP, width), F32),
            pltpu.VMEM((GROUP, width), F32),
            DMA((2,)),
        ],
        flops=6 * rows * padded * width * vision,
        moved=2 * rows * padded * 2 * (vision + width),
    )


def run_self_backward(length, dp_size, bound, tok, qkv, ctx1, dr1, weights, others):
    tokens, width = tok.shape
    block = TOKEN_ROWS * length
    steps = tokens // block
    last = shape_of((width, width), BF16)

    def early(lanes):
        return pl.BlockSpec((block, lanes), lambda i: (jnp.minimum(i, steps - 1), 0))

    extra, outs, scratch = [], [], []
    if others:
        dkv, dqo, _, pack, picture, wimage, *vectors = others
        image = shape_of(wimage.shape, BF16)
        small = shape_of((128, width), BF16)
        half = (width // 2, width)
        shapes = [shape_of(dkv.shape, BF16), shape_of(dqo.shape, BF16), small, image]
        extra = [full(dkv.shape), full(dqo.shape), SMEM, *(full(other.shape) for other in others[3:])]
        outs = [*((fixed(shape.shape), shape) for shape in shapes), (fixed(picture.shape), shape_of(picture.shape, F32))]
        scratch = [
            pltpu.VMEM((dp_size, *pack.shape), F32), pltpu.VMEM(image.shape, BF16), pltpu.VMEM(small.shape, BF16),
            DMA((dp_size,)), DMA((dp_size,)),
            *(spot for shape in (*(shape.shape for shape in shapes), half, half) for spot in Reduce.scratch(shape)),
        ]
    return call(
        partial(self_backward_kernel, length, bool(others)),
        2 * steps,
        [
            SMEM, early(width), early(3 * width), early(width),
            pl.BlockSpec((block, width), lambda i: (lax.rem(i, steps), 0)),
            full((2 * width, width)), square(width, 0), square(width, 1), *extra,
        ],
        [
            (
                pl.BlockSpec((block, width), lambda i: (jnp.maximum(i - steps, 0), 0)),
                shape_of((tokens, width), F32),
            ),
            (fixed(last.shape), last),
            *outs,
        ],
        (bound, tok, qkv, ctx1, dr1, weights[0], weights[1], weights[1], *others),
        scratch=[
            pltpu.VMEM((block, width), BF16),
            pltpu.VMEM((tokens, 3 * width), BF16),
            pltpu.VMEM((3, GROUP, width), F32),
            pltpu.VMEM((GROUP, width), F32),
            pltpu.VMEM(last.shape, BF16),
            *scratch,
        ],
        flops=10 * tokens * width * width,
        moved=20 * tokens * width,
        ident=4 if others else None,
    )


def run_widen(last, dkv, dqo, dimage, dup, ddown, dtext, small):
    width = last.shape[1]
    own = width // 4
    shapes = [(own, width)] * 6 + [(own, dkv.shape[1])] * 2
    shapes += [dup.shape, ddown.shape, dtext.shape, dimage.shape] + [(width,)] * 6 + [(1, 1)]
    args = (last, dkv, dqo, dimage, dup, ddown, dtext, small)
    return call(
        partial(widen_kernel, own),
        1,
        [fixed(array.shape) for array in args],
        [(fixed(shape), shape_of(shape, F32)) for shape in shapes],
        args,
        moved=20 * width * width,
    )


def body(
    dp_size,
    word_features,
    sentence_numbering,
    region_features,
    picture_global_feature,
    matched_picture,
    sharpness_array,
    incoming_adjoint,
    intra_asking_map,
    intra_lookup_map,
    intra_content_map,
    intra_attend_exit_map,
    visual_asking_map,
    visual_lookup_map,
    visual_content_map,
    visual_attend_exit_map,
    mlp_widening_factor,
    mlp_narrowing_factor,
    initial_standardize_scale,
    initial_standardize_offset,
    middle_standardize_scale,
    middle_standardize_offset,
    final_standardize_scale,
    final_standardize_offset,
    sentence_mapping_factor,
    picture_mapping_factor,
):
    rows, length = sentence_numbering.shape
    tokens, width = word_features.shape
    patch_count, vision = region_features.shape[1:]
    embed = sentence_mapping_factor.shape[1]
    hidden_units = mlp_widening_factor.shape[1] * 4
    own = width // 4
    which = lax.axis_index("mp").astype(jnp.int32).reshape(1)
    bound = (length - jnp.sum(sentence_numbering, axis=1)).astype(jnp.int32)
    target = matched_picture.reshape(-1, 1)
    norms = jnp.stack([
        initial_standardize_scale, initial_standardize_offset, middle_standardize_scale,
        middle_standardize_offset, final_standardize_scale, final_standardize_offset,
    ])

    selves = [(intra_asking_map.T, intra_lookup_map.T), (intra_content_map.T, intra_attend_exit_map)]
    crosses = (visual_asking_map.T, visual_attend_exit_map)
    wides = (visual_lookup_map.T, visual_content_map.T)
    ffns = (mlp_widening_factor.T, mlp_narrowing_factor)
    region = jnp.transpose(region_features, (1, 0, 2))
    local = dp_size == 8 and lax.axis_size("mp") == DEPTH

    def each(*shards):
        return list(shards) if local else []

    region, image_own, *found = run_prep(region, picture_global_feature, picture_mapping_factor, each(*selves))
    selves = found if local else [lax.all_gather(jnp.stack(pair), "mp", axis=1) for pair in selves]
    selves = [pair.reshape(-1, width) for pair in selves]
    qkv, ctx1, xhat1, rstd1, *found = run_self_forward(
        length, dp_size, bound, word_features, selves, image_own, each(crosses, wides)
    )
    if local:
        crosses, wides, image_all = found
    else:
        crosses, wides = (lax.all_gather(jnp.stack(group), "mp", axis=1) for group in (crosses, wides))
        image_all = lax.all_gather(image_own, "dp", axis=0, tiled=True)
    crosses = crosses.reshape(-1, width)
    wkv = wides.reshape(-1, vision)
    kv, cq, ctx2, xhat2, rstd2, probs, *found = run_cross_forward(
        length, patch_count, region, wkv, xhat1, norms, crosses, crosses, each(ffns)
    )
    ffns = (found[0] if local else lax.all_gather(jnp.stack(ffns), "mp", axis=1)).reshape(-1, width)
    (
        block_exit, loss, pack, dr2, dup, ddown, dgain2, dshift2, dgain3, dshift3, dtext, dtemp,
    ) = run_feed_forward(
        length, bound, which, sharpness_array, xhat2, rstd2, norms, ffns, incoming_adjoint, target, image_all,
        sentence_mapping_factor,
    )

    dp_sum = lambda grad: lax.psum(grad, "dp")
    dup, ddown, dtext = dp_sum((dup, ddown, dtext))
    dregion, dr1, dkv, dqo, dgain1, dshift1 = run_cross_backward(
        length, patch_count, which, region, kv, cq, ctx2, xhat1, rstd1, norms, dr2, wkv, crosses, crosses, probs
    )
    vectors = (dgain1, dshift1, dgain2, dshift2, dgain3, dshift3, dtemp)
    pictures = (picture_global_feature, picture_mapping_factor)
    dtok, last, *found = run_self_backward(
        length, dp_size, bound, word_features, qkv, ctx1, dr1, selves,
        each(dkv, dqo, sharpness_array, pack, *pictures, *vectors),
    )
    if local:
        dkv, dqo, small, dimage, dpicture = found
    else:
        pack_all = lax.all_gather(pack, "dp", axis=0, tiled=True)
        first = (lax.axis_index("dp") * rows).astype(jnp.int32).reshape(1)
        dpicture, dimage = call(
            image_backward_kernel,
            1,
            [SMEM, SMEM, *(full(array.shape) for array in (*pictures, pack_all))],
            [
                (fixed((rows, vision)), shape_of((rows, vision), F32)),
                (fixed((vision, embed)), shape_of((vision, embed), BF16)),
            ],
            (first, sharpness_array, *pictures, pack_all),
        )
        lines = [*vectors[:6], jnp.broadcast_to(dtemp, (1, width)), jnp.zeros((9, width), F32)]
        small = jnp.concatenate(lines).astype(BF16)
        dkv, dqo, dimage, last, small = dp_sum((dkv, dqo, dimage, last, small))
    dq, dk, dv, dso, dcq, dco, dck, dcv, dup, ddown, dtext, dimage, *vectors = run_widen(
        last, dkv, dqo, dimage, dup, ddown, dtext, small
    )
    return (
        loss.reshape(rows, 2),
        block_exit,
        dtok,
        jnp.transpose(dregion, (1, 0, 2)),
        dpicture,
        vectors[6].reshape(1),
        dq.T,
        dk.T,
        dv.T,
        dso,
        dcq.T,
        dck.T,
        dcv.T,
        dco,
        dup,
        ddown,
        *vectors[:6],
        dtext,
        dimage,
    )


def solution(mesh):
    rows = P("dp", None)
    by_column = P(None, "mp")
    by_row = P("mp", None)
    in_specs = (
        rows, rows, P("dp", None, None), rows, rows, P(), rows,
        by_column, by_column, by_column, by_row, by_column, by_column, by_column, by_row, by_column, by_row,
        P(), P(), P(), P(), P(), P(), P(), P(),
    )
    out_specs = (
        rows, rows, rows, P("dp", None, None), rows, P(),
        by_column, by_column, by_column, by_row, by_column, by_column, by_column, by_row, by_column, by_row,
        P(), P(), P(), P(), P(), P(), P(), P(),
    )
    return jax.shard_map(
        partial(body, mesh.shape["dp"]), mesh=mesh, in_specs=in_specs, out_specs=out_specs, check_vma=False
    )
```

```python
from functools import partial

import jax
import jax.numpy as jnp
from jax import lax
from jax.experimental import pallas as pl
from jax.experimental.pallas import tpu as pltpu
from jax.sharding import PartitionSpec as P

HEAD = 64
GROUP = 4 * HEAD
LN_EPS = 1e-06
NORM_EPS = 1e-06
BIG_NEG = -1000000000.0
F32 = jnp.float32
BF16 = jnp.bfloat16
VMEM_LIMIT = 60 * 2**20


def dot_nn(left, right):
    return lax.dot_general(left, right, (((1,), (0,)), ((), ())), preferred_element_type=F32)


def dot_nt(left, right):
    return lax.dot_general(left, right, (((1,), (1,)), ((), ())), preferred_element_type=F32)


def dot_tn(left, right):
    return lax.dot_general(left, right, (((0,), (0,)), ((), ())), preferred_element_type=F32)


def normalize(inputs):
    center = inputs - jnp.mean(inputs, axis=-1, keepdims=True)
    rstd = lax.rsqrt(jnp.mean(center * center, axis=-1, keepdims=True) + LN_EPS)
    return center * rstd, rstd


def norm_pull(grad, xhat, rstd, gain):
    scaled = grad * gain
    first = jnp.mean(scaled, axis=-1, keepdims=True)
    second = jnp.mean(scaled * xhat, axis=-1, keepdims=True)
    grad_in = rstd * (scaled - first - xhat * second)
    return grad_in, jnp.sum(grad * xhat, axis=0, keepdims=True), jnp.sum(grad, axis=0, keepdims=True)


def unit_pull(raw, grad):
    scale = lax.rsqrt(jnp.sum(raw * raw, axis=-1, keepdims=True) + NORM_EPS)
    inner = jnp.sum(grad * raw, axis=-1, keepdims=True)
    return scale * grad - raw * (scale * scale * scale * inner)


MESH = pl.DeviceIdType.MESH
DMA = pltpu.SemaphoreType.DMA


class Gather:
    def __init__(self, shards, outs, refs, split=1):
        count = len(outs)
        self.units = [(array, piece) for array in range(count) for piece in range(split)]
        self.split = split
        self.ins, self.outs, self.shards, sems = refs[:count], outs, shards, refs[count:]
        self.local, self.up, self.down, self.across, self.below, self.above, self.near, self.out, self.back = sems
        self.dp, self.z = lax.axis_index("dp"), lax.axis_index("mp")
        dp, z = self.dp, self.z
        self.core, self.x, self.y = dp % 2, dp // 2 % 2, dp // 4
        self.depth = outs[0].shape[1]
        self.color = (self.x + self.y) % 2
        east, north = 2 - 4 * self.x, 4 - 8 * self.y
        self.peers = [(dp + east, z), (dp + north, z), (dp + east + north, z)]
        self.twin = (dp + 1 - 2 * self.core, z)

    @staticmethod
    def semaphores(count, depth):
        grid = (count, depth)
        return [DMA((count,)), DMA(grid), DMA(grid), DMA((3, *grid)), DMA(grid), DMA(grid), DMA((3, *grid)), DMA(grid), DMA(grid)]

    def enter(self, everyone=0):
        barrier = pltpu.get_barrier_semaphore()
        peers = [*self.peers, self.twin]
        if everyone:
            peers = [((self.dp + k) % everyone, self.z) for k in range(1, everyone)]
        for peer in peers:
            pl.semaphore_signal(barrier, inc=1, device_id=peer, device_id_type=MESH)
        for step in (-1, 1):

            @pl.when(self.inside(self.z + step))
            def _(step=step):
                pl.semaphore_signal(barrier, inc=1, device_id=(self.dp, self.z + step), device_id_type=MESH)

        ends = (self.z > 0).astype(jnp.int32) + (self.z < self.depth - 1).astype(jnp.int32)
        pl.semaphore_wait(barrier, len(peers) + ends)

    def inside(self, z):
        return (z >= 0) & (z < self.depth)

    def tall(self, index):
        return self.ins[self.units[index][0]].shape[1] // self.split

    def part(self, index, source, first, size, core=None):
        array, piece = self.units[index]
        mats = self.ins[array].shape[0] // 2
        core = self.core if core is None else core
        first = pl.multiple_of(piece * self.tall(index) + first, 16)
        return self.outs[array].at[pl.ds(core * mats, mats), source, pl.ds(first, size), :]

    def copy(self, src, dst, send, recv, to):
        return pltpu.make_async_remote_copy(
            src_ref=src, dst_ref=dst, send_sem=send, recv_sem=recv, device_id=to, device_id_type=MESH
        )

    def span(self, index):
        tall = self.tall(index)
        return self.color * (tall // 2) + self.y * (tall // 6), tall // 3

    def hop(self, index, source, step):
        spot = self.part(index, source, *self.span(index))
        send, recv = (self.up, self.below) if step > 0 else (self.down, self.above)
        return self.copy(spot, spot, send.at[index, source], recv.at[index, source], (self.dp, self.z + step))

    def first_hop(self, index, step):
        first, size = self.span(index)
        array, piece = self.units[index]
        mats = self.ins[array].shape[0] // 2
        begin = pl.multiple_of(piece * self.tall(index) + first, 16)
        src = self.ins[array].at[pl.ds(self.core * mats, mats), pl.ds(begin, size), :]
        send, recv = (self.up, self.below) if step > 0 else (self.down, self.above)
        spot = self.part(index, self.z, first, size)
        return self.copy(src, spot, send.at[index, self.z], recv.at[index, self.z], (self.dp, self.z + step))

    def side(self, index, source, which, inward=False):
        tall = self.tall(index)
        color, y = self.color, self.y
        if inward:
            color, y = (1 - color, y) if which == 0 else (1 - color, 1 - y) if which == 1 else (color, 1 - y)
        pace, size = ((tall // 4, tall // 4), (tall // 4, tall // 4), (tall // 3, tall // 6))[which]
        spot = self.part(index, source, color * (tall // 2) + y * pace, size)
        sems = self.across.at[which, index, source], self.near.at[which, index, source]
        return self.copy(spot, spot, *sems, self.peers[which])

    def pass_on(self, index, source, inward=False):
        core = 1 - self.core if inward else self.core
        spot = self.part(index, source, 0, self.tall(index), core)
        return self.copy(spot, spot, self.out.at[index, source], self.back.at[index, source], self.twin)

    def keep(self, index):
        array, piece = self.units[index]
        rows = pl.ds(piece * self.tall(index), self.tall(index))
        spot = self.outs[array].at[:, self.z, rows, :]
        return pltpu.make_async_copy(self.ins[array].at[:, rows, :], spot, self.local.at[index])

    def start(self, everyone=0):
        count = 0
        for stack in self.ins:
            for index in range(stack.shape[0]):
                stack[index] = self.shards[count][...]
                count += 1
        self.enter(everyone)
        for index in range(len(self.units)):
            for step in (1, -1):

                @pl.when(self.inside(self.z + step))
                def _(index=index, step=step):
                    self.first_hop(index, step).start()

            self.keep(index).start()

    def each(self, distance, what, only=None):
        for index in range(len(self.units)) if only is None else (only,):
            for step in (1, -1):
                source = self.z - step * distance

                @pl.when(self.inside(source))
                def _(index=index, step=step, source=source):
                    what(index, step, source)

    def pull(self, distance, only=None):
        def what(index, step, source):
            self.hop(index, source, step).wait_recv()

            @pl.when(self.inside(self.z + step))
            def _():
                self.hop(index, source, step).start()

            for which in range(3):
                self.side(index, source, which).start()

        self.each(distance, what, only)

    def pair(self, distance):
        def what(index, step, source):
            for which in range(3):
                self.side(index, source, which, inward=True).wait_recv()
            self.pass_on(index, source).start()

        self.each(distance, what)

    def finish(self):
        def what(index, step, source):
            self.pass_on(index, source, inward=True).wait_recv()
            self.pass_on(index, source).wait_send()
            for which in range(3):
                self.side(index, source, which).wait_send()

            @pl.when(self.inside(self.z + step))
            def _():
                self.hop(index, source, step).wait_send()

        for distance in range(1, self.depth):
            self.each(distance, what)
        for index in range(len(self.units)):
            for step in (1, -1):

                @pl.when(self.inside(self.z + step))
                def _(index=index, step=step):
                    self.first_hop(index, step).wait_send()

            self.keep(index).wait()


class Reduce:
    def __init__(self, src, done, half, part, quarter, twin_sems, plane_sems):
        self.src, self.done, self.half, self.part, self.quarter = src, done, half, part, quarter
        self.twin_sems, self.plane_sems = twin_sems, plane_sems
        dp, z = lax.axis_index("dp"), lax.axis_index("mp")
        self.core, self.chip = dp % 2, dp // 2
        x, y = self.chip % 2, self.chip // 2
        east, north = 2 - 4 * x, 4 - 8 * y
        self.shifts = (east, north, east + north)
        self.peers = [(dp + shift, z) for shift in self.shifts]
        self.twin = (dp + 1 - 2 * self.core, z)
        self.tall = src.shape[0]

    @staticmethod
    def scratch(shape):
        rows, columns = shape
        sizes = ((rows, columns), (rows // 2, columns), (rows // 2, columns), (3, rows // 8, columns))
        return [*(pltpu.VMEM(size, BF16) for size in sizes), DMA((4,)), DMA((4, 3))]

    def enter(self):
        barrier = pltpu.get_barrier_semaphore()
        for peer in [*self.peers, self.twin]:
            pl.semaphore_signal(barrier, inc=1, device_id=peer, device_id_type=MESH)
        pl.semaphore_wait(barrier, 4)

    def copy(self, src, dst, send, recv, to):
        return pltpu.make_async_remote_copy(
            src_ref=src, dst_ref=dst, send_sem=send, recv_sem=recv, device_id=to, device_id_type=MESH
        )

    def mine(self, core):
        return pl.ds(pl.multiple_of(core * (self.tall // 2), 16), self.tall // 2)

    def slot(self, chip, core=None):
        first = chip * (self.tall // 8)
        if core is not None:
            first = first + core * (self.tall // 2)
        return pl.ds(pl.multiple_of(first, 16), self.tall // 8)

    def to_twin(self):
        sems = self.twin_sems.at[0], self.twin_sems.at[1]
        return self.copy(self.src.at[self.mine(1 - self.core)], self.half, *sems, self.twin)

    def scatter(self, which):
        chip = self.chip + self.shifts[which] // 2
        sems = self.plane_sems.at[0, which], self.plane_sems.at[1, which]
        return self.copy(self.part.at[self.slot(chip)], self.quarter.at[which], *sems, self.peers[which])

    def spread(self, which, chip):
        spot = self.done.at[self.slot(chip, self.core)]
        sems = self.plane_sems.at[2, which], self.plane_sems.at[3, which]
        return self.copy(spot, spot, *sems, self.peers[which])

    def back(self, core):
        spot = self.done.at[self.mine(core)]
        return self.copy(spot, spot, self.twin_sems.at[2], self.twin_sems.at[3], self.twin)

    def stage(self, number):
        if number == 1:
            self.to_twin().start()
        elif number == 2:
            self.to_twin().wait_recv()
            total = self.src[self.mine(self.core), :].astype(F32) + self.half[...].astype(F32)
            self.part[...] = total.astype(BF16)
            for which in range(3):
                self.scatter(which).start()
        elif number == 3:
            total = self.part[self.slot(self.chip), :].astype(F32)
            for which in range(3):
                self.scatter(which).wait_recv()
                total = total + self.quarter[which].astype(F32)
            self.done[self.slot(self.chip, self.core), :] = total.astype(BF16)
            for which in range(3):
                self.spread(which, self.chip).start()
        elif number == 4:
            for which in range(3):
                self.spread(which, self.chip + self.shifts[which] // 2).wait_recv()
            self.back(self.core).start()
        else:
            self.back(1 - self.core).wait_recv()
            self.to_twin().wait_send()
            for which in range(3):
                self.scatter(which).wait_send()
                self.spread(which, self.chip).wait_send()
            self.back(self.core).wait_send()


ARRIVALS = ((1, 0), (1, 1), (2, 0), (2, 1), (3, 0), (3, 1))


def spread_heads(tensor):
    count = tensor.shape[0]
    left = lax.broadcasted_iota(jnp.int32, (count, 2 * HEAD), 1) < HEAD
    low, high = tensor[:, : 2 * HEAD], tensor[:, 2 * HEAD :]
    zero = jnp.zeros_like(low)
    blank = jnp.zeros((2 * count, 2 * HEAD), tensor.dtype)
    near = jnp.concatenate([jnp.where(left, low, zero), jnp.where(left, zero, low), blank], axis=0)
    far = jnp.concatenate([blank, jnp.where(left, high, zero), jnp.where(left, zero, high)], axis=0)
    return jnp.concatenate([near, far], axis=1).astype(BF16)


def collect_heads(stacked, count):
    left = lax.broadcasted_iota(jnp.int32, (count, 2 * HEAD), 1) < HEAD
    low = jnp.where(left, stacked[:count, : 2 * HEAD], stacked[count : 2 * count, : 2 * HEAD])
    high = jnp.where(
        left, stacked[2 * count : 3 * count, 2 * HEAD :], stacked[3 * count :, 2 * HEAD :]
    )
    return jnp.concatenate([low, high], axis=1)


def attend_probs(query_blocks, keys, keep):
    scores = dot_nt(keys, query_blocks)
    scores = jnp.where(keep, scores, BIG_NEG)
    top = jnp.max(scores, axis=0, keepdims=True)
    shifted = jnp.exp(scores - top)
    total = jnp.sum(shifted, axis=0, keepdims=True)
    return shifted * (1.0 / total)


def attend_forward(query, keys, values, keep):
    probs = attend_probs(spread_heads(query), keys, keep).astype(BF16)
    return collect_heads(dot_tn(probs, values), query.shape[0]), probs


def split_heads(tensor):
    left = lax.broadcasted_iota(jnp.int32, tensor.shape, 1) < HEAD
    zero = jnp.zeros_like(tensor)
    return jnp.concatenate([jnp.where(left, tensor, zero), jnp.where(left, zero, tensor)], axis=0).astype(BF16)


def attend_short(query, keys, values, keep):
    count = query.shape[0]
    left = lax.broadcasted_iota(jnp.int32, (count, 2 * HEAD), 1) < HEAD
    out = []
    for half in range(2):
        at = slice(half * 2 * HEAD, (half + 1) * 2 * HEAD)
        probs = attend_probs(split_heads(query[:, at]), keys[:, at], keep[:, : 2 * count])
        stacked = dot_nn(jnp.transpose(probs.astype(BF16)), values[:, at])
        out.append(jnp.where(left, stacked[:count], stacked[count:]))
    return jnp.concatenate(out, axis=1)


def attend_backward(query, keys, values, keep, grad_context, kept=None):
    query_blocks = spread_heads(query)
    grad_blocks = spread_heads(grad_context)
    probs = attend_probs(query_blocks, keys, keep) if kept is None else kept.astype(F32)
    grad_probs = dot_nt(values, grad_blocks)
    inner = jnp.sum(grad_probs * probs, axis=0, keepdims=True)
    grad_scores = (probs * (grad_probs - inner)).astype(BF16)
    grad_values = dot_nn(probs.astype(BF16) if kept is None else kept, grad_blocks)
    grad_keys = dot_nn(grad_scores, query_blocks)
    grad_query = collect_heads(dot_tn(grad_scores, keys), query.shape[0]) * 0.125
    return grad_query, grad_keys, grad_values


def row_keep(bound, length):
    key = lax.broadcasted_iota(jnp.int32, (length, 4 * length), 0)
    query = lax.broadcasted_iota(jnp.int32, (length, 4 * length), 1) % length
    return (key >= bound) == (query >= bound)


def window(which, width):
    return pl.ds(pl.multiple_of(which * 3 // 2 * (width // 2), width // 2), width)


def own_rows(acc, which, own):
    odd = which % 2 == 1
    return jnp.where(odd, acc[acc.shape[0] - own :], acc[:own])


def prep_kernel(gathers, count, *refs):
    region_ref, picture_ref, weight_ref = refs[:3]
    shards, refs = refs[3 : 3 + count], refs[3 + count :]
    moved_ref, embed_ref = refs[:2]
    whole, refs = refs[2 : 2 + gathers], refs[2 + gathers :]
    flat_ref = refs[0]
    patch_count, images, lanes = region_ref.shape
    padded = moved_ref.shape[1]
    full_tiles = patch_count // 8 * 8
    step = pl.program_id(0)
    steps = pl.num_programs(0)
    gather = Gather(shards, whole, refs[1:]) if gathers else None

    @pl.when(step == 0)
    def _():
        if gather:
            gather.start()
        raw = dot_nn(picture_ref[...], weight_ref[...])
        scale = lax.rsqrt(jnp.sum(raw * raw, axis=-1, keepdims=True) + NORM_EPS)
        embed_ref[...] = (raw * scale).astype(BF16)

    flat_ref[...] = region_ref[...].reshape(patch_count * images, lanes).astype(F32)
    row = lax.broadcasted_iota(jnp.int32, (padded - full_tiles, lanes), 0)
    for image in range(images):
        main = flat_ref[pl.ds(image, full_tiles, stride=images), :]
        moved_ref[image, 0:full_tiles, :] = main.astype(BF16)
        last = flat_ref[pl.ds(full_tiles * images + image, 1), :]
        moved_ref[image, full_tiles:padded, :] = jnp.where(row == 0, last, 0.0).astype(BF16)

    if gather:

        for place, arrival in enumerate(ARRIVALS):

            @pl.when(step == place + 1)
            def _(arrival=arrival):
                gather.pull(*arrival)

        @pl.when(step == steps - 1)
        def _():
            gather.pair(1)
            gather.pair(2)
            gather.pair(3)
            gather.finish()


def self_forward_kernel(length, gathers, count, *refs):
    bound_ref, tok_ref, wqk_ref, wv_ref, wout_ref, embed_ref = refs[:6]
    shards, refs = refs[6 : 6 + count], refs[6 + count :]
    qkv_ref, ctx_ref, xhat_ref, rstd_ref = refs[:4]
    whole, refs = refs[4 : 4 + gathers], refs[4 + gathers :]
    width = tok_ref.shape[1]
    rows = tok_ref.shape[0] // length
    step = pl.program_id(0)
    steps = pl.num_programs(0)
    if gathers:
        images_ref, embed_local, embed_send, embed_recv = refs[:4]
        gather = Gather(shards, whole, refs[4:])
        dp, z = lax.axis_index("dp"), lax.axis_index("mp")
        dp_size = images_ref.shape[0] // embed_ref.shape[0]
        held = embed_ref.shape[0]

        def embed_copy(k, owner, to):
            spot = images_ref.at[pl.ds(pl.multiple_of(owner * held, 16), held), :]
            return pltpu.make_async_remote_copy(
                src_ref=embed_ref, dst_ref=spot, send_sem=embed_send.at[k], recv_sem=embed_recv.at[k],
                device_id=(to, z), device_id_type=MESH,
            )

        def embed_own():
            spot = images_ref.at[pl.ds(pl.multiple_of(dp * held, 16), held), :]
            return pltpu.make_async_copy(embed_ref, spot, embed_local)

        @pl.when(step == 0)
        def _():
            gather.start(everyone=dp_size)
            embed_own().start()
            for k in range(1, dp_size):
                embed_copy(k, dp, (dp + k) % dp_size).start()

        for distance in range(1, 4):

            @pl.when(step == distance)
            def _(distance=distance):
                gather.pull(distance, 1 if distance == 3 else None)

    tok = tok_ref[...]
    for part in range(3):
        weight = wv_ref[...] if part == 2 else wqk_ref[part * width : (part + 1) * width, :]
        proj = dot_nt(tok, weight)
        if part == 0:
            proj = proj * 0.125
        qkv_ref[:, part * width : (part + 1) * width] = proj.astype(BF16)

    if gathers:

        @pl.when(step == 2)
        def _():
            gather.pull(3, 0)

    def pair(index, carry):
        span = pl.ds(pl.multiple_of(index * 2 * length, 16), 2 * length)
        keeps = [row_keep(bound_ref[step * rows + 2 * index + j], length) for j in range(2)]
        for group in range(width // GROUP):
            q, k, v = (
                qkv_ref[span, part * width + group * GROUP : part * width + (group + 1) * GROUP].astype(F32)
                for part in range(3)
            )
            out = []
            for j in range(2):
                at = slice(j * length, (j + 1) * length)
                out.append(attend_short(q[at], k[at].astype(BF16), v[at].astype(BF16), keeps[j]))
            ctx_ref[span, group * GROUP : (group + 1) * GROUP] = jnp.concatenate(out, axis=0).astype(BF16)
        return carry

    lax.fori_loop(0, rows // 2, pair, 0, unroll=2)
    attn = dot_nn(ctx_ref[...], wout_ref[...])
    xhat, rstd = normalize(tok.astype(F32) + attn)
    xhat_ref[...] = xhat
    rstd_ref[...] = rstd

    if gathers:

        @pl.when(step == steps - 1)
        def _():
            for distance in range(1, 4):
                gather.pair(distance)
            for k in range(1, dp_size):
                embed_copy(k, (dp + dp_size - k) % dp_size, (dp + k) % dp_size).wait_recv()
                embed_copy(k, dp, (dp + k) % dp_size).wait_send()
            embed_own().wait()
            gather.finish()


def cross_forward_kernel(patch_count, length, gathers, count, *refs):
    region_ref, wkv_ref, xhat1_ref, norm_ref, wcq_ref, wout_ref = refs[:6]
    shards, refs = refs[6 : 6 + count], refs[6 + count :]
    kv_ref, cq_ref, ctx_ref, xhat_ref, rstd_ref, probs_ref = refs[:6]
    whole, refs = refs[6 : 6 + gathers], refs[6 + gathers :]
    images, padded, vision = region_ref.shape
    width = cq_ref.shape[1]
    step = pl.program_id(0)
    steps = pl.num_programs(0)
    gather = Gather(shards, whole, refs, split=2) if gathers else None
    if gathers:

        @pl.when(step == 0)
        def _():
            gather.start()

        for place, arrival in enumerate(ARRIVALS[1::2]):

            @pl.when(step == place + 1)
            def _(arrival=arrival):
                gather.pull(*arrival)

    hidden1 = xhat1_ref[...] * norm_ref[0:1] + norm_ref[1:2]
    cq_ref[...] = (dot_nt(hidden1.astype(BF16), wcq_ref[...]) * 0.125).astype(BF16)
    flat = region_ref[...].reshape(images * padded, vision)

    def chunk(index, carry):
        at = pl.ds(pl.multiple_of(index * 512, 512), 512)
        proj = dot_nt(flat, wkv_ref[at, :])
        kv_ref[:, :, at] = proj.astype(BF16).reshape(images, padded, 512)
        return carry

    lax.fori_loop(0, 2 * width // 512, chunk, 0, unroll=True)
    if gathers:
        for place, arrival in enumerate(ARRIVALS[::2]):

            @pl.when(step == place)
            def _(arrival=arrival):
                gather.pull(*arrival)

    keep = lax.broadcasted_iota(jnp.int32, (padded, 4 * length), 0) < patch_count

    def pair(index, carry):
        span = pl.ds(pl.multiple_of(index * 2 * length, 16), 2 * length)
        for group in range(width // GROUP):
            lanes = slice(group * GROUP, (group + 1) * GROUP)
            q = cq_ref[span, lanes].astype(F32)
            out = []
            for j in range(2):
                image = 2 * index + j
                keys = kv_ref[image, :, lanes]
                values = kv_ref[image, :, width + group * GROUP : width + (group + 1) * GROUP]
                context, probs = attend_forward(q[j * length : (j + 1) * length], keys, values, keep)
                out.append(context)
                probs_ref[image, group] = probs
            ctx_ref[span, lanes] = jnp.concatenate(out, axis=0).astype(BF16)
        return carry

    lax.fori_loop(0, images // 2, pair, 0, unroll=4)
    xhat, rstd = normalize(hidden1 + dot_nn(ctx_ref[...], wout_ref[...]))
    xhat_ref[...] = xhat
    rstd_ref[...] = rstd

    if gathers:

        @pl.when(step == steps - 1)
        def _():
            for distance in range(1, 4):
                gather.pair(distance)
            gather.finish()


def gelu_parts(inputs):
    cdf = 0.5 * (1.0 + lax.erf(inputs * 0.7071067811865476))
    density = jnp.exp(inputs * inputs * -0.5) * 0.3989422804014327
    return inputs * cdf, cdf + inputs * density


def feed_forward_kernel(
    length, bound_ref, which_ref, temp_ref, xhat2_ref, rstd2_ref, norm_ref,
    wup_ref, wdown_ref, adj_ref, target_ref, images_ref, wtext_ref,
    out_ref, loss_ref, pack_ref, dr2_ref, dup_ref, ddown_ref, dgain2_ref, dshift2_ref, dgain3_ref, dshift3_ref,
    dtext_ref, dtemp_ref,
    act_ref, slope_ref, final_ref, grad_ref, lead_ref, up_acc, down_acc, text_acc,
):
    step = pl.program_id(0)
    steps = pl.num_programs(0)
    tokens, width = xhat2_ref.shape
    hidden_units = wup_ref.shape[0]
    rows = tokens // length
    chunk = min(768, hidden_units)

    @pl.when(step == 0)
    def _():
        for ref in (dgain2_ref, dshift2_ref, dgain3_ref, dshift3_ref, dtemp_ref, up_acc, down_acc, text_acc):
            ref[...] = jnp.zeros_like(ref)

    xhat2 = xhat2_ref[...]
    hidden2 = xhat2 * norm_ref[2:3] + norm_ref[3:4]
    low = hidden2.astype(BF16)
    final_ref[...] = hidden2

    def forward(index, carry):
        at = pl.ds(pl.multiple_of(index * chunk, chunk), chunk)
        act, slope = gelu_parts(dot_nt(low, wup_ref[at, :]))
        act = act.astype(BF16)
        act_ref[:, at] = act
        slope_ref[:, at] = slope
        final_ref[...] += dot_nn(act, wdown_ref[at, :])
        return carry

    lax.fori_loop(0, hidden_units // chunk, forward, 0, unroll=True)
    xhat3, rstd3 = normalize(final_ref[...])
    final = xhat3 * norm_ref[4:5] + norm_ref[5:6]
    out_ref[...] = final.astype(BF16)
    final_ref[...] = final
    grad_ref[...] = adj_ref[...].astype(F32)

    for row in range(rows):
        lead_ref[pl.ds(2 * row, 1), :] = final_ref[pl.ds(row * length, 1), :]
        second = row * length + bound_ref[step * rows + row]
        lead_ref[pl.ds(2 * row + 1, 1), :] = final_ref[pl.ds(second, 1), :]
    lead = lead_ref[...].astype(BF16)
    raw = dot_nn(lead, wtext_ref[...])
    text = raw * lax.rsqrt(jnp.sum(raw * raw, axis=-1, keepdims=True) + NORM_EPS)
    text_low = text.astype(BF16)
    temp = temp_ref[0]
    logits = dot_nt(text_low, images_ref[...]) / temp
    top = jnp.max(logits, axis=1, keepdims=True)
    lse = top + jnp.log(jnp.sum(jnp.exp(logits - top), axis=1, keepdims=True))
    target = target_ref[...]
    hit = lax.broadcasted_iota(jnp.int32, logits.shape, 1) == target
    loss_ref[...] = lse - jnp.sum(jnp.where(hit, logits, 0.0), axis=1, keepdims=True)
    dlogits = jnp.exp(logits - lse) - hit.astype(F32)
    dtemp_ref[...] += -jnp.sum(jnp.sum(dlogits * logits, axis=1, keepdims=True), axis=0, keepdims=True) / temp
    embed = raw.shape[1]
    lane = lax.broadcasted_iota(jnp.int32, (2 * rows, 128), 1)
    pack_ref[:, :embed] = text_low.astype(F32)
    pack_ref[:, embed:] = jnp.where(lane == 0, lse, jnp.where(lane == 1, target.astype(F32), 0.0))
    dtext = dot_nn((dlogits / temp).astype(BF16), images_ref[...])
    draw = unit_pull(raw, dtext).astype(BF16)
    text_acc[...] += dot_tn(lead, draw)
    lead_ref[...] = dot_nt(draw, wtext_ref[...])
    for row in range(rows):
        first = pl.ds(row * length, 1)
        grad_ref[first, :] += lead_ref[pl.ds(2 * row, 1), :]
        second = pl.ds(row * length + bound_ref[step * rows + row], 1)
        grad_ref[second, :] += lead_ref[pl.ds(2 * row + 1, 1), :]

    dr3, dgain3, dshift3 = norm_pull(grad_ref[...], xhat3, rstd3, norm_ref[4:5])
    dgain3_ref[...] += dgain3
    dshift3_ref[...] += dshift3
    grad_ref[...] = dr3
    dfinal = dr3.astype(BF16)
    own = hidden_units // 4
    own_at = pl.ds(pl.multiple_of(which_ref[0] * own, own), own)
    down_acc[...] += dot_tn(act_ref[:, own_at], dfinal)

    def backward(index, carry):
        at = pl.ds(pl.multiple_of(index * chunk, chunk), chunk)
        dact = dot_nt(dfinal, wdown_ref[at, :])
        dinner = (dact * slope_ref[:, at]).astype(BF16)
        act_ref[:, at] = dinner
        grad_ref[...] += dot_nn(dinner, wup_ref[at, :])
        return carry

    lax.fori_loop(0, hidden_units // chunk, backward, 0, unroll=True)
    up_acc[...] += dot_tn(low, act_ref[:, own_at])
    dr2, dgain2, dshift2 = norm_pull(grad_ref[...], xhat2, rstd2_ref[...], norm_ref[2:3])
    dgain2_ref[...] += dgain2
    dshift2_ref[...] += dshift2
    dr2_ref[...] = dr2

    @pl.when(step == steps - 1)
    def _():
        dup_ref[...] = up_acc[...].astype(BF16)
        ddown_ref[...] = down_acc[...].astype(BF16)
        dtext_ref[...] = text_acc[...].astype(BF16)


def cross_backward_kernel(
    patch_count, length, which_ref, region_ref, kv_ref, cq_ref, ctx_ref, xhat1_ref, rstd1_ref, norm_ref,
    dr2_ref, wkv_ref, wout_ref, wcq_ref, probs_ref,
    dregion_ref, dr1_ref, dkv_ref, dqo_ref, dgain_ref, dshift_ref,
    dctx_ref, dq_ref, grads_ref, flat_ref, stage_ref, kv_acc, cq_acc, out_acc, sem,
):
    step = pl.program_id(0)
    steps = pl.num_programs(0)
    images, padded, vision = region_ref.shape
    width = cq_ref.shape[1]
    own = width // 4
    which = which_ref[0]
    mine = window(which, GROUP)
    wide = stage_ref.shape[2]
    parts = wide // images
    stored = flat_ref.shape[1] // wide

    @pl.when(step == 0)
    def _():
        for ref in (dgain_ref, dshift_ref, kv_acc, cq_acc, out_acc):
            ref[...] = jnp.zeros_like(ref)

    dr2 = dr2_ref[...]
    dx = dr2.astype(BF16)
    dctx_ref[...] = dot_nt(dx, wout_ref[...]).astype(BF16)
    out_acc[...] += dot_tn(ctx_ref[:, mine], dx)

    def pair(index, carry):
        span = pl.ds(pl.multiple_of(index * 2 * length, 16), 2 * length)
        for group in range(width // GROUP):
            lanes = slice(group * GROUP, (group + 1) * GROUP)
            value_lanes = slice(width + group * GROUP, width + (group + 1) * GROUP)
            q = cq_ref[span, lanes].astype(F32)
            d = dctx_ref[span, lanes].astype(F32)
            out = []
            for j in range(2):
                image = 2 * index + j
                at = slice(j * length, (j + 1) * length)
                dq, dk, dv = attend_backward(
                    q[at], kv_ref[image, :, lanes], kv_ref[image, :, value_lanes], None, d[at], probs_ref[image, group]
                )
                out.append(dq)
                grads_ref[image, :, lanes] = dk.astype(BF16)
                grads_ref[image, :, value_lanes] = dv.astype(BF16)
            dq_ref[span, lanes] = jnp.concatenate(out, axis=0).astype(BF16)
        return carry

    lax.fori_loop(0, images // 2, pair, 0, unroll=4)

    some = images
    for index in range(images // some):
        grads = grads_ref[index * some : (index + 1) * some].reshape(some * padded, 2 * width)
        dregion = dot_nn(grads, wkv_ref[...])
        for image in range(some):
            spot = pl.ds(step % parts * images + index * some + image, stored, stride=wide)
            for lane in range(vision // 128):
                flat_ref[lane, spot, :] = dregion[
                    image * padded : image * padded + stored, lane * 128 : (lane + 1) * 128
                ]
    region = region_ref[...].reshape(images * padded, vision)
    for part in range(2):
        at = window(which, GROUP)
        grads = grads_ref[:, :, pl.ds(pl.multiple_of(which * 3 // 2 * 128 + part * width, 128), GROUP)]
        kv_acc[part] += dot_tn(grads.reshape(images * padded, GROUP), region)

    pieces = 5
    patches = patch_count // pieces
    tall = patches * wide

    def send(index):
        slot = index % 2
        base = pl.multiple_of(step // parts * wide, 16)
        return pltpu.make_async_copy(
            stage_ref.at[slot],
            dregion_ref.at[pl.ds(index * patches, patches), pl.ds(base, wide), :],
            sem.at[slot],
        )

    @pl.when(step % parts == parts - 1)
    def _():
        for index in range(pieces):
            rows = slice(index * tall, (index + 1) * tall)
            low = jnp.concatenate([flat_ref[c, rows, :].astype(BF16) for c in range(vision // 128)], axis=1)
            if index >= 2:
                send(index - 2).wait()
            stage_ref[index % 2] = low.reshape(patches, wide, vision)
            send(index).start()
        send(pieces - 2).wait()
        send(pieces - 1).wait()

    xhat1 = xhat1_ref[...]
    hidden1 = (xhat1 * norm_ref[0:1] + norm_ref[1:2]).astype(BF16)
    cq_acc[...] += dot_tn(dq_ref[:, mine], hidden1)
    dh1 = dr2 + dot_nn(dq_ref[...], wcq_ref[...])
    dr1, dgain, dshift = norm_pull(dh1, xhat1, rstd1_ref[...], norm_ref[0:1])
    dr1_ref[...] = dr1
    dgain_ref[...] += dgain
    dshift_ref[...] += dshift

    @pl.when(step == steps - 1)
    def _():
        for part in range(2):
            dkv_ref[part * own : (part + 1) * own, :] = own_rows(kv_acc[part], which, own).astype(BF16)
        dqo_ref[:own, :] = own_rows(cq_acc[...], which, own).astype(BF16)
        dqo_ref[own:, :] = own_rows(out_acc[...], which, own).astype(BF16)


def self_backward_kernel(length, sums, *refs):
    bound_ref, tok_ref, qkv_ref, ctx_ref, dr1_ref, wqk_ref, wv_ref, wout_ref = refs[:8]
    refs = refs[8:]
    if sums:
        dkv_ref, dqo_ref, temp_ref, pack_ref, picture_ref, wimage_ref = refs[:6]
        vectors, refs = refs[6:13], refs[13:]
    dtok_ref, last_ref = refs[:2]
    refs = refs[2:]
    if sums:
        outs, dpicture_ref, refs = refs[:4], refs[4], refs[5:]
    dctx_ref, grads_ref, qkv_acc, out_acc, last = refs[:5]
    refs = refs[5:]
    step = pl.program_id(0)
    steps = pl.num_programs(0)
    half = steps // 2
    tokens, width = tok_ref.shape
    rows = tokens // length
    own = width // 4
    which = lax.axis_index("mp")
    if sums:
        packs, dimage, small, pack_sent, pack_came = refs[:5]
        refs = refs[5:]
        spots = (dkv_ref, dqo_ref, small, dimage, last.at[: 2 * own], last.at[2 * own :])
        kv_sum, qo_sum, small_sum, image_sum, *finals = (
            Reduce(spot, *refs[6 * i : 6 * i + 6]) for i, spot in enumerate(spots)
        )
        dp, z = lax.axis_index("dp"), lax.axis_index("mp")
        dp_size = packs.shape[0]

        def pack_copy(k, owner):
            return pltpu.make_async_remote_copy(
                src_ref=pack_ref, dst_ref=packs.at[owner], send_sem=pack_sent.at[k], recv_sem=pack_came.at[k],
                device_id=((dp + k) % dp_size, z), device_id_type=MESH,
            )

        @pl.when(step == 0)
        def _():
            small[...] = jnp.zeros(small.shape, BF16)
            lines = [ref[...] for ref in vectors[:6]] + [jnp.broadcast_to(vectors[6][...], (1, width))]
            lines = [*lines, jnp.zeros((16 - len(lines), width), F32)]
            small[0:16, :] = jnp.concatenate(lines, axis=0).astype(BF16)
            barrier = pltpu.get_barrier_semaphore()
            for k in range(1, dp_size):
                pl.semaphore_signal(barrier, inc=1, device_id=((dp + k) % dp_size, z), device_id_type=MESH)
            pl.semaphore_wait(barrier, dp_size - 1)
            for k in range(1, dp_size):
                pack_copy(k, dp).start()
            packs[dp] = pack_ref[...]
            for reduce in (kv_sum, qo_sum, small_sum):
                reduce.stage(1)

        @pl.when(step == 1)
        def _():
            for reduce in (kv_sum, qo_sum, small_sum):
                reduce.stage(2)
            for k in range(1, dp_size):
                pack_copy(k, (dp + dp_size - k) % dp_size).wait_recv()
                pack_copy(k, dp).wait_send()
            everyone = packs[...].reshape(-1, packs.shape[2])
            first = dp * picture_ref.shape[0]
            dpicture, dweight = image_backward(first, temp_ref[0], picture_ref[...], wimage_ref[...], everyone)
            dpicture_ref[...] = dpicture
            dimage[...] = dweight.astype(BF16)
            image_sum.stage(1)

        for number in (3, 4):

            @pl.when(step == number - 1)
            def _(number=number):
                for reduce in (kv_sum, qo_sum, small_sum):
                    reduce.stage(number)
                image_sum.stage(number - 1)

    @pl.when(step == 0)
    def _():
        for ref in (qkv_acc, out_acc):
            ref[...] = jnp.zeros_like(ref)

    @pl.when(step < half)
    def _():
        all_rows = pl.ds(pl.multiple_of(step * tokens, 16), tokens)
        da = dr1_ref[...].astype(BF16)
        dctx_ref[...] = dot_nt(da, wout_ref[...]).astype(BF16)
        out_acc[...] += dot_tn(ctx_ref[:, window(which, GROUP)], da)

        def pair(index, carry):
            span = pl.ds(pl.multiple_of(index * 2 * length, 16), 2 * length)
            far = pl.ds(pl.multiple_of(step * tokens + index * 2 * length, 16), 2 * length)
            keeps = [row_keep(bound_ref[step * rows + 2 * index + j], length) for j in range(2)]
            for group in range(width // GROUP):
                q, k, v = (
                    qkv_ref[span, part * width + group * GROUP : part * width + (group + 1) * GROUP].astype(F32)
                    for part in range(3)
                )
                d = dctx_ref[span, group * GROUP : (group + 1) * GROUP].astype(F32)
                outs = []
                for j in range(2):
                    at = slice(j * length, (j + 1) * length)
                    outs.append(attend_backward(q[at], k[at].astype(BF16), v[at].astype(BF16), keeps[j], d[at]))
                for part in range(3):
                    both = jnp.concatenate([outs[0][part], outs[1][part]], axis=0).astype(BF16)
                    grads_ref[far, part * width + group * GROUP : part * width + (group + 1) * GROUP] = both
            return carry

        lax.fori_loop(0, rows // 2, pair, 0, unroll=4)
        tok = tok_ref[...]
        for part in range(3):
            mine = grads_ref[all_rows, pl.ds(pl.multiple_of(which * 3 // 2 * 128 + part * width, 128), GROUP)]
            qkv_acc[part] += dot_tn(mine, tok)

    @pl.when(step == half - 1)
    def _():
        for part in range(3):
            last[part * own : (part + 1) * own, :] = own_rows(qkv_acc[part], which, own).astype(BF16)
        last[3 * own : 4 * own, :] = own_rows(out_acc[...], which, own).astype(BF16)
        if sums:
            for reduce in finals:
                reduce.stage(1)

    @pl.when(step >= half)
    def _():
        done = pl.ds(pl.multiple_of((step - half) * tokens, 16), tokens)
        part = dr1_ref[...] + dot_nn(grads_ref[done, : 2 * width], wqk_ref[...])
        dtok_ref[...] = part + dot_nn(grads_ref[done, 2 * width :], wv_ref[...])

    if sums:

        @pl.when(step == half)
        def _():
            image_sum.stage(4)
            for reduce in finals:
                reduce.stage(2)

    @pl.when(step == steps - 1)
    def _():
        if sums:
            for reduce in finals:
                reduce.stage(3)
            for reduce in (kv_sum, qo_sum, small_sum, image_sum):
                reduce.stage(5)
            for reduce, out in zip((kv_sum, qo_sum, small_sum, image_sum), outs, strict=True):
                out[...] = reduce.done[...]
            for number in (4, 5):
                for reduce in finals:
                    reduce.stage(number)
            last_ref[: 2 * own, :] = finals[0].done[...]
            last_ref[2 * own :, :] = finals[1].done[...]
        else:
            last_ref[...] = last[...]


def image_backward(first, temp, picture, weight, pack):
    raw = dot_nn(picture, weight)
    own = (raw * lax.rsqrt(jnp.sum(raw * raw, axis=-1, keepdims=True) + NORM_EPS)).astype(BF16)
    embed = raw.shape[1]
    text = pack[:, :embed].astype(BF16)
    lse = pack[:, embed : embed + 1]
    target = pack[:, embed + 1 : embed + 2].astype(jnp.int32)
    logits = dot_nt(text, own) / temp
    hit = lax.broadcasted_iota(jnp.int32, logits.shape, 1) + first == target
    dlogits = jnp.exp(logits - lse) - hit.astype(F32)
    dimage = dot_tn((dlogits / temp).astype(BF16), text)
    draw = unit_pull(raw, dimage).astype(BF16)
    return dot_nt(draw, weight), dot_tn(picture, draw)


def image_backward_kernel(
    first_ref, temp_ref, picture_ref, weight_ref, pack_ref, dpicture_ref, dweight_ref
):
    dpicture, dweight = image_backward(
        first_ref[0], temp_ref[0], picture_ref[...], weight_ref[...], pack_ref[...]
    )
    dpicture_ref[...] = dpicture
    dweight_ref[...] = dweight.astype(BF16)


def widen_kernel(own, last_ref, dkv_ref, dqo_ref, dimage_ref, dup_ref, ddown_ref, dtext_ref, small_ref, *outs):
    for index in range(4):
        outs[index][...] = last_ref[index * own : (index + 1) * own, :].astype(F32)
    for index in range(2):
        outs[4 + index][...] = dqo_ref[index * own : (index + 1) * own, :].astype(F32)
        outs[6 + index][...] = dkv_ref[index * own : (index + 1) * own, :].astype(F32)
    for out, ref in zip(outs[8:12], (dup_ref, ddown_ref, dtext_ref, dimage_ref), strict=True):
        out[...] = ref[...].astype(F32)
    small = small_ref[0:16, :].astype(F32)
    for index in range(6):
        outs[12 + index][...] = small[index]
    outs[18][...] = small[6:7, 0:1]


def full(shape):
    return pl.BlockSpec(shape, lambda i: (0,) * len(shape), pipeline_mode=pl.Buffered(1))


def fixed(shape):
    return pl.BlockSpec(shape, lambda i: (0,) * len(shape))


def rows_of(count, width):
    return pl.BlockSpec((count, width), lambda i: (i, 0))


SMEM = pl.BlockSpec(memory_space=pltpu.SMEM)


def shape_of(shape, kind):
    return jax.ShapeDtypeStruct(shape, kind)


def call(kernel, steps, ins, outs, args, scratch=(), flops=0, moved=0, ident=None):
    specs, shapes = zip(*outs, strict=True)
    remote = {} if ident is None else {"collective_id": ident, "has_side_effects": True}
    return pl.pallas_call(
        kernel,
        grid=(steps,),
        in_specs=list(ins),
        out_specs=list(specs),
        out_shape=list(shapes),
        scratch_shapes=list(scratch),
        compiler_params=pltpu.CompilerParams(
            vmem_limit_bytes=VMEM_LIMIT, dimension_semantics=("arbitrary",), **remote
        ),
        cost_estimate=pl.CostEstimate(flops=flops, bytes_accessed=moved, transcendentals=0),
    )(*args)


DEPTH = 4


def gathered(groups, split=1):
    shapes = [(len(group), *group[0].shape) for group in groups]
    outs = [
        (pl.BlockSpec(memory_space=pl.ANY), shape_of((shape[0], DEPTH, *shape[1:]), BF16)) for shape in shapes
    ]
    scratch = [pltpu.VMEM(shape, BF16) for shape in shapes]
    specs = [full(shard.shape) for group in groups for shard in group]
    return specs, outs, [*scratch, *Gather.semaphores(len(groups) * split, DEPTH)] if groups else []


def flatten(groups):
    return [shard for group in groups for shard in group]


TOKEN_ROWS = 8
IMAGE_ROWS = 16


def square(width, index):
    return pl.BlockSpec((width, width), lambda i: (index, 0), pipeline_mode=pl.Buffered(1))


def run_prep(region, picture, wimage, shards):
    patch_count, rows, vision = region.shape
    padded = -(-patch_count // 16) * 16
    embed = wimage.shape[1]
    specs, outs, sems = gathered(shards)
    return call(
        partial(prep_kernel, len(shards), len(flatten(shards))),
        vision // 128,
        [pl.BlockSpec((patch_count, rows, 128), lambda i: (0, 0, i)), full(picture.shape), full(wimage.shape), *specs],
        [
            (pl.BlockSpec((rows, padded, 128), lambda i: (0, 0, i)), shape_of((rows, padded, vision), BF16)),
            (fixed((rows, embed)), shape_of((rows, embed), BF16)),
            *outs,
        ],
        (region, picture, wimage, *flatten(shards)),
        scratch=[pltpu.VMEM((patch_count * rows, 128), F32), *sems],
        moved=4 * rows * padded * vision,
        ident=1 if shards else None,
    )


def run_self_forward(length, dp_size, bound, tok, weights, embed, shards):
    tokens, width = tok.shape
    block = TOKEN_ROWS * length
    specs, outs, sems = gathered(shards)
    if shards:
        shape = shape_of((dp_size * embed.shape[0], embed.shape[1]), BF16)
        outs = [*outs, (pl.BlockSpec(memory_space=pl.ANY), shape)]
        sems = [DMA, DMA((dp_size,)), DMA((dp_size,)), *sems]
    return call(
        partial(self_forward_kernel, length, len(shards), len(flatten(shards))),
        tokens // block,
        [SMEM, rows_of(block, width), full((2 * width, width)), square(width, 0), square(width, 1), full(embed.shape), *specs],
        [
            (rows_of(block, 3 * width), shape_of((tokens, 3 * width), BF16)),
            (rows_of(block, width), shape_of((tokens, width), BF16)),
            (rows_of(block, width), shape_of((tokens, width), F32)),
            (rows_of(block, 1), shape_of((tokens, 1), F32)),
            *outs,
        ],
        (bound, tok, weights[0], weights[1], weights[1], embed, *flatten(shards)),
        scratch=sems,
        flops=10 * tokens * width * width,
        moved=20 * tokens * width,
        ident=2 if shards else None,
    )


def probs_spec(width, length, padded):
    return pl.BlockSpec((TOKEN_ROWS, width // GROUP, padded, 4 * length), lambda i: (i, 0, 0, 0))


def run_cross_forward(length, patch_count, region, wkv, xhat1, norms, wcq, wout, shards):
    rows, padded, vision = region.shape
    tokens, width = xhat1.shape
    images = TOKEN_ROWS
    block = images * length
    specs, outs, sems = gathered(shards, split=2)
    return call(
        partial(cross_forward_kernel, patch_count, length, len(shards), len(flatten(shards))),
        rows // images,
        [
            pl.BlockSpec((images, padded, vision), lambda i: (i, 0, 0)), full((2 * width, vision)),
            rows_of(block, width), full(norms.shape), square(width, 0), square(width, 1), *specs,
        ],
        [
            (
                pl.BlockSpec((images, padded, 2 * width), lambda i: (i, 0, 0)),
                shape_of((rows, padded, 2 * width), BF16),
            ),
            (rows_of(block, width), shape_of((tokens, width), BF16)),
            (rows_of(block, width), shape_of((tokens, width), BF16)),
            (rows_of(block, width), shape_of((tokens, width), F32)),
            (rows_of(block, 1), shape_of((tokens, 1), F32)),
            (probs_spec(width, length, padded), shape_of((rows, width // GROUP, padded, 4 * length), BF16)),
            *outs,
        ],
        (region, wkv, xhat1, norms, wcq, wout, *flatten(shards)),
        scratch=sems,
        flops=4 * rows * padded * width * vision,
        moved=2 * rows * padded * (vision + 2 * width),
        ident=3 if shards else None,
    )


def run_feed_forward(
    length, bound, which, temp, xhat2, rstd2, norms, ffn, adjoint, target, image_all, wtext
):
    tokens, width = xhat2.shape
    hidden_units = ffn.shape[0] // 2
    embed = wtext.shape[1]
    block = IMAGE_ROWS * length
    captions = 2 * IMAGE_ROWS
    ff_own = hidden_units // 4
    return call(
        partial(feed_forward_kernel, length),
        tokens // block,
        [
            SMEM, SMEM, SMEM, rows_of(block, width), rows_of(block, 1), full(norms.shape),
            full((hidden_units, width)),
            pl.BlockSpec((hidden_units, width), lambda i: (1, 0), pipeline_mode=pl.Buffered(1)),
            rows_of(block, width), rows_of(captions, 1),
            full(image_all.shape), full((width, embed)),
        ],
        [
            (rows_of(block, width), shape_of((tokens, width), BF16)),
            (rows_of(captions, 1), shape_of(target.shape, F32)),
            (rows_of(captions, embed + 128), shape_of((target.shape[0], embed + 128), F32)),
            (rows_of(block, width), shape_of((tokens, width), F32)),
            (fixed((width, ff_own)), shape_of((width, ff_own), BF16)),
            (fixed((ff_own, width)), shape_of((ff_own, width), BF16)),
            (fixed((1, width)), shape_of((1, width), F32)),
            (fixed((1, width)), shape_of((1, width), F32)),
            (fixed((1, width)), shape_of((1, width), F32)),
            (fixed((1, width)), shape_of((1, width), F32)),
            (fixed((width, embed)), shape_of((width, embed), BF16)),
            (fixed((1, 1)), shape_of((1, 1), F32)),
        ],
        (
            bound, which, temp, xhat2, rstd2, norms, ffn, ffn, adjoint, target, image_all,
            wtext,
        ),
        scratch=[
            pltpu.VMEM((block, hidden_units), BF16),
            pltpu.VMEM((block, hidden_units), F32),
            pltpu.VMEM((block, width), F32),
            pltpu.VMEM((block, width), F32),
            pltpu.VMEM((captions, width), F32),
            pltpu.VMEM((width, ff_own), F32),
            pltpu.VMEM((ff_own, width), F32),
            pltpu.VMEM((width, embed), F32),
        ],
        flops=10 * tokens * width * hidden_units,
        moved=20 * tokens * width,
    )


def run_cross_backward(length, patch_count, which, region, kv, cq, ctx2, xhat1, rstd1, norms, dr2, wkv, wcq, wout, probs):
    rows, padded, vision = region.shape
    tokens, width = cq.shape
    images = TOKEN_ROWS
    block = images * length
    own = width // 4
    stored = -(-patch_count // 8) * 8
    return call(
        partial(cross_backward_kernel, patch_count, length),
        rows // images,
        [
            SMEM,
            pl.BlockSpec((images, padded, vision), lambda i: (i, 0, 0)),
            pl.BlockSpec((images, padded, 2 * width), lambda i: (i, 0, 0)),
            rows_of(block, width), rows_of(block, width), rows_of(block, width), rows_of(block, 1), full(norms.shape),
            rows_of(block, width), full((2 * width, vision)), square(width, 1), square(width, 0),
            probs_spec(width, length, padded),
        ],
        [
            (pl.BlockSpec(memory_space=pl.ANY), shape_of((patch_count, rows, vision), BF16)),
            (rows_of(block, width), shape_of((tokens, width), F32)),
            (fixed((2 * own, vision)), shape_of((2 * own, vision), BF16)),
            (fixed((2 * own, width)), shape_of((2 * own, width), BF16)),
            (fixed((1, width)), shape_of((1, width), F32)),
            (fixed((1, width)), shape_of((1, width), F32)),
        ],
        (which, region, kv, cq, ctx2, xhat1, rstd1, norms, dr2, wkv, wout, wcq, probs),
        scratch=[
            pltpu.VMEM((block, width), BF16),
            pltpu.VMEM((block, width), BF16),
            pltpu.VMEM((images, padded, 2 * width), BF16),
            pltpu.VMEM((vision // 128, stored * IMAGE_ROWS, 128), F32),
            pltpu.VMEM((2, patch_count // 5, IMAGE_ROWS, vision), BF16),
            pltpu.VMEM((2, GROUP, vision), F32),
            pltpu.VMEM((GROUP, width), F32),
            pltpu.VMEM((GROUP, width), F32),
            DMA((2,)),
        ],
        flops=6 * rows * padded * width * vision,
        moved=2 * rows * padded * 2 * (vision + width),
    )


def run_self_backward(length, dp_size, bound, tok, qkv, ctx1, dr1, weights, others):
    tokens, width = tok.shape
    block = TOKEN_ROWS * length
    steps = tokens // block
    last = shape_of((width, width), BF16)

    def early(lanes):
        return pl.BlockSpec((block, lanes), lambda i: (jnp.minimum(i, steps - 1), 0))

    extra, outs, scratch = [], [], []
    if others:
        dkv, dqo, _, pack, picture, wimage, *vectors = others
        image = shape_of(wimage.shape, BF16)
        small = shape_of((128, width), BF16)
        half = (width // 2, width)
        shapes = [shape_of(dkv.shape, BF16), shape_of(dqo.shape, BF16), small, image]
        extra = [full(dkv.shape), full(dqo.shape), SMEM, *(full(other.shape) for other in others[3:])]
        outs = [*((fixed(shape.shape), shape) for shape in shapes), (fixed(picture.shape), shape_of(picture.shape, F32))]
        scratch = [
            pltpu.VMEM((dp_size, *pack.shape), F32), pltpu.VMEM(image.shape, BF16), pltpu.VMEM(small.shape, BF16),
            DMA((dp_size,)), DMA((dp_size,)),
            *(spot for shape in (*(shape.shape for shape in shapes), half, half) for spot in Reduce.scratch(shape)),
        ]
    return call(
        partial(self_backward_kernel, length, bool(others)),
        2 * steps,
        [
            SMEM, early(width), early(3 * width), early(width),
            pl.BlockSpec((block, width), lambda i: (lax.rem(i, steps), 0)),
            full((2 * width, width)), square(width, 0), square(width, 1), *extra,
        ],
        [
            (
                pl.BlockSpec((block, width), lambda i: (jnp.maximum(i - steps, 0), 0)),
                shape_of((tokens, width), F32),
            ),
            (fixed(last.shape), last),
            *outs,
        ],
        (bound, tok, qkv, ctx1, dr1, weights[0], weights[1], weights[1], *others),
        scratch=[
            pltpu.VMEM((block, width), BF16),
            pltpu.VMEM((tokens, 3 * width), BF16),
            pltpu.VMEM((3, GROUP, width), F32),
            pltpu.VMEM((GROUP, width), F32),
            pltpu.VMEM(last.shape, BF16),
            *scratch,
        ],
        flops=10 * tokens * width * width,
        moved=20 * tokens * width,
        ident=4 if others else None,
    )


def run_widen(last, dkv, dqo, dimage, dup, ddown, dtext, small):
    width = last.shape[1]
    own = width // 4
    shapes = [(own, width)] * 6 + [(own, dkv.shape[1])] * 2
    shapes += [dup.shape, ddown.shape, dtext.shape, dimage.shape] + [(width,)] * 6 + [(1, 1)]
    args = (last, dkv, dqo, dimage, dup, ddown, dtext, small)
    return call(
        partial(widen_kernel, own),
        1,
        [fixed(array.shape) for array in args],
        [(fixed(shape), shape_of(shape, F32)) for shape in shapes],
        args,
        moved=20 * width * width,
    )


def body(
    dp_size,
    word_features,
    sentence_numbering,
    region_features,
    picture_global_feature,
    matched_picture,
    sharpness_array,
    incoming_adjoint,
    intra_asking_map,
    intra_lookup_map,
    intra_content_map,
    intra_attend_exit_map,
    visual_asking_map,
    visual_lookup_map,
    visual_content_map,
    visual_attend_exit_map,
    mlp_widening_factor,
    mlp_narrowing_factor,
    initial_standardize_scale,
    initial_standardize_offset,
    middle_standardize_scale,
    middle_standardize_offset,
    final_standardize_scale,
    final_standardize_offset,
    sentence_mapping_factor,
    picture_mapping_factor,
):
    rows, length = sentence_numbering.shape
    tokens, width = word_features.shape
    patch_count, vision = region_features.shape[1:]
    embed = sentence_mapping_factor.shape[1]
    hidden_units = mlp_widening_factor.shape[1] * 4
    own = width // 4
    which = lax.axis_index("mp").astype(jnp.int32).reshape(1)
    bound = (length - jnp.sum(sentence_numbering, axis=1)).astype(jnp.int32)
    target = matched_picture.reshape(-1, 1)
    norms = jnp.concatenate([
        initial_standardize_scale, initial_standardize_offset, middle_standardize_scale,
        middle_standardize_offset, final_standardize_scale, final_standardize_offset,
    ]).reshape(6, width)

    selves = [(intra_asking_map.T, intra_lookup_map.T), (intra_content_map.T, intra_attend_exit_map)]
    crosses = (visual_asking_map.T, visual_attend_exit_map)
    wides = (visual_lookup_map.T, visual_content_map.T)
    ffns = (mlp_widening_factor.T, mlp_narrowing_factor)
    region = jnp.transpose(region_features, (1, 0, 2))
    local = dp_size == 8 and lax.axis_size("mp") == DEPTH

    def each(*shards):
        return list(shards) if local else []

    region, image_own, *found = run_prep(region, picture_global_feature, picture_mapping_factor, each(*selves))
    selves = found if local else [lax.all_gather(jnp.stack(pair), "mp", axis=1) for pair in selves]
    selves = [pair.reshape(-1, width) for pair in selves]
    qkv, ctx1, xhat1, rstd1, *found = run_self_forward(
        length, dp_size, bound, word_features, selves, image_own, each(crosses, wides)
    )
    if local:
        crosses, wides, image_all = found
    else:
        crosses, wides = (lax.all_gather(jnp.stack(group), "mp", axis=1) for group in (crosses, wides))
        image_all = lax.all_gather(image_own, "dp", axis=0, tiled=True)
    crosses = crosses.reshape(-1, width)
    wkv = wides.reshape(-1, vision)
    kv, cq, ctx2, xhat2, rstd2, probs, *found = run_cross_forward(
        length, patch_count, region, wkv, xhat1, norms, crosses, crosses, each(ffns)
    )
    ffns = (found[0] if local else lax.all_gather(jnp.stack(ffns), "mp", axis=1)).reshape(-1, width)
    (
        block_exit, loss, pack, dr2, dup, ddown, dgain2, dshift2, dgain3, dshift3, dtext, dtemp,
    ) = run_feed_forward(
        length, bound, which, sharpness_array, xhat2, rstd2, norms, ffns, incoming_adjoint, target, image_all,
        sentence_mapping_factor,
    )

    dp_sum = lambda grad: lax.psum(grad, "dp")
    dup, ddown, dtext = dp_sum((dup, ddown, dtext))
    dregion, dr1, dkv, dqo, dgain1, dshift1 = run_cross_backward(
        length, patch_count, which, region, kv, cq, ctx2, xhat1, rstd1, norms, dr2, wkv, crosses, crosses, probs
    )
    vectors = (dgain1, dshift1, dgain2, dshift2, dgain3, dshift3, dtemp)
    pictures = (picture_global_feature, picture_mapping_factor)
    dtok, last, *found = run_self_backward(
        length, dp_size, bound, word_features, qkv, ctx1, dr1, selves,
        each(dkv, dqo, sharpness_array, pack, *pictures, *vectors),
    )
    if local:
        dkv, dqo, small, dimage, dpicture = found
    else:
        pack_all = lax.all_gather(pack, "dp", axis=0, tiled=True)
        first = (lax.axis_index("dp") * rows).astype(jnp.int32).reshape(1)
        dpicture, dimage = call(
            image_backward_kernel,
            1,
            [SMEM, SMEM, *(full(array.shape) for array in (*pictures, pack_all))],
            [
                (fixed((rows, vision)), shape_of((rows, vision), F32)),
                (fixed((vision, embed)), shape_of((vision, embed), BF16)),
            ],
            (first, sharpness_array, *pictures, pack_all),
        )
        lines = [*vectors[:6], jnp.broadcast_to(dtemp, (1, width)), jnp.zeros((9, width), F32)]
        small = jnp.concatenate(lines).astype(BF16)
        dkv, dqo, dimage, last, small = dp_sum((dkv, dqo, dimage, last, small))
    dq, dk, dv, dso, dcq, dco, dck, dcv, dup, ddown, dtext, dimage, *vectors = run_widen(
        last, dkv, dqo, dimage, dup, ddown, dtext, small
    )
    return (
        loss.reshape(rows, 2),
        block_exit,
        dtok,
        jnp.transpose(dregion, (1, 0, 2)),
        dpicture,
        vectors[6].reshape(1),
        dq.T,
        dk.T,
        dv.T,
        dso,
        dcq.T,
        dck.T,
        dcv.T,
        dco,
        dup,
        ddown,
        *vectors[:6],
        dtext,
        dimage,
    )


def solution(mesh):
    rows = P("dp", None)
    by_column = P(None, "mp")
    by_row = P("mp", None)
    in_specs = (
        rows, rows, P("dp", None, None), rows, rows, P(), rows,
        by_column, by_column, by_column, by_row, by_column, by_column, by_column, by_row, by_column, by_row,
        P(), P(), P(), P(), P(), P(), P(), P(),
    )
    out_specs = (
        rows, rows, rows, P("dp", None, None), rows, P(),
        by_column, by_column, by_column, by_row, by_column, by_column, by_column, by_row, by_column, by_row,
        P(), P(), P(), P(), P(), P(), P(), P(),
    )
    return jax.shard_map(
        partial(body, mesh.shape["dp"]), mesh=mesh, in_specs=in_specs, out_specs=out_specs, check_vma=False
    )
```
